32 devices in a mesh: dom: 8 (over z, x), edge: 4 (over y, core).
Axes of the slice: x: 2, y: 2, z: 4, core: 2. Of those that a mesh axis runs over, the one named last changes fastest.
Arguments:
- node_feats: bfloat16 [4096, 1024], P(('dom', 'edge')), may hold values from -6 to 6
- gat_weight: bfloat16 [1024, 1024], P('edge'), may hold values from -0.1875 to 0.1875
- attn_src: float32 [8, 128], replicated
- attn_dst: float32 [8, 128], replicated
- neighbours: int32 [4096, 16], P(('dom', 'edge')), may hold values from 0 to 383
- degree: int32 [4096], P(('dom', 'edge')), may hold values from 0 to 16
- halo_rows: int32 [8, 4, 8, 32], P('dom', 'edge'), may hold values from 0 to 127
- halo_count: int32 [8, 4, 8], P('dom', 'edge'), may hold values from 1 to 32, as said below
- endpoint_rows: int32 [8, 4, 8, 4, 2], P('dom', 'edge'), may hold values from 0 to 127
- cand_ends: int32 [8, 4, 2, 256], P('dom', 'edge'), may hold values from 0 to 63
- cand_count: int32 [8, 4], P('dom', 'edge'), may hold values from 16 to 256, as said below
- labels: int32 [8, 4, 256], P('dom', 'edge'), may hold values 0 or 1
- mlp_weight: bfloat16 [2048, 512], P('edge'), may hold values from -0.125 to 0.125
- out_weight: float32 [512], replicated, may hold values from -0.6 to 0.6
Outputs:
- node_out: bfloat16 [4096, 1024], P(('dom', 'edge'))
- scores: float32 [8, 4, 256], P('dom', 'edge')
- node_grad: float32 [4096, 1024], P(('dom', 'edge'))
The draws below stay inside these ranges and needn't reach their ends.
Inputs may be any that keep to these rules, and one draw needn't show every extreme that they name: `neighbours`: an entry below 128 names the device's own row; entry 128 + s * 32 + k names row k of the boundary block from dom index s. `halo_count`: in every draw some dom index receives full blocks from every sender. `cand_ends`: slot (s * 4 + r) * 2 + k is row k that device (s, r) sends. `cand_count`: some device has all 256 candidate slots live.
All inputs are finite; a program needn't handle non-finite values. No bound on the sum of `labels` on one device may be relied on, other than what follows from the above.
Results may differ from the reference program's by a relative error of at most 0.012.
The reference program's roundings to bfloat16 on the way count: a program that leaves them out, or rounds other values in their place, can miss the bound.
Values may be sent and summed in bfloat16 or wider, within the bound.
No kernel may reach another device: no remote copies, remote signals or barrier semaphores. Data moves between devices by JAX's collectives and lax.ppermute only.
A program may use at most 64 MiB of HBM per device.

```python
import jax
import jax.numpy as jnp
from jax import lax

D = 1024
HEADS = 8
HID = 512
NODE_DEV = 128
DEG = 16
BLK = 32
ESLOT = 2
CAND = 256
NODES = 4096
SLOTS = 64
TABLE = 384
N_DOM = 8
N_EDGE = 4


def head_vectors(key, scales):
    normal_draw = jnp.clip(jax.random.normal(key, (HEADS, D // HEADS), jnp.float32), -3.0, 3.0)
    return normal_draw * scales[:, None] * (D // HEADS) ** (-0.5)


def draw_attn_src(key, part):
    key = jax.random.fold_in(key, 3)
    scale_key, normal_key = jax.random.split(key)
    scales = jax.random.uniform(scale_key, (HEADS,), jnp.float32, 0.5, 1.5)
    return head_vectors(normal_key, scales)


def draw_attn_dst(key, part):
    key = jax.random.fold_in(key, 5)
    scale_key, normal_key = jax.random.split(key)
    scales = jax.random.uniform(scale_key, (HEADS,), jnp.float32, 0.5, 1.5)
    return head_vectors(normal_key, scales)


def draw_halo_count(key, part):
    key = jax.random.fold_in(key, 7)
    count_key, full_key = jax.random.split(key)
    counts = jax.random.randint(count_key, (N_DOM, N_EDGE, N_DOM), 1, BLK + 1)
    full_dom = jax.random.randint(full_key, (), 0, N_DOM)
    target = jnp.arange(N_DOM)[None, None, :]
    return jnp.where(target == full_dom, BLK, counts).astype(jnp.int32)


def draw_cand_count(key, part):
    key = jax.random.fold_in(key, 11)
    shift_key, trim_key, full_key = jax.random.split(key, 3)
    level_shift = jax.random.randint(shift_key, (N_DOM, N_EDGE), 0, 2)
    halved = jnp.right_shift(jnp.full((N_DOM, N_EDGE), CAND, jnp.int32), level_shift.astype(jnp.int32))
    trimmed = jax.random.randint(trim_key, (N_DOM, N_EDGE), 0, 8 * CAND) % (halved // 2)
    counts = halved - trimmed
    full_at = jax.random.randint(full_key, (), 0, N_DOM * N_EDGE)
    device_ids = jnp.arange(N_DOM * N_EDGE).reshape(N_DOM, N_EDGE)
    return jnp.where(device_ids == full_at, CAND, counts).astype(jnp.int32)


def plant(array, own_key, smallest, high):
    dims = array.shape
    spot = [jax.random.randint(jax.random.fold_in(own_key, axis), (), 0, dims[axis]) for axis in range(len(dims))]
    array = array.at[tuple(spot)].set(smallest)
    longest = dims.index(max(dims))
    spot[longest] = (spot[longest] + 1) % dims[longest]
    return array.at[tuple(spot)].set(high)


def block_levels(rng, dims, pieces, low, top_value):
    factor_of = 1.0
    for position, parts in pieces:
        draws = jax.random.uniform(jax.random.fold_in(jax.random.fold_in(rng, 6), position), (parts,), jnp.float32, low / len(pieces), top_value / len(pieces))
        factor_of = factor_of * jnp.repeat(jnp.exp(draws), dims[position] // parts).reshape((-1,) + (1,) * (len(dims) - 1 - position))
    return factor_of


def scatter_about(rng, dims, spread, reach, cuts=(), kind=jnp.bfloat16):
    values = spread * jax.random.normal(rng, dims, jnp.float32)
    if cuts:
        values = values * block_levels(rng, dims, cuts, -0.22, 0.18)
    return jnp.clip(values, -reach, reach).astype(kind)


def setup_inputs(seed: int = 0) -> dict:
    key_of = jax.random.split(jax.random.key(seed), 15)
    return {
        "node_feats": scatter_about(key_of[0], (NODES, D), 1.0, 6.0, ((0, 32),)),
        "gat_weight": scatter_about(key_of[1], (D, D), D ** -0.5, 0.1875, ((0, 4),)),
        "attn_src": draw_attn_src(jax.random.fold_in(key_of[14], 71), 0),
        "attn_dst": draw_attn_dst(jax.random.fold_in(key_of[14], 71), 0),
        "neighbours": plant(jax.random.randint(key_of[4], (NODES, DEG), 0, TABLE), jax.random.fold_in(key_of[4], 1), 0, TABLE - 1).astype(jnp.int32),
        "degree": plant(jax.random.randint(key_of[5], (NODES,), 0, DEG + 1), jax.random.fold_in(key_of[5], 1), 0, DEG).astype(jnp.int32),
        "halo_rows": plant(jax.random.randint(key_of[6], (N_DOM, N_EDGE, N_DOM, BLK), 0, NODE_DEV), jax.random.fold_in(key_of[6], 1), 0, NODE_DEV - 1).astype(jnp.int32),
        "halo_count": draw_halo_count(jax.random.fold_in(key_of[14], 71), 0),
        "endpoint_rows": plant(jax.random.randint(key_of[8], (N_DOM, N_EDGE, N_DOM, N_EDGE, ESLOT), 0, NODE_DEV), jax.random.fold_in(key_of[8], 1), 0, NODE_DEV - 1).astype(jnp.int32),
        "cand_ends": plant(jax.random.randint(key_of[9], (N_DOM, N_EDGE, 2, CAND), 0, SLOTS), jax.random.fold_in(key_of[9], 1), 0, SLOTS - 1).astype(jnp.int32),
        "cand_count": draw_cand_count(jax.random.fold_in(key_of[14], 71), 0),
        "labels": plant((jax.random.randint(key_of[11], (N_DOM, N_EDGE, CAND), 0, 2) < 1).astype(jnp.int32), jax.random.fold_in(key_of[11], 1), 0, 1),
        "mlp_weight": scatter_about(key_of[12], (2 * D, HID), (2 * D) ** -0.5, 0.125, ((0, 4),)),
        "out_weight": scatter_about(key_of[13], (HID,), 0.1, 0.6, (), jnp.float32),
    }


def leaky_relu(values):
    return jnp.where(values > 0, values, 0.2 * values)

def silu_grad(pre_act):
    sigmoid_at = jax.nn.sigmoid(pre_act)
    return sigmoid_at * (1.0 + pre_act * (1.0 - sigmoid_at))

def reference(node_feats, gat_weight, attn_src, attn_dst, neighbours, degree, halo_rows, halo_count, endpoint_rows, cand_ends, cand_count, labels, mlp_weight, out_weight):
    head_size = D // HEADS
    projected = jnp.dot(node_feats, gat_weight, preferred_element_type=jnp.float32).astype(jnp.bfloat16)
    per_head = projected.astype(jnp.float32).reshape(-1, HEADS, head_size)
    src_score = jnp.einsum('nhc,hc->nh', per_head, attn_src, precision=lax.Precision.HIGHEST).astype(jnp.bfloat16)
    dst_score = jnp.einsum('nhc,hc->nh', per_head, attn_dst, precision=lax.Precision.HIGHEST)
    proj_dev = projected.reshape(N_DOM, N_EDGE, NODE_DEV, D)
    src_dev = src_score.reshape(N_DOM, N_EDGE, NODE_DEV, HEADS)
    dst_dev = dst_score.reshape(N_DOM, N_EDGE, NODE_DEV, HEADS)
    neighbour_dev = neighbours.reshape(N_DOM, N_EDGE, NODE_DEV, DEG)
    degree_dev = degree.reshape(N_DOM, N_EDGE, NODE_DEV)
    sources = jnp.arange(N_DOM)[:, None]

    def attend(device):
        dom_at = device // N_EDGE
        edge_at = device % N_EDGE
        own_rows = proj_dev[dom_at, edge_at]
        pick_rows = halo_rows[:, edge_at, dom_at, :]
        blocks = proj_dev[sources, edge_at, pick_rows].reshape(N_DOM * BLK, D)
        key_table = jnp.concatenate([own_rows, blocks], axis=0)
        own_src = src_dev[dom_at, edge_at]
        table_src = jnp.concatenate([own_src, src_dev[sources, edge_at, pick_rows].reshape(N_DOM * BLK, HEADS)], axis=0)
        halo_live = (jnp.arange(BLK)[None, :] < halo_count[:, edge_at, dom_at][:, None]).reshape(N_DOM * BLK)
        table_live = jnp.concatenate([jnp.ones((NODE_DEV,), jnp.bool_), halo_live])
        neighbour_ids = neighbour_dev[dom_at, edge_at]
        live_mask = (jnp.arange(DEG)[None, :] < degree_dev[dom_at, edge_at][:, None]) & table_live[neighbour_ids]
        dst_here = dst_dev[dom_at, edge_at]
        logits = leaky_relu(dst_here[:, None, :] + table_src[neighbour_ids].astype(jnp.float32))
        self_logit = leaky_relu(dst_here + own_src.astype(jnp.float32))
        row_peak = jnp.maximum(self_logit, lax.optimization_barrier(jnp.max(jnp.where(live_mask[:, :, None], logits, -jnp.inf), axis=1)))
        exp_terms = jnp.where(live_mask[:, :, None], jnp.exp(logits - row_peak[:, None, :]), 0.0)
        self_exp = jnp.exp(self_logit - row_peak)
        running = self_exp + lax.optimization_barrier(jnp.sum(exp_terms, axis=1))
        weights = (exp_terms / running[:, None, :]).astype(jnp.bfloat16)
        self_weight = (self_exp / running).astype(jnp.bfloat16)
        gathered = key_table[neighbour_ids].astype(jnp.float32).reshape(NODE_DEV, DEG, HEADS, head_size)
        aggregate = jnp.einsum('rjh,rjhc->rhc', weights.astype(jnp.float32), gathered)
        aggregate = aggregate + self_weight.astype(jnp.float32)[:, :, None] * own_rows.astype(jnp.float32).reshape(NODE_DEV, HEADS, head_size)
        return jax.nn.elu(aggregate).reshape(NODE_DEV, D).astype(jnp.bfloat16)
    node_out = lax.map(attend, jnp.arange(N_DOM * N_EDGE))
    out_dev = node_out.reshape(N_DOM, N_EDGE, NODE_DEV, D)
    owner_dom = jnp.arange(N_DOM)[:, None, None]
    owner_edge = jnp.arange(N_EDGE)[None, :, None]

    def score_device(carry, device):
        dom_at = device // N_EDGE
        edge_at = device % N_EDGE
        pick_rows = endpoint_rows[:, :, dom_at, edge_at, :]
        slot_rows = out_dev[owner_dom, owner_edge, pick_rows].reshape(SLOTS, D)
        end_slots = cand_ends[dom_at, edge_at]
        pair_rows = jnp.concatenate([slot_rows[end_slots[0]], slot_rows[end_slots[1]]], axis=1)
        pre_act = jnp.dot(pair_rows, mlp_weight, preferred_element_type=jnp.float32)
        edge_score = jnp.dot(jax.nn.silu(pre_act), out_weight, precision=lax.Precision.HIGHEST)
        live_mask = jnp.arange(CAND) < cand_count[dom_at, edge_at]
        edge_score = jnp.where(live_mask, edge_score, 0.0)
        grad_score = jnp.where(live_mask, jax.nn.sigmoid(edge_score) - labels[dom_at, edge_at].astype(jnp.float32), 0.0)
        grad_pre = (grad_score[:, None] * out_weight[None, :] * silu_grad(pre_act)).astype(jnp.bfloat16)
        grad_pair = jnp.dot(grad_pre, mlp_weight.T, preferred_element_type=jnp.float32)
        slot_grad = jax.ops.segment_sum(grad_pair[:, :D], end_slots[0], num_segments=SLOTS)
        slot_grad = (slot_grad + jax.ops.segment_sum(grad_pair[:, D:], end_slots[1], num_segments=SLOTS)).astype(jnp.bfloat16)
        targets = ((owner_dom * N_EDGE + owner_edge) * NODE_DEV + pick_rows).reshape(SLOTS)
        carry = carry.at[targets].add(slot_grad.astype(jnp.float32))
        return (carry, edge_score)
    node_grad, scores = lax.scan(score_device, jnp.zeros((NODES, D), jnp.float32), jnp.arange(N_DOM * N_EDGE))
    return (node_out.reshape(NODES, D), scores.reshape(N_DOM, N_EDGE, CAND), node_grad)
```

```python
import functools

import jax
import jax.numpy as jnp
from jax import lax
from jax.experimental import pallas as pl
from jax.experimental.pallas import tpu as pltpu
from jax.sharding import PartitionSpec as P

F32 = jnp.float32
BF16 = jnp.bfloat16
DEAD = 64.0
VMEM = pl.BlockSpec(memory_space=pltpu.VMEM)
SPACES = {
    "v": VMEM,
    "s": pl.BlockSpec(memory_space=pltpu.SMEM),
    "any": pl.BlockSpec(memory_space=pl.ANY),
}


def dot(a, b, dims=((1,), (0,))):
    return lax.dot_general(a, b, (dims, ((), ())), preferred_element_type=F32)


def call(kernel, outs, ins, scratch=()):
    specs = [SPACES[space] for space, _ in ins]
    return pl.pallas_call(
        kernel,
        out_shape=outs,
        in_specs=specs,
        out_specs=jax.tree.map(lambda _: VMEM, outs),
        scratch_shapes=list(scratch),
        compiler_params=pltpu.CompilerParams(vmem_limit_bytes=48 * 1024 * 1024),
    )(*[array for _, array in ins])


def halo_kernel(count_ref, rows_ref, feats_ref, out_ref):
    doms, block = rows_ref.shape
    at = lax.broadcasted_iota(jnp.int32, (1, block), 1)
    pieces = [
        jnp.where(at < count_ref[0, s], rows_ref[s : s + 1, :], -1) for s in range(doms)
    ]
    flat = jnp.concatenate(pieces, axis=1)
    total = doms * block
    nodes = feats_ref.shape[0]
    pick = (lax.broadcasted_iota(jnp.int32, (nodes, total), 0) == flat).astype(F32).astype(BF16)
    rows = dot(pick, feats_ref[...], ((0,), (0,)))
    first = lax.broadcasted_iota(jnp.int32, (16, total), 0) == 0
    dead = jnp.where(first & (flat < 0), 1.0, 0.0).astype(BF16)
    mark_at = (lax.broadcasted_iota(jnp.int32, (16, 128), 0) == 0) & (
        lax.broadcasted_iota(jnp.int32, (16, 128), 1) == 0
    )
    mark = jnp.where(mark_at, DEAD, 0.0).astype(BF16)
    out_ref[:, :128] = (rows[:, :128] + dot(dead, mark, ((0,), (0,)))).astype(BF16)
    out_ref[:, 128:] = rows[:, 128:].astype(BF16)


def count_kernel(neigh_ref, degree_ref, out_ref):
    nodes, table = out_ref.shape
    slots = neigh_ref.shape[0]
    degree = degree_ref[...]
    for base in range(0, table, nodes):
        at = base + lax.broadcasted_iota(jnp.int32, (nodes, nodes), 0)
        total = jnp.zeros((nodes, nodes), F32)
        if base == 0:
            total = (at == lax.broadcasted_iota(jnp.int32, (nodes, nodes), 1)).astype(F32)
        for j in range(slots):
            ids = jnp.where(j < degree, neigh_ref[j : j + 1, :], -1)
            total = total + (at == ids).astype(F32)
        out_ref[:, base : base + nodes] = total.T


def block_diagonal(vectors):
    heads, size = vectors.shape
    wide = jnp.concatenate([vectors] * heads, axis=1)
    lane_head = lax.broadcasted_iota(jnp.int32, wide.shape, 1) // size
    wide = jnp.where(lane_head == lax.broadcasted_iota(jnp.int32, wide.shape, 0), wide, 0.0)
    high = wide.astype(BF16).astype(F32)
    middle = (wide - high).astype(BF16).astype(F32)
    low = (wide - high - middle).astype(BF16).astype(F32)
    return jnp.concatenate([high, middle, low, jnp.zeros_like(wide)], axis=0).astype(BF16)


def load_shards(at_ref, shards, weight_ref, sems):
    depth = shards[0].shape[0]
    copies = []
    for i, shard in enumerate(shards):
        rows = pl.ds(pl.multiple_of(at_ref[i] * depth, depth), depth)
        copies.append(pltpu.make_async_copy(shard, weight_ref.at[rows, :], sems.at[i]))
        copies[-1].start()
    return copies


def attend_kernel(
    shard_count, at_ref, own_ref, got_ref, count_ref, src_ref, dst_ref, ends_ref, *rest
):
    shards = rest[:shard_count]
    out_ref, send_ref, proj_ref, stage_ref, weight_ref, sems = rest[shard_count:]
    copies = load_shards(at_ref, shards, weight_ref, sems)
    nodes, width = own_ref.shape
    heads, size = src_ref.shape
    for copy in copies:
        copy.wait()
    for first, ref in ((0, own_ref), (nodes, got_ref)):
        proj_ref[first : first + ref.shape[0], :] = dot(ref[...], weight_ref[...]).astype(BF16)
    parts = dot(block_diagonal(src_ref[...]), proj_ref[...], ((1,), (1,)))
    src = parts[:heads] + parts[heads : 2 * heads] + parts[2 * heads : 3 * heads]
    src = src.astype(BF16).astype(F32)
    parts = dot(proj_ref[:nodes, :], block_diagonal(dst_ref[...]), ((1,), (1,)))
    dst = parts[:, :heads] + parts[:, heads : 2 * heads] + parts[:, 2 * heads : 3 * heads]
    first_lane = (lax.broadcasted_iota(jnp.int32, (16, 128), 1) == 0).astype(F32).astype(BF16)
    mark = dot(first_lane, got_ref[:, :128], ((1,), (1,)))[:1]
    live = jnp.concatenate([jnp.ones((1, nodes), F32), jnp.where(mark < DEAD / 2, 1.0, 0.0)], axis=1)
    count = count_ref[...] * live
    seen = count > 0
    for h in range(heads):
        logit = dst[:, h : h + 1] + src[h : h + 1, :]
        logit = jnp.where(seen, jnp.maximum(logit, 0.2 * logit), -jnp.inf)
        peak = jnp.max(logit, axis=1, keepdims=True)
        terms = jnp.exp(logit - peak)
        running = jnp.sum(count * terms, axis=1, keepdims=True)
        weight = (terms * (1.0 / running)).astype(BF16).astype(F32) * count
        high = weight.astype(BF16)
        low = (weight - high.astype(F32)).astype(BF16)
        rows = proj_ref[:, h * size : (h + 1) * size]
        total = dot(high, rows) + dot(low, rows)
        total = jnp.where(total > 0, total, jnp.exp(jnp.minimum(total, 0.0)) - 1.0)
        out_ref[:, h * size : (h + 1) * size] = total.astype(BF16)
    slots = ends_ref.shape[1]
    pick = (lax.broadcasted_iota(jnp.int32, (nodes, slots), 0) == ends_ref[...]).astype(F32)
    pack_rows(dot(pick.astype(BF16), out_ref[...], ((0,), (0,))), stage_ref, send_ref)


def pack_rows(rows, stage_ref, out_ref):
    slots, width = rows.shape
    pieces = width // 128
    for c in range(pieces):
        stage_ref[pl.ds(c, slots, stride=pieces), :] = rows[:, c * 128 : (c + 1) * 128]
    out_ref[...] = stage_ref[...].astype(BF16)


def unpack_rows(ref, stage_ref, pieces):
    stage_ref[...] = ref[...].astype(F32)
    slots = ref.shape[0] // pieces
    parts = [stage_ref[pl.ds(c, slots, stride=pieces), :] for c in range(pieces)]
    return jnp.concatenate(parts, axis=1).astype(BF16)


def score_kernel(shard_count, at_ref, live_ref, got_ref, ends_ref, labels_ref, out_w_ref, *rest):
    shards = rest[:shard_count]
    scores_ref, back_ref, pair_ref, stage_ref, weight_ref, sems = rest[shard_count:]
    copies = load_shards(at_ref, shards, weight_ref, sems)
    cands = ends_ref.shape[1]
    width = weight_ref.shape[0] // 2
    slots = got_ref.shape[0] * 128 // width
    rows = unpack_rows(got_ref, stage_ref, width // 128)
    slot_at = lax.broadcasted_iota(jnp.int32, (slots, cands), 0)
    picks = [(slot_at == ends_ref[i : i + 1, :]).astype(F32).astype(BF16) for i in range(2)]
    for i in range(2):
        pair_ref[:, i * width : (i + 1) * width] = dot(picks[i], rows, ((0,), (0,))).astype(BF16)
    for copy in copies:
        copy.wait()
    pre_act = dot(pair_ref[...], weight_ref[...])
    out_w = out_w_ref[...]
    gate = jax.nn.sigmoid(pre_act)
    score = jnp.sum(pre_act * gate * out_w, axis=1, keepdims=True)
    live = lax.broadcasted_iota(jnp.int32, (cands, 1), 0) < live_ref[0, 0]
    score = jnp.where(live, score, 0.0)
    scores_ref[...] = jnp.broadcast_to(score, (cands, 128)).T[:1]
    labels = jnp.broadcast_to(labels_ref[...].astype(F32), (8, cands)).T[:, :1]
    grad_score = jnp.where(live, jax.nn.sigmoid(score) - labels, 0.0)
    grad_pre = (grad_score * out_w * (gate * (1.0 + pre_act * (1.0 - gate)))).astype(BF16)
    slot_grad = jnp.zeros((2 * slots, width), F32)
    for i in range(2):
        total = dot(picks[i], grad_pre)
        high = total.astype(BF16)
        low = (total - high.astype(F32)).astype(BF16)
        both = jnp.concatenate([high, low], axis=0)
        slot_grad = slot_grad + dot(both, weight_ref[i * width : (i + 1) * width, :], ((1,), (1,)))
    pack_rows(slot_grad[:slots] + slot_grad[slots:], stage_ref, back_ref)


def scatter_kernel(ends_ref, got_ref, out_ref, stage_ref):
    nodes, width = out_ref.shape
    slots = ends_ref.shape[1]
    rows = unpack_rows(got_ref, stage_ref, width // 128)
    pick = (lax.broadcasted_iota(jnp.int32, (nodes, slots), 0) == ends_ref[...]).astype(F32)
    out_ref[...] = dot(pick.astype(BF16), rows)


def gather_edge(shard, me, edge_count):
    ys = edge_count // 2
    swap = [(e, e ^ 1) for e in range(edge_count)]
    found, at = [], []
    for k in range(ys):
        here = shard
        if k:
            here = lax.ppermute(
                shard, "edge", [(e, (e + 2 * k) % edge_count) for e in range(edge_count)]
            )
        source = (me - 2 * k) % edge_count
        found += [here, lax.ppermute(here, "edge", swap)]
        at += [source, source ^ 1]
    return found, jnp.stack(at).astype(jnp.int32)


def local(
    node_feats,
    gat_weight,
    attn_src,
    attn_dst,
    neighbours,
    degree,
    halo_rows,
    halo_count,
    endpoint_rows,
    cand_ends,
    cand_count,
    labels,
    mlp_weight,
    out_weight,
):
    nodes, width = node_feats.shape
    dom_count = lax.axis_size("dom")
    edge_count = lax.axis_size("edge")
    me = lax.axis_index("edge")
    block = halo_rows.shape[-1]
    cands = labels.shape[-1]
    hidden = out_weight.shape[0]
    halo = dom_count * block
    table = nodes + halo
    slots = dom_count * edge_count * endpoint_rows.shape[-1]
    pieces = width // 128
    everyone = ("dom", "edge")
    shape = jax.ShapeDtypeStruct

    send_rows = call(
        halo_kernel,
        shape((halo, width), BF16),
        [("s", halo_count[0]), ("v", halo_rows[0, 0]), ("v", node_feats)],
    )
    gat_shards, shard_at = gather_edge(gat_weight, me, edge_count)
    got_rows = lax.all_to_all(send_rows, "dom", split_axis=0, concat_axis=0, tiled=True)
    counts = call(
        count_kernel,
        shape((nodes, table), F32),
        [("v", neighbours.T), ("v", degree.reshape(1, nodes))],
    )
    ends_flat = endpoint_rows.reshape(1, slots)
    mlp_shards, _ = gather_edge(mlp_weight, me, edge_count)
    node_out, send_ends = call(
        functools.partial(attend_kernel, len(gat_shards)),
        (shape((nodes, width), BF16), shape((slots * pieces, 128), BF16)),
        [
            ("s", shard_at),
            ("v", node_feats),
            ("v", got_rows),
            ("v", counts),
            ("v", attn_src),
            ("v", attn_dst),
            ("v", ends_flat),
        ]
        + [("any", w) for w in gat_shards],
        [
            pltpu.VMEM((table, width), BF16),
            pltpu.VMEM((slots * pieces, 128), F32),
            pltpu.VMEM((width, width), BF16),
            pltpu.SemaphoreType.DMA((edge_count,)),
        ],
    )
    got_ends = lax.all_to_all(send_ends, everyone, split_axis=0, concat_axis=0, tiled=True)
    scores, send_back = call(
        functools.partial(score_kernel, len(mlp_shards)),
        (shape((1, cands), F32), shape((slots * pieces, 128), BF16)),
        [
            ("s", shard_at),
            ("s", cand_count),
            ("v", got_ends),
            ("v", cand_ends[0, 0]),
            ("v", labels[0]),
            ("v", out_weight.reshape(1, hidden)),
        ]
        + [("any", w) for w in mlp_shards],
        [
            pltpu.VMEM((cands, 2 * width), BF16),
            pltpu.VMEM((slots * pieces, 128), F32),
            pltpu.VMEM((2 * width, hidden), BF16),
            pltpu.SemaphoreType.DMA((edge_count,)),
        ],
    )
    got_back = lax.all_to_all(send_back, everyone, split_axis=0, concat_axis=0, tiled=True)
    node_grad = call(
        scatter_kernel,
        shape((nodes, width), F32),
        [("v", ends_flat), ("v", got_back)],
        [pltpu.VMEM((slots * pieces, 128), F32)],
    )
    return (node_out, scores.reshape(1, 1, cands), node_grad)


def solution(mesh):
    in_specs = (
        P(("dom", "edge"), None),
        P("edge", None),
        P(),
        P(),
        P(("dom", "edge"), None),
        P(("dom", "edge")),
        P("dom", "edge", None, None),
        P("dom", "edge", None),
        P("dom", "edge", None, None, None),
        P("dom", "edge", None, None),
        P("dom", "edge"),
        P("dom", "edge", None),
        P("edge", None),
        P(),
    )
    out_specs = (P(("dom", "edge"), None), P("dom", "edge", None), P(("dom", "edge"), None))
    return jax.shard_map(local, mesh=mesh, in_specs=in_specs, out_specs=out_specs, check_vma=False)
```

```python
import functools

import jax
import jax.numpy as jnp
from jax import lax
from jax.experimental import pallas as pl
from jax.experimental.pallas import tpu as pltpu
from jax.sharding import PartitionSpec as P

F32 = jnp.float32
BF16 = jnp.bfloat16
DEAD = 64.0
VMEM = pl.BlockSpec(memory_space=pltpu.VMEM)
SPACES = {
    "v": VMEM,
    "s": pl.BlockSpec(memory_space=pltpu.SMEM),
    "any": pl.BlockSpec(memory_space=pl.ANY),
}


def dot(a, b, dims=((1,), (0,))):
    return lax.dot_general(a, b, (dims, ((), ())), preferred_element_type=F32)


def call(kernel, outs, ins, scratch=()):
    fetched = [i for i, (space, _) in enumerate(ins) if space == "f"]

    def body(*refs):
        refs = list(refs)
        local_count = len(fetched) + 1
        own, (held, sems) = refs[:-local_count], (refs[-local_count:-1], refs[-1])
        copies = []
        for n, i in enumerate(fetched):
            copies.append(pltpu.make_async_copy(own[i], held[n], sems.at[n]))
            copies[-1].start()
            own[i] = held[n]

        def ready():
            for copy in copies:
                copy.wait()

        kernel(ready, *own)

    return pl.pallas_call(
        body,
        out_shape=outs,
        in_specs=[SPACES["any" if space == "f" else space] for space, _ in ins],
        out_specs=jax.tree.map(lambda _: VMEM, outs),
        scratch_shapes=list(scratch)
        + [pltpu.VMEM(ins[i][1].shape, ins[i][1].dtype) for i in fetched]
        + [pltpu.SemaphoreType.DMA((max(1, len(fetched)),))],
        compiler_params=pltpu.CompilerParams(vmem_limit_bytes=48 * 1024 * 1024),
    )(*[array for _, array in ins])


def halo_kernel(ready, me_ref, count_ref, rows_ref, feats_ref, *out_refs):
    doms, block = rows_ref.shape
    at = lax.broadcasted_iota(jnp.int32, (1, block), 1)
    ready()
    pieces = []
    for k in range(doms):
        s = me_ref[0] ^ k
        pieces.append(jnp.where(at < count_ref[0, s], rows_ref[pl.ds(s, 1), :], -1))
    flat = jnp.concatenate(pieces, axis=1)
    total = doms * block
    nodes = feats_ref.shape[0]
    pick = (lax.broadcasted_iota(jnp.int32, (nodes, total), 0) == flat).astype(F32).astype(BF16)
    rows = dot(pick, feats_ref[...], ((0,), (0,)))
    first = lax.broadcasted_iota(jnp.int32, (16, total), 0) == 0
    dead = jnp.where(first & (flat < 0), 1.0, 0.0).astype(BF16)
    mark_at = (lax.broadcasted_iota(jnp.int32, (16, 128), 0) == 0) & (
        lax.broadcasted_iota(jnp.int32, (16, 128), 1) == 0
    )
    mark = jnp.where(mark_at, DEAD, 0.0).astype(BF16)
    head = (rows[:, :128] + dot(dead, mark, ((0,), (0,)))).astype(BF16)
    tail = rows[:, 128:].astype(BF16)
    for k, out_ref in enumerate(out_refs):
        out_ref[:, :128] = head[k * block : (k + 1) * block, :]
        out_ref[:, 128:] = tail[k * block : (k + 1) * block, :]


def count_kernel(ready, neigh_ref, degree_ref, out_ref):
    ready()
    nodes, table = out_ref.shape
    slots = neigh_ref.shape[0]
    degree = degree_ref[...]
    for base in range(0, table, nodes):
        at = base + lax.broadcasted_iota(jnp.int32, (nodes, nodes), 0)
        total = jnp.zeros((nodes, nodes), F32)
        if base == 0:
            total = (at == lax.broadcasted_iota(jnp.int32, (nodes, nodes), 1)).astype(F32)
        for j in range(slots):
            ids = jnp.where(j < degree, neigh_ref[j : j + 1, :], -1)
            total = total + (at == ids).astype(F32)
        out_ref[:, base : base + nodes] = total.T


def block_diagonal(vectors):
    heads, size = vectors.shape
    wide = jnp.concatenate([vectors] * heads, axis=1)
    lane_head = lax.broadcasted_iota(jnp.int32, wide.shape, 1) // size
    wide = jnp.where(lane_head == lax.broadcasted_iota(jnp.int32, wide.shape, 0), wide, 0.0)
    high = wide.astype(BF16).astype(F32)
    middle = (wide - high).astype(BF16).astype(F32)
    low = (wide - high - middle).astype(BF16).astype(F32)
    return jnp.concatenate([high, middle, low, jnp.zeros_like(wide)], axis=0).astype(BF16)


def load_shards(at_ref, shards, weight_ref, sems):
    depth = shards[0].shape[0]
    copies = []
    for i, shard in enumerate(shards):
        rows = pl.ds(pl.multiple_of(at_ref[i] * depth, depth), depth)
        copies.append(pltpu.make_async_copy(shard, weight_ref.at[rows, :], sems.at[i]))
        copies[-1].start()
    return copies


def attend_kernel(
    shard_count, ready, at_ref, block_at_ref, own_ref, count_ref, src_ref, dst_ref, ends_ref, *rest
):
    shards, blocks = rest[:shard_count], rest[shard_count:-8]
    out_ref, send_ref, proj_ref, stage_ref, weight_ref, sems, got_ref, block_sems = rest[-8:]
    copies = load_shards(at_ref, shards, weight_ref, sems)
    copies += load_shards(block_at_ref, blocks, got_ref, block_sems)
    ready()
    nodes, width = own_ref.shape
    heads, size = src_ref.shape
    for copy in copies:
        copy.wait()
    for first, ref in ((0, own_ref), (nodes, got_ref)):
        proj_ref[first : first + ref.shape[0], :] = dot(ref[...], weight_ref[...]).astype(BF16)
    parts = dot(block_diagonal(src_ref[...]), proj_ref[...], ((1,), (1,)))
    src = parts[:heads] + parts[heads : 2 * heads] + parts[2 * heads : 3 * heads]
    src = src.astype(BF16).astype(F32)
    parts = dot(proj_ref[:nodes, :], block_diagonal(dst_ref[...]), ((1,), (1,)))
    dst = parts[:, :heads] + parts[:, heads : 2 * heads] + parts[:, 2 * heads : 3 * heads]
    first_lane = (lax.broadcasted_iota(jnp.int32, (16, 128), 1) == 0).astype(F32).astype(BF16)
    mark = dot(first_lane, got_ref[:, :128], ((1,), (1,)))[:1]
    live = jnp.concatenate([jnp.ones((1, nodes), F32), jnp.where(mark < DEAD / 2, 1.0, 0.0)], axis=1)
    count = count_ref[...] * live
    seen = count > 0
    for h in range(heads):
        logit = dst[:, h : h + 1] + src[h : h + 1, :]
        logit = jnp.where(seen, jnp.maximum(logit, 0.2 * logit), -jnp.inf)
        peak = jnp.max(logit, axis=1, keepdims=True)
        terms = jnp.exp(logit - peak)
        running = jnp.sum(count * terms, axis=1, keepdims=True)
        weight = (terms * (1.0 / running)).astype(BF16).astype(F32) * count
        high = weight.astype(BF16)
        low = (weight - high.astype(F32)).astype(BF16)
        rows = proj_ref[:, h * size : (h + 1) * size]
        total = dot(high, rows) + dot(low, rows)
        total = jnp.where(total > 0, total, jnp.exp(jnp.minimum(total, 0.0)) - 1.0)
        out_ref[:, h * size : (h + 1) * size] = total.astype(BF16)
    slots = ends_ref.shape[1]
    pick = (lax.broadcasted_iota(jnp.int32, (nodes, slots), 0) == ends_ref[...]).astype(F32)
    pack_rows(dot(pick.astype(BF16), out_ref[...], ((0,), (0,))), stage_ref, send_ref)


def pack_rows(rows, stage_ref, out_ref):
    slots, width = rows.shape
    pieces = width // 128
    for c in range(pieces):
        stage_ref[pl.ds(c, slots, stride=pieces), :] = rows[:, c * 128 : (c + 1) * 128]
    out_ref[...] = stage_ref[...].astype(BF16)


def unpack_rows(ref, stage_ref, pieces):
    stage_ref[...] = ref[...].astype(F32)
    slots = ref.shape[0] // pieces
    parts = [stage_ref[pl.ds(c, slots, stride=pieces), :] for c in range(pieces)]
    return jnp.concatenate(parts, axis=1).astype(BF16)


def score_kernel(
    shard_count, ready, at_ref, live_ref, got_ref, ends_ref, labels_ref, out_w_ref, *rest
):
    shards = rest[:shard_count]
    scores_ref, back_ref, pair_ref, stage_ref, weight_ref, sems = rest[shard_count:]
    copies = load_shards(at_ref, shards, weight_ref, sems)
    cands = ends_ref.shape[1]
    width = weight_ref.shape[0] // 2
    ready()
    slots = got_ref.shape[0] * 128 // width
    rows = unpack_rows(got_ref, stage_ref, width // 128)
    slot_at = lax.broadcasted_iota(jnp.int32, (slots, cands), 0)
    picks = [(slot_at == ends_ref[i : i + 1, :]).astype(F32).astype(BF16) for i in range(2)]
    for i in range(2):
        pair_ref[:, i * width : (i + 1) * width] = dot(picks[i], rows, ((0,), (0,))).astype(BF16)
    for copy in copies:
        copy.wait()
    pre_act = dot(pair_ref[...], weight_ref[...])
    out_w = out_w_ref[...]
    gate = jax.nn.sigmoid(pre_act)
    score = jnp.sum(pre_act * gate * out_w, axis=1, keepdims=True)
    live = lax.broadcasted_iota(jnp.int32, (cands, 1), 0) < live_ref[0, 0]
    score = jnp.where(live, score, 0.0)
    scores_ref[...] = jnp.broadcast_to(score, (cands, 128)).T[:1]
    labels = jnp.broadcast_to(labels_ref[...].astype(F32), (8, cands)).T[:, :1]
    grad_score = jnp.where(live, jax.nn.sigmoid(score) - labels, 0.0)
    grad_pre = (grad_score * out_w * (gate * (1.0 + pre_act * (1.0 - gate)))).astype(BF16)
    slot_grad = jnp.zeros((2 * slots, width), F32)
    for i in range(2):
        total = dot(picks[i], grad_pre)
        high = total.astype(BF16)
        low = (total - high.astype(F32)).astype(BF16)
        both = jnp.concatenate([high, low], axis=0)
        slot_grad = slot_grad + dot(both, weight_ref[i * width : (i + 1) * width, :], ((1,), (1,)))
    pack_rows(slot_grad[:slots] + slot_grad[slots:], stage_ref, back_ref)


def scatter_kernel(ready, ends_ref, got_ref, out_ref, stage_ref):
    ready()
    nodes, width = out_ref.shape
    slots = ends_ref.shape[1]
    rows = unpack_rows(got_ref, stage_ref, width // 128)
    pick = (lax.broadcasted_iota(jnp.int32, (nodes, slots), 0) == ends_ref[...]).astype(F32)
    out_ref[...] = dot(pick.astype(BF16), rows)


def swap(array, axis, k):
    count = lax.axis_size(axis)
    return lax.ppermute(array, axis, [(i, i ^ k) for i in range(count)])


def across(shard, edge_count):
    return [shard] + [swap(shard, "edge", 2 * k) for k in range(1, edge_count // 2)]


def from_core(shards):
    return [one for shard in shards for one in (shard, swap(shard, "edge", 1))]


def local(
    node_feats,
    gat_weight,
    attn_src,
    attn_dst,
    neighbours,
    degree,
    halo_rows,
    halo_count,
    endpoint_rows,
    cand_ends,
    cand_count,
    labels,
    mlp_weight,
    out_weight,
):
    nodes, width = node_feats.shape
    dom_count = lax.axis_size("dom")
    edge_count = lax.axis_size("edge")
    block = halo_rows.shape[-1]
    cands = labels.shape[-1]
    hidden = out_weight.shape[0]
    halo = dom_count * block
    table = nodes + halo
    slots = dom_count * edge_count * endpoint_rows.shape[-1]
    pieces = width // 128
    everyone = ("dom", "edge")
    shape = jax.ShapeDtypeStruct

    dom_at = (lax.axis_index("dom") ^ jnp.arange(dom_count)).astype(jnp.int32)
    shard_at = (lax.axis_index("edge") ^ jnp.arange(edge_count)).astype(jnp.int32)
    gat_across = across(gat_weight, edge_count)
    blocks = call(
        halo_kernel,
        [shape((block, width), BF16)] * dom_count,
        [("s", dom_at), ("s", halo_count[0]), ("f", halo_rows[0, 0]), ("f", node_feats)],
    )
    blocks = [blocks[0]] + [swap(blocks[k], "dom", k) for k in range(1, dom_count)]
    gat_shards = from_core(gat_across)
    counts = call(
        count_kernel,
        shape((nodes, table), F32),
        [("f", neighbours.T), ("f", degree.reshape(1, nodes))],
    )
    ends_flat = endpoint_rows.reshape(1, slots)
    mlp_weight, *gat_shards = lax.optimization_barrier((mlp_weight, *gat_shards))
    mlp_across = across(mlp_weight, edge_count)
    node_out, send_ends = call(
        functools.partial(attend_kernel, edge_count),
        (shape((nodes, width), BF16), shape((slots * pieces, 128), BF16)),
        [
            ("s", shard_at),
            ("s", dom_at),
            ("f", node_feats),
            ("v", counts),
            ("f", attn_src),
            ("f", attn_dst),
            ("v", ends_flat),
        ]
        + [("any", w) for w in gat_shards + list(blocks)],
        [
            pltpu.VMEM((table, width), BF16),
            pltpu.VMEM((slots * pieces, 128), F32),
            pltpu.VMEM((width, width), BF16),
            pltpu.SemaphoreType.DMA((edge_count,)),
            pltpu.VMEM((halo, width), BF16),
            pltpu.SemaphoreType.DMA((dom_count,)),
        ],
    )
    send_ends, *mlp_across = lax.optimization_barrier((send_ends, *mlp_across))
    mlp_shards = from_core(mlp_across)
    got_ends = lax.all_to_all(send_ends, everyone, split_axis=0, concat_axis=0, tiled=True)
    scores, send_back = call(
        functools.partial(score_kernel, edge_count),
        (shape((1, cands), F32), shape((slots * pieces, 128), BF16)),
        [
            ("s", shard_at),
            ("s", cand_count),
            ("v", got_ends),
            ("f", cand_ends[0, 0]),
            ("f", labels[0]),
            ("f", out_weight.reshape(1, hidden)),
        ]
        + [("any", w) for w in mlp_shards],
        [
            pltpu.VMEM((cands, 2 * width), BF16),
            pltpu.VMEM((slots * pieces, 128), F32),
            pltpu.VMEM((2 * width, hidden), BF16),
            pltpu.SemaphoreType.DMA((edge_count,)),
        ],
    )
    got_back = lax.all_to_all(send_back, everyone, split_axis=0, concat_axis=0, tiled=True)
    node_grad = call(
        scatter_kernel,
        shape((nodes, width), F32),
        [("v", ends_flat), ("v", got_back)],
        [pltpu.VMEM((slots * pieces, 128), F32)],
    )
    return (node_out, scores.reshape(1, 1, cands), node_grad)


def solution(mesh):
    in_specs = (
        P(("dom", "edge"), None),
        P("edge", None),
        P(),
        P(),
        P(("dom", "edge"), None),
        P(("dom", "edge")),
        P("dom", "edge", None, None),
        P("dom", "edge", None),
        P("dom", "edge", None, None, None),
        P("dom", "edge", None, None),
        P("dom", "edge"),
        P("dom", "edge", None),
        P("edge", None),
        P(),
    )
    out_specs = (P(("dom", "edge"), None), P("dom", "edge", None), P(("dom", "edge"), None))
    return jax.shard_map(local, mesh=mesh, in_specs=in_specs, out_specs=out_specs, check_vma=False)
```

```python
import functools

import jax
import jax.numpy as jnp
from jax import lax
from jax.experimental import pallas as pl
from jax.experimental.pallas import tpu as pltpu
from jax.sharding import PartitionSpec as P

F32 = jnp.float32
BF16 = jnp.bfloat16
DEAD = 64.0
VMEM = pl.BlockSpec(memory_space=pltpu.VMEM)
SPACES = {
    "v": VMEM,
    "s": pl.BlockSpec(memory_space=pltpu.SMEM),
    "any": pl.BlockSpec(memory_space=pl.ANY),
}


def dot(a, b, dims=((1,), (0,))):
    return lax.dot_general(a, b, (dims, ((), ())), preferred_element_type=F32)


def call(kernel, outs, ins, scratch=(), vmem_mib=48):
    fetched = [i for i, (space, _) in enumerate(ins) if space == "f"]

    def body(*refs):
        refs = list(refs)
        local_count = len(fetched) + 1
        own, (held, sems) = refs[:-local_count], (refs[-local_count:-1], refs[-1])
        copies = []
        for n, i in enumerate(fetched):
            copies.append(pltpu.make_async_copy(own[i], held[n], sems.at[n]))
            copies[-1].start()
            own[i] = held[n]

        def ready():
            for copy in copies:
                copy.wait()

        kernel(ready, *own)

    return pl.pallas_call(
        body,
        out_shape=outs,
        in_specs=[SPACES["any" if space == "f" else space] for space, _ in ins],
        out_specs=jax.tree.map(lambda _: VMEM, outs),
        scratch_shapes=list(scratch)
        + [pltpu.VMEM(ins[i][1].shape, ins[i][1].dtype) for i in fetched]
        + [pltpu.SemaphoreType.DMA((max(1, len(fetched)),))],
        compiler_params=pltpu.CompilerParams(vmem_limit_bytes=vmem_mib * 1024 * 1024),
    )(*[array for _, array in ins])


def halo_kernel(ready, count_ref, rows_ref, feats_ref, out_ref):
    doms, block = rows_ref.shape
    at = lax.broadcasted_iota(jnp.int32, (1, block), 1)
    ready()
    pieces = [
        jnp.where(at < count_ref[:, s : s + 1], rows_ref[s : s + 1, :], -1) for s in range(doms)
    ]
    flat = jnp.concatenate(pieces, axis=1)
    total = doms * block
    nodes = feats_ref.shape[0]
    pick = (lax.broadcasted_iota(jnp.int32, (nodes, total), 0) == flat).astype(F32).astype(BF16)
    rows = dot(pick, feats_ref[...], ((0,), (0,)))
    first = lax.broadcasted_iota(jnp.int32, (16, total), 0) == 0
    dead = jnp.where(first & (flat < 0), 1.0, 0.0).astype(BF16)
    mark_at = (lax.broadcasted_iota(jnp.int32, (16, 128), 0) == 0) & (
        lax.broadcasted_iota(jnp.int32, (16, 128), 1) == 0
    )
    mark = jnp.where(mark_at, DEAD, 0.0).astype(BF16)
    out_ref[:, :128] = (rows[:, :128] + dot(dead, mark, ((0,), (0,)))).astype(BF16)
    out_ref[:, 128:] = rows[:, 128:].astype(BF16)


def count_kernel(ready, neigh_ref, degree_ref, out_ref):
    ready()
    nodes, table = out_ref.shape
    slots = neigh_ref.shape[0]
    degree = degree_ref[...]
    for base in range(0, table, nodes):
        at = base + lax.broadcasted_iota(jnp.int32, (nodes, nodes), 0)
        total = jnp.zeros((nodes, nodes), F32)
        if base == 0:
            total = (at == lax.broadcasted_iota(jnp.int32, (nodes, nodes), 1)).astype(F32)
        for j in range(slots):
            ids = jnp.where(j < degree, neigh_ref[j : j + 1, :], -1)
            total = total + (at == ids).astype(F32)
        out_ref[:, base : base + nodes] = total.T


def block_diagonal(vectors):
    heads, size = vectors.shape
    wide = jnp.concatenate([vectors] * heads, axis=1)
    lane_head = lax.broadcasted_iota(jnp.int32, wide.shape, 1) // size
    wide = jnp.where(lane_head == lax.broadcasted_iota(jnp.int32, wide.shape, 0), wide, 0.0)
    high = wide.astype(BF16).astype(F32)
    middle = (wide - high).astype(BF16).astype(F32)
    low = (wide - high - middle).astype(BF16).astype(F32)
    return jnp.concatenate([high, middle, low, jnp.zeros_like(wide)], axis=0).astype(BF16)


def load_shards(at_ref, shards, weight_ref, sems):
    depth = shards[0].shape[0]
    copies = []
    for i, shard in enumerate(shards):
        rows = pl.ds(pl.multiple_of(at_ref[i] * depth, depth), depth)
        copies.append(pltpu.make_async_copy(shard, weight_ref.at[rows, :], sems.at[i]))
        copies[-1].start()
    return copies


def attend_kernel(
    shard_count, ready, at_ref, own_ref, got_ref, count_ref, src_ref, dst_ref, ends_ref, *rest
):
    shards = rest[:shard_count]
    out_ref, send_ref, proj_ref, stage_ref, weight_ref, sems = rest[shard_count:]
    copies = load_shards(at_ref, shards, weight_ref, sems)
    ready()
    nodes, width = own_ref.shape
    heads, size = src_ref.shape
    for copy in copies:
        copy.wait()
    for first, ref in ((0, own_ref), (nodes, got_ref)):
        proj_ref[first : first + ref.shape[0], :] = dot(ref[...], weight_ref[...]).astype(BF16)
    parts = dot(block_diagonal(src_ref[...]), proj_ref[...], ((1,), (1,)))
    src = parts[:heads] + parts[heads : 2 * heads] + parts[2 * heads : 3 * heads]
    src = src.astype(BF16).astype(F32)
    parts = dot(proj_ref[:nodes, :], block_diagonal(dst_ref[...]), ((1,), (1,)))
    dst = parts[:, :heads] + parts[:, heads : 2 * heads] + parts[:, 2 * heads : 3 * heads]
    first_lane = (lax.broadcasted_iota(jnp.int32, (16, 128), 1) == 0).astype(F32).astype(BF16)
    mark = dot(first_lane, got_ref[:, :128], ((1,), (1,)))[:1]
    live = jnp.concatenate([jnp.ones((1, nodes), F32), jnp.where(mark < DEAD / 2, 1.0, 0.0)], axis=1)
    count = count_ref[...] * live
    seen = count > 0
    for h in range(heads):
        logit = dst[:, h : h + 1] + src[h : h + 1, :]
        logit = jnp.where(seen, jnp.maximum(logit, 0.2 * logit), -jnp.inf)
        peak = jnp.max(logit, axis=1, keepdims=True)
        terms = jnp.exp(logit - peak)
        running = jnp.sum(count * terms, axis=1, keepdims=True)
        weight = (terms * (1.0 / running)).astype(BF16).astype(F32) * count
        high = weight.astype(BF16)
        low = (weight - high.astype(F32)).astype(BF16)
        rows = proj_ref[:, h * size : (h + 1) * size]
        total = dot(high, rows) + dot(low, rows)
        total = jnp.where(total > 0, total, jnp.exp(jnp.minimum(total, 0.0)) - 1.0)
        out_ref[:, h * size : (h + 1) * size] = total.astype(BF16)
    slots = ends_ref.shape[1]
    pick = (lax.broadcasted_iota(jnp.int32, (nodes, slots), 0) == ends_ref[...]).astype(F32)
    pack_rows(dot(pick.astype(BF16), out_ref[...], ((0,), (0,))), stage_ref, send_ref)


def pack_rows(rows, stage_ref, out_ref):
    slots, width = rows.shape
    pieces = width // 128
    for c in range(pieces):
        stage_ref[pl.ds(c, slots, stride=pieces), :] = rows[:, c * 128 : (c + 1) * 128]
    out_ref[...] = stage_ref[...].astype(BF16)


def unpack_rows(ref, stage_ref, pieces):
    stage_ref[...] = ref[...].astype(F32)
    slots = ref.shape[0] // pieces
    parts = [stage_ref[pl.ds(c, slots, stride=pieces), :] for c in range(pieces)]
    return jnp.concatenate(parts, axis=1).astype(BF16)


def score_kernel(
    shard_count, ready, at_ref, live_ref, got_ref, ends_ref, labels_ref, out_w_ref, *rest
):
    shards = rest[:shard_count]
    scores_ref, back_ref, pair_ref, stage_ref, weight_ref, sems = rest[shard_count:]
    copies = load_shards(at_ref, shards, weight_ref, sems)
    cands = ends_ref.shape[1]
    width = weight_ref.shape[0] // 2
    ready()
    slots = got_ref.shape[0] * 128 // width
    rows = unpack_rows(got_ref, stage_ref, width // 128)
    slot_at = lax.broadcasted_iota(jnp.int32, (slots, cands), 0)
    picks = [(slot_at == ends_ref[i : i + 1, :]).astype(F32).astype(BF16) for i in range(2)]
    for i in range(2):
        pair_ref[:, i * width : (i + 1) * width] = dot(picks[i], rows, ((0,), (0,))).astype(BF16)
    for copy in copies:
        copy.wait()
    pre_act = dot(pair_ref[...], weight_ref[...])
    out_w = out_w_ref[...]
    gate = jax.nn.sigmoid(pre_act)
    score = jnp.sum(pre_act * gate * out_w, axis=1, keepdims=True)
    live = lax.broadcasted_iota(jnp.int32, (cands, 1), 0) < live_ref[0, 0]
    score = jnp.where(live, score, 0.0)
    scores_ref[...] = jnp.broadcast_to(score, (cands, 128)).T[:1]
    labels = jnp.broadcast_to(labels_ref[...].astype(F32), (8, cands)).T[:, :1]
    grad_score = jnp.where(live, jax.nn.sigmoid(score) - labels, 0.0)
    grad_pre = (grad_score * out_w * (gate * (1.0 + pre_act * (1.0 - gate)))).astype(BF16)
    slot_grad = jnp.zeros((2 * slots, width), F32)
    for i in range(2):
        total = dot(picks[i], grad_pre)
        high = total.astype(BF16)
        low = (total - high.astype(F32)).astype(BF16)
        both = jnp.concatenate([high, low], axis=0)
        slot_grad = slot_grad + dot(both, weight_ref[i * width : (i + 1) * width, :], ((1,), (1,)))
    pack_rows(slot_grad[:slots] + slot_grad[slots:], stage_ref, back_ref)


def scatter_kernel(ready, ends_ref, got_ref, out_ref, stage_ref):
    ready()
    nodes, width = out_ref.shape
    slots = ends_ref.shape[1]
    rows = unpack_rows(got_ref, stage_ref, width // 128)
    pick = (lax.broadcasted_iota(jnp.int32, (nodes, slots), 0) == ends_ref[...]).astype(F32)
    out_ref[...] = dot(pick.astype(BF16), rows)


def swap(array, axis, k):
    count = lax.axis_size(axis)
    return lax.ppermute(array, axis, [(i, i ^ k) for i in range(count)])


def across(shard, edge_count):
    return [shard] + [swap(shard, "edge", 2 * k) for k in range(1, edge_count // 2)]


def from_core(shards):
    return [one for shard in shards for one in (shard, swap(shard, "edge", 1))]


def local(
    node_feats,
    gat_weight,
    attn_src,
    attn_dst,
    neighbours,
    degree,
    halo_rows,
    halo_count,
    endpoint_rows,
    cand_ends,
    cand_count,
    labels,
    mlp_weight,
    out_weight,
):
    nodes, width = node_feats.shape
    dom_count = lax.axis_size("dom")
    edge_count = lax.axis_size("edge")
    block = halo_rows.shape[-1]
    cands = labels.shape[-1]
    hidden = out_weight.shape[0]
    halo = dom_count * block
    table = nodes + halo
    slots = dom_count * edge_count * endpoint_rows.shape[-1]
    pieces = width // 128
    everyone = ("dom", "edge")
    shape = jax.ShapeDtypeStruct

    shard_at = (lax.axis_index("edge") ^ jnp.arange(edge_count)).astype(jnp.int32)
    gat_across = across(gat_weight, edge_count)
    send_rows = call(
        halo_kernel,
        shape((halo, width), BF16),
        [("f", halo_count[0]), ("f", halo_rows[0, 0]), ("f", node_feats)],
        vmem_mib=60,
    )
    send_rows, *gat_across = lax.optimization_barrier((send_rows, *gat_across))
    got_rows = lax.all_to_all(send_rows, "dom", split_axis=0, concat_axis=0, tiled=True)
    mlp_weight, *gat_across = lax.optimization_barrier((mlp_weight, *gat_across))
    gat_shards = from_core(gat_across)
    counts = call(
        count_kernel,
        shape((nodes, table), F32),
        [("f", neighbours.T), ("f", degree.reshape(1, nodes))],
    )
    ends_flat = endpoint_rows.reshape(1, slots)
    mlp_across = across(mlp_weight, edge_count)
    node_out, send_ends = call(
        functools.partial(attend_kernel, edge_count),
        (shape((nodes, width), BF16), shape((slots * pieces, 128), BF16)),
        [
            ("s", shard_at),
            ("f", node_feats),
            ("f", got_rows),
            ("f", counts),
            ("f", attn_src),
            ("f", attn_dst),
            ("f", ends_flat),
        ]
        + [("any", w) for w in gat_shards],
        [
            pltpu.VMEM((table, width), BF16),
            pltpu.VMEM((slots * pieces, 128), F32),
            pltpu.VMEM((width, width), BF16),
            pltpu.SemaphoreType.DMA((edge_count,)),
        ],
    )
    send_ends, *mlp_across = lax.optimization_barrier((send_ends, *mlp_across))
    mlp_shards = from_core(mlp_across)
    got_ends = lax.all_to_all(send_ends, everyone, split_axis=0, concat_axis=0, tiled=True)
    scores, send_back = call(
        functools.partial(score_kernel, edge_count),
        (shape((1, cands), F32), shape((slots * pieces, 128), BF16)),
        [
            ("s", shard_at),
            ("s", cand_count),
            ("f", got_ends),
            ("f", cand_ends[0, 0]),
            ("f", labels[0]),
            ("f", out_weight.reshape(1, hidden)),
        ]
        + [("any", w) for w in mlp_shards],
        [
            pltpu.VMEM((cands, 2 * width), BF16),
            pltpu.VMEM((slots * pieces, 128), F32),
            pltpu.VMEM((2 * width, hidden), BF16),
            pltpu.SemaphoreType.DMA((edge_count,)),
        ],
    )
    got_back = lax.all_to_all(send_back, everyone, split_axis=0, concat_axis=0, tiled=True)
    node_grad = call(
        scatter_kernel,
        shape((nodes, width), F32),
        [("f", ends_flat), ("f", got_back)],
        [pltpu.VMEM((slots * pieces, 128), F32)],
    )
    return (node_out, scores.reshape(1, 1, cands), node_grad)


def solution(mesh):
    in_specs = (
        P(("dom", "edge"), None),
        P("edge", None),
        P(),
        P(),
        P(("dom", "edge"), None),
        P(("dom", "edge")),
        P("dom", "edge", None, None),
        P("dom", "edge", None),
        P("dom", "edge", None, None, None),
        P("dom", "edge", None, None),
        P("dom", "edge"),
        P("dom", "edge", None),
        P("edge", None),
        P(),
    )
    out_specs = (P(("dom", "edge"), None), P("dom", "edge", None), P(("dom", "edge"), None))
    return jax.shard_map(local, mesh=mesh, in_specs=in_specs, out_specs=out_specs, check_vma=False)
```

```python
import functools

import jax
import jax.numpy as jnp
from jax import lax
from jax.experimental import pallas as pl
from jax.experimental.pallas import tpu as pltpu
from jax.sharding import PartitionSpec as P

F32 = jnp.float32
BF16 = jnp.bfloat16
DEAD = 64.0
VMEM = pl.BlockSpec(memory_space=pltpu.VMEM)
SPACES = {
    "v": VMEM,
    "s": pl.BlockSpec(memory_space=pltpu.SMEM),
    "any": pl.BlockSpec(memory_space=pl.ANY),
}


def dot(a, b, dims=((1,), (0,))):
    return lax.dot_general(a, b, (dims, ((), ())), preferred_element_type=F32)


def call(kernel, outs, ins, scratch=(), vmem_mib=48):
    fetched = [i for i, (space, _) in enumerate(ins) if space == "f"]

    def body(*refs):
        refs = list(refs)
        local_count = len(fetched) + 1
        own, (held, sems) = refs[:-local_count], (refs[-local_count:-1], refs[-1])
        copies = []
        for n, i in enumerate(fetched):
            copies.append(pltpu.make_async_copy(own[i], held[n], sems.at[n]))
            copies[-1].start()
            own[i] = held[n]

        def ready():
            for copy in copies:
                copy.wait()

        kernel(ready, *own)

    return pl.pallas_call(
        body,
        out_shape=outs,
        in_specs=[SPACES["any" if space == "f" else space] for space, _ in ins],
        out_specs=jax.tree.map(lambda _: VMEM, outs),
        scratch_shapes=list(scratch)
        + [pltpu.VMEM(ins[i][1].shape, ins[i][1].dtype) for i in fetched]
        + [pltpu.SemaphoreType.DMA((max(1, len(fetched)),))],
        compiler_params=pltpu.CompilerParams(vmem_limit_bytes=vmem_mib * 1024 * 1024),
    )(*[array for _, array in ins])


def halo_kernel(ready, count_ref, rows_ref, feats_ref, out_ref):
    doms, block = rows_ref.shape
    at = lax.broadcasted_iota(jnp.int32, (1, block), 1)
    ready()
    pieces = [
        jnp.where(at < count_ref[:, s : s + 1], rows_ref[s : s + 1, :], -1) for s in range(doms)
    ]
    flat = jnp.concatenate(pieces, axis=1)
    total = doms * block
    nodes = feats_ref.shape[0]
    pick = (lax.broadcasted_iota(jnp.int32, (nodes, total), 0) == flat).astype(F32).astype(BF16)
    rows = dot(pick, feats_ref[...], ((0,), (0,)))
    first = lax.broadcasted_iota(jnp.int32, (16, total), 0) == 0
    dead = jnp.where(first & (flat < 0), 1.0, 0.0).astype(BF16)
    mark_at = (lax.broadcasted_iota(jnp.int32, (16, 128), 0) == 0) & (
        lax.broadcasted_iota(jnp.int32, (16, 128), 1) == 0
    )
    mark = jnp.where(mark_at, DEAD, 0.0).astype(BF16)
    out_ref[:, :128] = (rows[:, :128] + dot(dead, mark, ((0,), (0,)))).astype(BF16)
    out_ref[:, 128:] = rows[:, 128:].astype(BF16)


def count_kernel(ready, neigh_ref, degree_ref, out_ref):
    ready()
    nodes, table = out_ref.shape
    slots = neigh_ref.shape[0]
    degree = degree_ref[...]
    for base in range(0, table, nodes):
        at = base + lax.broadcasted_iota(jnp.int32, (nodes, nodes), 0)
        total = jnp.zeros((nodes, nodes), F32)
        if base == 0:
            total = (at == lax.broadcasted_iota(jnp.int32, (nodes, nodes), 1)).astype(F32)
        for j in range(slots):
            ids = jnp.where(j < degree, neigh_ref[j : j + 1, :], -1)
            total = total + (at == ids).astype(F32)
        out_ref[:, base : base + nodes] = total.T


def block_diagonal(vectors):
    heads, size = vectors.shape
    wide = jnp.concatenate([vectors] * heads, axis=1)
    lane_head = lax.broadcasted_iota(jnp.int32, wide.shape, 1) // size
    wide = jnp.where(lane_head == lax.broadcasted_iota(jnp.int32, wide.shape, 0), wide, 0.0)
    high = wide.astype(BF16).astype(F32)
    middle = (wide - high).astype(BF16).astype(F32)
    low = (wide - high - middle).astype(BF16).astype(F32)
    return jnp.concatenate([high, middle, low, jnp.zeros_like(wide)], axis=0).astype(BF16)


def load_shards(at_ref, shards, weight_ref, sems):
    depth = shards[0].shape[0]
    copies = []
    for i, shard in enumerate(shards):
        rows = pl.ds(pl.multiple_of(at_ref[i] * depth, depth), depth)
        copies.append(pltpu.make_async_copy(shard, weight_ref.at[rows, :], sems.at[i]))
        copies[-1].start()
    return copies


def attend_kernel(
    shard_count, ready, at_ref, own_ref, got_ref, count_ref, src_ref, dst_ref, ends_ref, *rest
):
    shards = rest[:shard_count]
    out_ref, send_ref, proj_ref, stage_ref, weight_ref, sems = rest[shard_count:]
    copies = load_shards(at_ref, shards, weight_ref, sems)
    ready()
    nodes, width = own_ref.shape
    heads, size = src_ref.shape
    for copy in copies:
        copy.wait()
    for first, ref in ((0, own_ref), (nodes, got_ref)):
        proj_ref[first : first + ref.shape[0], :] = dot(ref[...], weight_ref[...]).astype(BF16)
    parts = dot(block_diagonal(src_ref[...]), proj_ref[...], ((1,), (1,)))
    src = parts[:heads] + parts[heads : 2 * heads] + parts[2 * heads : 3 * heads]
    src = src.astype(BF16).astype(F32)
    parts = dot(proj_ref[:nodes, :], block_diagonal(dst_ref[...]), ((1,), (1,)))
    dst = parts[:, :heads] + parts[:, heads : 2 * heads] + parts[:, 2 * heads : 3 * heads]
    first_lane = (lax.broadcasted_iota(jnp.int32, (16, 128), 1) == 0).astype(F32).astype(BF16)
    mark = dot(first_lane, got_ref[:, :128], ((1,), (1,)))[:1]
    live = jnp.concatenate([jnp.ones((1, nodes), F32), jnp.where(mark < DEAD / 2, 1.0, 0.0)], axis=1)
    count = count_ref[...] * live
    seen = count > 0
    for h in range(heads):
        logit = dst[:, h : h + 1] + src[h : h + 1, :]
        logit = jnp.where(seen, jnp.maximum(logit, 0.2 * logit), -jnp.inf)
        peak = jnp.max(logit, axis=1, keepdims=True)
        terms = jnp.exp(logit - peak)
        running = jnp.sum(count * terms, axis=1, keepdims=True)
        weight = (terms * (1.0 / running)).astype(BF16).astype(F32) * count
        high = weight.astype(BF16)
        low = (weight - high.astype(F32)).astype(BF16)
        rows = proj_ref[:, h * size : (h + 1) * size]
        total = dot(high, rows) + dot(low, rows)
        total = jnp.where(total > 0, total, jnp.exp(jnp.minimum(total, 0.0)) - 1.0)
        out_ref[:, h * size : (h + 1) * size] = total.astype(BF16)
    slots = ends_ref.shape[1]
    pick = (lax.broadcasted_iota(jnp.int32, (nodes, slots), 0) == ends_ref[...]).astype(F32)
    pack_rows(dot(pick.astype(BF16), out_ref[...], ((0,), (0,))), stage_ref, send_ref)


def pack_rows(rows, stage_ref, out_ref):
    slots, width = rows.shape
    pieces = width // 128
    for c in range(pieces):
        stage_ref[pl.ds(c, slots, stride=pieces), :] = rows[:, c * 128 : (c + 1) * 128]
    out_ref[...] = stage_ref[...].astype(BF16)


def unpack_rows(ref, stage_ref, pieces):
    stage_ref[...] = ref[...].astype(F32)
    slots = ref.shape[0] // pieces
    parts = [stage_ref[pl.ds(c, slots, stride=pieces), :] for c in range(pieces)]
    return jnp.concatenate(parts, axis=1).astype(BF16)


def score_kernel(
    shard_count, ready, at_ref, live_ref, got_ref, ends_ref, labels_ref, out_w_ref, *rest
):
    shards = rest[:shard_count]
    scores_ref, back_ref, pair_ref, stage_ref, weight_ref, sems = rest[shard_count:]
    copies = load_shards(at_ref, shards, weight_ref, sems)
    cands = ends_ref.shape[1]
    width = weight_ref.shape[0] // 2
    ready()
    slots = got_ref.shape[0] * 128 // width
    rows = unpack_rows(got_ref, stage_ref, width // 128)
    slot_at = lax.broadcasted_iota(jnp.int32, (slots, cands), 0)
    picks = [(slot_at == ends_ref[i : i + 1, :]).astype(F32).astype(BF16) for i in range(2)]
    for i in range(2):
        pair_ref[:, i * width : (i + 1) * width] = dot(picks[i], rows, ((0,), (0,))).astype(BF16)
    for copy in copies:
        copy.wait()
    pre_act = dot(pair_ref[...], weight_ref[...])
    out_w = out_w_ref[...]
    gate = jax.nn.sigmoid(pre_act)
    score = jnp.sum(pre_act * gate * out_w, axis=1, keepdims=True)
    live = lax.broadcasted_iota(jnp.int32, (cands, 1), 0) < live_ref[0, 0]
    score = jnp.where(live, score, 0.0)
    scores_ref[...] = jnp.broadcast_to(score, (cands, 128)).T[:1]
    labels = jnp.broadcast_to(labels_ref[...].astype(F32), (8, cands)).T[:, :1]
    grad_score = jnp.where(live, jax.nn.sigmoid(score) - labels, 0.0)
    grad_pre = (grad_score * out_w * (gate * (1.0 + pre_act * (1.0 - gate)))).astype(BF16)
    slot_grad = jnp.zeros((2 * slots, width), F32)
    for i in range(2):
        total = dot(picks[i], grad_pre)
        high = total.astype(BF16)
        low = (total - high.astype(F32)).astype(BF16)
        both = jnp.concatenate([high, low], axis=0)
        slot_grad = slot_grad + dot(both, weight_ref[i * width : (i + 1) * width, :], ((1,), (1,)))
    pack_rows(slot_grad[:slots] + slot_grad[slots:], stage_ref, back_ref)


def scatter_kernel(ready, ends_ref, got_ref, out_ref, stage_ref):
    ready()
    nodes, width = out_ref.shape
    slots = ends_ref.shape[1]
    rows = unpack_rows(got_ref, stage_ref, width // 128)
    pick = (lax.broadcasted_iota(jnp.int32, (nodes, slots), 0) == ends_ref[...]).astype(F32)
    out_ref[...] = dot(pick.astype(BF16), rows)


def swap(array, axis, k):
    count = lax.axis_size(axis)
    return lax.ppermute(array, axis, [(i, i ^ k) for i in range(count)])


def across(shard, edge_count):
    return [shard] + [swap(shard, "edge", 2 * k) for k in range(1, edge_count // 2)]


def from_core(shards):
    return [one for shard in shards for one in (shard, swap(shard, "edge", 1))]


def local(
    node_feats,
    gat_weight,
    attn_src,
    attn_dst,
    neighbours,
    degree,
    halo_rows,
    halo_count,
    endpoint_rows,
    cand_ends,
    cand_count,
    labels,
    mlp_weight,
    out_weight,
):
    nodes, width = node_feats.shape
    dom_count = lax.axis_size("dom")
    edge_count = lax.axis_size("edge")
    block = halo_rows.shape[-1]
    cands = labels.shape[-1]
    hidden = out_weight.shape[0]
    halo = dom_count * block
    table = nodes + halo
    slots = dom_count * edge_count * endpoint_rows.shape[-1]
    pieces = width // 128
    everyone = ("dom", "edge")
    shape = jax.ShapeDtypeStruct

    shard_at = (lax.axis_index("edge") ^ jnp.arange(edge_count)).astype(jnp.int32)
    gat_across = across(gat_weight, edge_count)
    send_rows = call(
        halo_kernel,
        shape((halo, width), BF16),
        [("f", halo_count[0]), ("f", halo_rows[0, 0]), ("f", node_feats)],
        vmem_mib=60,
    )
    gat_across = lax.optimization_barrier((send_rows, *gat_across))[1:]
    got_rows = lax.all_to_all(send_rows, "dom", split_axis=0, concat_axis=0, tiled=True)
    mlp_weight = lax.optimization_barrier((mlp_weight, *gat_across))[0]
    gat_shards = from_core(gat_across)
    counts = call(
        count_kernel,
        shape((nodes, table), F32),
        [("f", neighbours.T), ("f", degree.reshape(1, nodes))],
    )
    ends_flat = endpoint_rows.reshape(1, slots)
    mlp_across = across(mlp_weight, edge_count)
    node_out, send_ends = call(
        functools.partial(attend_kernel, edge_count),
        (shape((nodes, width), BF16), shape((slots * pieces, 128), BF16)),
        [
            ("s", shard_at),
            ("f", node_feats),
            ("f", got_rows),
            ("f", counts),
            ("f", attn_src),
            ("f", attn_dst),
            ("f", ends_flat),
        ]
        + [("any", w) for w in gat_shards],
        [
            pltpu.VMEM((table, width), BF16),
            pltpu.VMEM((slots * pieces, 128), F32),
            pltpu.VMEM((width, width), BF16),
            pltpu.SemaphoreType.DMA((edge_count,)),
        ],
    )
    mlp_across = lax.optimization_barrier((send_ends, *mlp_across))[1:]
    mlp_shards = from_core(mlp_across)
    got_ends = lax.all_to_all(send_ends, everyone, split_axis=0, concat_axis=0, tiled=True)
    scores, send_back = call(
        functools.partial(score_kernel, edge_count),
        (shape((1, cands), F32), shape((slots * pieces, 128), BF16)),
        [
            ("s", shard_at),
            ("s", cand_count),
            ("f", got_ends),
            ("f", cand_ends[0, 0]),
            ("f", labels[0]),
            ("f", out_weight.reshape(1, hidden)),
        ]
        + [("any", w) for w in mlp_shards],
        [
            pltpu.VMEM((cands, 2 * width), BF16),
            pltpu.VMEM((slots * pieces, 128), F32),
            pltpu.VMEM((2 * width, hidden), BF16),
            pltpu.SemaphoreType.DMA((edge_count,)),
        ],
    )
    got_back = lax.all_to_all(send_back, everyone, split_axis=0, concat_axis=0, tiled=True)
    node_grad = call(
        scatter_kernel,
        shape((nodes, width), F32),
        [("f", ends_flat), ("f", got_back)],
        [pltpu.VMEM((slots * pieces, 128), F32)],
    )
    return (node_out, scores.reshape(1, 1, cands), node_grad)


def solution(mesh):
    in_specs = (
        P(("dom", "edge"), None),
        P("edge", None),
        P(),
        P(),
        P(("dom", "edge"), None),
        P(("dom", "edge")),
        P("dom", "edge", None, None),
        P("dom", "edge", None),
        P("dom", "edge", None, None, None),
        P("dom", "edge", None, None),
        P("dom", "edge"),
        P("dom", "edge", None),
        P("edge", None),
        P(),
    )
    out_specs = (P(("dom", "edge"), None), P("dom", "edge", None), P(("dom", "edge"), None))
    return jax.shard_map(local, mesh=mesh, in_specs=in_specs, out_specs=out_specs, check_vma=False)
```

```python
import functools

import jax
import jax.numpy as jnp
from jax import lax
from jax.experimental import pallas as pl
from jax.experimental.pallas import tpu as pltpu
from jax.sharding import PartitionSpec as P

F32 = jnp.float32
BF16 = jnp.bfloat16
LOG2_E = 1.4426950408889634
DEAD = 64.0
VMEM = pl.BlockSpec(memory_space=pltpu.VMEM)
SPACES = {
    "v": VMEM,
    "s": pl.BlockSpec(memory_space=pltpu.SMEM),
    "f": pl.BlockSpec(memory_space=pl.ANY),
}


def dot(a, b, dims=((1,), (0,))):
    return lax.dot_general(a, b, (dims, ((), ())), preferred_element_type=F32)


def call(kernel, outs, ins, scratch=(), vmem_mib=48):
    fetched = [i for i, (space, _) in enumerate(ins) if space == "f"]

    def body(*refs):
        refs = list(refs)
        local_count = len(fetched) + 1
        own, (held, sems) = refs[:-local_count], (refs[-local_count:-1], refs[-1])
        copies = []
        for n, i in enumerate(fetched):
            copies.append(pltpu.make_async_copy(own[i], held[n], sems.at[n]))
            copies[-1].start()
            own[i] = held[n]

        def ready():
            for copy in copies:
                copy.wait()

        kernel(ready, *own)

    return pl.pallas_call(
        body,
        out_shape=outs,
        in_specs=[SPACES[space] for space, _ in ins],
        out_specs=jax.tree.map(lambda _: VMEM, outs),
        scratch_shapes=list(scratch)
        + [pltpu.VMEM(ins[i][1].shape, ins[i][1].dtype) for i in fetched]
        + [pltpu.SemaphoreType.DMA((max(1, len(fetched)),))],
        compiler_params=pltpu.CompilerParams(vmem_limit_bytes=vmem_mib * 1024 * 1024),
    )(*[array for _, array in ins])


def halo_kernel(ready, count_ref, rows_ref, feats_ref, *out_refs):
    doms, block = rows_ref.shape
    at = lax.broadcasted_iota(jnp.int32, (1, block), 1)
    me = lax.axis_index("dom")
    ready()
    pieces = []
    for k in range(doms):
        s = me ^ k
        pieces.append(jnp.where(at < count_ref[0, s], rows_ref[pl.ds(s, 1), :], -1))
    flat = jnp.concatenate(pieces, axis=1)
    total = doms * block
    nodes = feats_ref.shape[0]
    pick = (lax.broadcasted_iota(jnp.int32, (nodes, total), 0) == flat).astype(F32).astype(BF16)
    rows = dot(pick, feats_ref[...], ((0,), (0,)))
    first = lax.broadcasted_iota(jnp.int32, (16, total), 0) == 0
    dead = jnp.where(first & (flat < 0), 1.0, 0.0).astype(BF16)
    mark_at = (lax.broadcasted_iota(jnp.int32, (16, 128), 0) == 0) & (
        lax.broadcasted_iota(jnp.int32, (16, 128), 1) == 0
    )
    mark = jnp.where(mark_at, DEAD, 0.0).astype(BF16)
    head = (rows[:, :128] + dot(dead, mark, ((0,), (0,)))).astype(BF16)
    tail = rows[:, 128:].astype(BF16)
    for k, out_ref in enumerate(out_refs):
        out_ref[:, :128] = head[k * block : (k + 1) * block, :]
        out_ref[:, 128:] = tail[k * block : (k + 1) * block, :]


def block_diagonal(vectors):
    heads, size = vectors.shape
    wide = jnp.concatenate([vectors] * heads, axis=1)
    lane_head = lax.broadcasted_iota(jnp.int32, wide.shape, 1) // size
    wide = jnp.where(lane_head == lax.broadcasted_iota(jnp.int32, wide.shape, 0), wide, 0.0)
    high = wide.astype(BF16).astype(F32)
    middle = (wide - high).astype(BF16).astype(F32)
    low = (wide - high - middle).astype(BF16).astype(F32)
    return jnp.concatenate([high, middle, low, jnp.zeros_like(wide)], axis=0).astype(BF16)


def prepare_kernel(
    block,
    ready,
    live_ref,
    neigh_ref,
    degree_ref,
    src_ref,
    dst_ref,
    ends_ref,
    cand_ref,
    labels_ref,
    out_w_ref,
    gat_ref,
    mlp_ref,
    count_ref,
    factor_ref,
    diag_src_ref,
    diag_dst_ref,
    pick_ref,
    gather_ref,
    scatter_ref,
    known_ref,
    weight_ref,
    gat_own_ref,
    mlp_own_ref,
):
    ready()
    nodes, table = count_ref.shape
    slots = neigh_ref.shape[0]
    ids = neigh_ref[...]
    past = ids - nodes
    moved = nodes + ((past // block) ^ lax.axis_index("dom")) * block + past % block
    ids = jnp.where(ids < nodes, ids, moved)
    ids = jnp.where(lax.broadcasted_iota(jnp.int32, ids.shape, 0) < degree_ref[...], ids, -1)
    for base in range(0, table, nodes):
        at = base + lax.broadcasted_iota(jnp.int32, (nodes, nodes), 0)
        total = jnp.zeros((nodes, nodes), F32)
        if base == 0:
            total = (at == lax.broadcasted_iota(jnp.int32, (nodes, nodes), 1)).astype(F32)
        for j in range(slots):
            total = total + (at == ids[j : j + 1, :]).astype(F32)
        total = total.T
        power = jnp.where(total > 1, 2.0, total)
        power = jnp.where(total > 2, 4.0, power)
        power = jnp.where(total > 5, 8.0, power)
        power = jnp.where(total > 13, 16.0, power)
        count_ref[:, base : base + nodes] = total
        factor_ref[0, :, base : base + nodes] = power.astype(BF16)
        factor_ref[1, :, base : base + nodes] = (total - power).astype(BF16)
    diag_src_ref[...] = block_diagonal(src_ref[...])
    diag_dst_ref[...] = block_diagonal(dst_ref[...])
    ends = ends_ref.shape[1]
    node_at = lax.broadcasted_iota(jnp.int32, (nodes, ends), 0)
    pick_ref[...] = (node_at == ends_ref[...]).astype(F32).astype(BF16)
    cands = cand_ref.shape[1]
    slot_at = lax.broadcasted_iota(jnp.int32, (ends, cands), 0)
    for i in range(2):
        one_hot = (slot_at == cand_ref[i : i + 1, :]).astype(F32)
        scatter_ref[i] = one_hot.astype(BF16)
        gather_ref[i] = one_hot.T.astype(BF16)
    live = (lax.broadcasted_iota(jnp.int32, (1, cands), 1) < live_ref[0, 0]).astype(F32)
    known = jnp.concatenate([live, labels_ref[...].astype(F32), jnp.zeros((126, cands), F32)], axis=0)
    known_ref[...] = known.T
    weight_ref[...] = out_w_ref[...]
    gat_own_ref[...] = gat_ref[...]
    mlp_own_ref[...] = mlp_ref[...]


def shard_dots(rows_ref, shards, whole_ref=None):
    me = lax.axis_index("edge")
    depth = shards[0].shape[0]
    if depth % 128:
        for i, shard in enumerate(shards):
            whole_ref[pl.ds(pl.multiple_of((me ^ i) * depth, depth), depth), :] = shard[...]
        return dot(rows_ref[...], whole_ref[...])
    total = None
    for i, shard in enumerate(shards):
        cols = pl.ds(pl.multiple_of((me ^ i) * depth, depth), depth)
        part = dot(rows_ref[:, cols], shard[...])
        total = part if total is None else total + part
    return total


def attend_kernel(
    shard_count,
    ready,
    own_ref,
    count_ref,
    factor_ref,
    diag_src_ref,
    diag_dst_ref,
    pick_ref,
    *rest,
):
    shards, blocks = rest[:shard_count], rest[shard_count:-8]
    out_ref, send_ref, proj_ref, stage_ref, rows_ref, bias_ref, mix_ref, whole_ref = rest[-8:]
    ready()
    nodes, width = own_ref.shape
    table = proj_ref.shape[0]
    block = blocks[0].shape[0]
    heads = diag_src_ref.shape[0] // 4
    size = width // heads
    rows_ref[:nodes, :] = own_ref[...]
    for k, ref in enumerate(blocks):
        rows_ref[nodes + k * block : nodes + (k + 1) * block, :] = ref[...]
    proj_ref[...] = shard_dots(rows_ref, shards, whole_ref).astype(BF16)
    parts = dot(diag_src_ref[...], proj_ref[...], ((1,), (1,)))
    src = parts[:heads] + parts[heads : 2 * heads] + parts[2 * heads : 3 * heads]
    src = src.astype(BF16).astype(F32) * LOG2_E
    parts = dot(proj_ref[:nodes, :], diag_dst_ref[...], ((1,), (1,)))
    dst = parts[:, :heads] + parts[:, heads : 2 * heads] + parts[:, 2 * heads : 3 * heads]
    dst = dst * LOG2_E
    first_lane = (lax.broadcasted_iota(jnp.int32, (16, 128), 1) == 0).astype(F32).astype(BF16)
    mark = dot(first_lane, rows_ref[nodes:, :128], ((1,), (1,)))[:1]
    hide = jnp.where(mark < DEAD / 2, 0.0, -jnp.inf)
    hide = jnp.concatenate([jnp.zeros((1, nodes), F32), hide], axis=1)
    bias_ref[...] = jnp.where(count_ref[...] > 0, hide, -jnp.inf)
    chunk = 32
    for h in range(heads):
        for r in range(0, nodes, chunk):
            here = slice(r, r + chunk)
            logit = dst[here, h : h + 1] + src[h : h + 1, :]
            logit = jnp.maximum(logit, 0.2 * logit) + bias_ref[here, :]
            terms = jnp.exp2(logit - jnp.max(logit, axis=1, keepdims=True))
            running = jnp.sum(count_ref[here, :] * terms, axis=1, keepdims=True)
            weight = (terms * (1.0 / running)).astype(BF16)
            mix_ref[h % 2, here, :] = weight * factor_ref[0, here, :]
            mix_ref[h % 2, nodes + r : nodes + r + chunk, :] = weight * factor_ref[1, here, :]
        both = dot(mix_ref[h % 2], proj_ref[:, h * size : (h + 1) * size])
        total = both[:nodes] + both[nodes:]
        total = jnp.where(total > 0, total, jnp.exp(jnp.minimum(total, 0.0)) - 1.0)
        out_ref[:, h * size : (h + 1) * size] = total.astype(BF16)
    pack_rows(dot(pick_ref[...], out_ref[...], ((0,), (0,))), stage_ref, send_ref)


def pack_rows(rows, stage_ref, out_ref):
    slots, width = rows.shape
    pieces = width // 128
    for c in range(pieces):
        stage_ref[pl.ds(c, slots, stride=pieces), :] = rows[:, c * 128 : (c + 1) * 128]
    out_ref[...] = stage_ref[...].astype(BF16)


def unpack_rows(ref, stage_ref, pieces):
    stage_ref[...] = ref[...].astype(F32)
    slots = ref.shape[0] // pieces
    parts = [stage_ref[pl.ds(c, slots, stride=pieces), :] for c in range(pieces)]
    return jnp.concatenate(parts, axis=1).astype(BF16)


def score_kernel(
    shard_count, ready, got_ref, gather_ref, scatter_ref, known_ref, out_w_ref, *rest
):
    shards = rest[:shard_count]
    scores_ref, back_ref, pair_ref, stage_ref, sum_ref, grad_ref = rest[shard_count:]
    ready()
    cands = known_ref.shape[0]
    depth = shards[0].shape[0]
    slots, width = grad_ref.shape[1:]
    rows = unpack_rows(got_ref, stage_ref, width // 128)
    for i in range(2):
        pair_ref[:, i * width : (i + 1) * width] = dot(gather_ref[i], rows).astype(BF16)
    pre_act = shard_dots(pair_ref, shards)
    out_w = out_w_ref[...]
    live = known_ref[:, :1]
    gate = jax.nn.sigmoid(pre_act)
    score = jnp.sum(pre_act * gate * out_w, axis=1, keepdims=True) * live
    scores_ref[...] = jnp.broadcast_to(score, (cands, 128)).T[:1]
    grad_score = (jax.nn.sigmoid(score) - known_ref[:, 1:2]) * live
    grad_pre = (grad_score * out_w * (gate * (1.0 + pre_act * (1.0 - gate)))).astype(BF16)
    for i in range(2):
        total = dot(scatter_ref[i], grad_pre)
        high = total.astype(BF16)
        sum_ref[i, :slots, :] = high
        sum_ref[i, slots:, :] = (total - high.astype(F32)).astype(BF16)
    per_half = width // depth
    for i, shard in enumerate(shards):
        at = lax.axis_index("edge") ^ i
        half = at // per_half
        col = pl.multiple_of((at % per_half) * depth, depth)
        both = dot(sum_ref[half], shard[...], ((1,), (1,)))
        grad_ref[half, :, pl.ds(col, depth)] = both[:slots] + both[slots:]
    pack_rows(grad_ref[0] + grad_ref[1], stage_ref, back_ref)


def scatter_kernel(ready, pick_ref, got_ref, out_ref, stage_ref):
    ready()
    rows = unpack_rows(got_ref, stage_ref, out_ref.shape[1] // 128)
    out_ref[...] = dot(pick_ref[...], rows)


def swap(array, axis, k):
    count = lax.axis_size(axis)
    return lax.ppermute(array, axis, [(i, i ^ k) for i in range(count)])


def across(shard, edge_count):
    return [shard] + [swap(shard, "edge", 2 * k) for k in range(1, edge_count // 2)]


def from_core(shards):
    return [one for shard in shards for one in (shard, swap(shard, "edge", 1))]


def local(
    node_feats,
    gat_weight,
    attn_src,
    attn_dst,
    neighbours,
    degree,
    halo_rows,
    halo_count,
    endpoint_rows,
    cand_ends,
    cand_count,
    labels,
    mlp_weight,
    out_weight,
):
    nodes, width = node_feats.shape
    dom_count = lax.axis_size("dom")
    edge_count = lax.axis_size("edge")
    block = halo_rows.shape[-1]
    cands = labels.shape[-1]
    hidden = out_weight.shape[0]
    halo = dom_count * block
    table = nodes + halo
    slots = dom_count * edge_count * endpoint_rows.shape[-1]
    pieces = width // 128
    everyone = ("dom", "edge")
    shape = jax.ShapeDtypeStruct

    heads = attn_src.shape[0]
    gat_across = across(gat_weight, edge_count)
    blocks = call(
        halo_kernel,
        [shape((block, width), BF16)] * dom_count,
        [("s", halo_count[0]), ("f", halo_rows[0, 0]), ("f", node_feats)],
        vmem_mib=60,
    )
    far = range(dom_count // 2, dom_count)
    moved = {0: blocks[0]}
    for k in [*far, *range(1, dom_count // 2)]:
        moved[k] = swap(blocks[k], "dom", k)
    gat_across = lax.optimization_barrier((*gat_across, *[moved[k] for k in far]))[: len(gat_across)]
    held_mlp = lax.optimization_barrier((mlp_weight, *gat_across))[0]
    gat_shards = from_core(gat_across)
    prepared = call(
        functools.partial(prepare_kernel, block),
        (
            shape((nodes, table), F32),
            shape((2, nodes, table), BF16),
            shape((4 * heads, width), BF16),
            shape((4 * heads, width), BF16),
            shape((nodes, slots), BF16),
            shape((2, cands, slots), BF16),
            shape((2, slots, cands), BF16),
            shape((cands, 128), F32),
            shape((1, hidden), F32),
            shape(gat_weight.shape, BF16),
            shape(mlp_weight.shape, BF16),
        ),
        [
            ("s", cand_count),
            ("f", neighbours.T),
            ("f", degree.reshape(1, nodes)),
            ("f", attn_src),
            ("f", attn_dst),
            ("f", endpoint_rows.reshape(1, slots)),
            ("f", cand_ends[0, 0]),
            ("f", labels[0]),
            ("f", out_weight.reshape(1, hidden)),
            ("f", gat_weight),
            ("f", mlp_weight),
        ],
    )
    counts, factors, diag_src, diag_dst, pick, gather, scatter, known, out_row, *own = prepared
    gat_shards[0] = own[0]
    mlp_across = across(held_mlp, edge_count)
    packed = pltpu.VMEM((slots * pieces, 128), F32)
    node_out, send_ends = call(
        functools.partial(attend_kernel, edge_count),
        (shape((nodes, width), BF16), shape((slots * pieces, 128), BF16)),
        [
            ("v", node_feats),
            ("v", counts),
            ("v", factors),
            ("v", diag_src),
            ("v", diag_dst),
            ("v", pick),
        ]
        + [("v", w) for w in gat_shards]
        + [("v", moved[k]) for k in range(dom_count)],
        [
            pltpu.VMEM((table, width), BF16),
            packed,
            pltpu.VMEM((table, width), BF16),
            pltpu.VMEM((nodes, table), F32),
            pltpu.VMEM((2, 2 * nodes, table), BF16),
            pltpu.VMEM((width if width // edge_count % 128 else 16, width), BF16),
        ],
    )
    mlp_across = lax.optimization_barrier((send_ends, *mlp_across))[1:]
    mlp_shards = from_core(mlp_across)
    mlp_shards[0] = own[1]
    got_ends = lax.all_to_all(send_ends, everyone, split_axis=0, concat_axis=0, tiled=True)
    scores, send_back = call(
        functools.partial(score_kernel, edge_count),
        (shape((1, cands), F32), shape((slots * pieces, 128), BF16)),
        [
            ("v", got_ends),
            ("v", gather),
            ("v", scatter),
            ("v", known),
            ("v", out_row),
        ]
        + [("v", w) for w in mlp_shards],
        [
            pltpu.VMEM((cands, 2 * width), BF16),
            packed,
            pltpu.VMEM((2, 2 * slots, hidden), BF16),
            pltpu.VMEM((2, slots, width), F32),
        ],
    )
    got_back = lax.all_to_all(send_back, everyone, split_axis=0, concat_axis=0, tiled=True)
    node_grad = call(
        scatter_kernel, shape((nodes, width), F32), [("v", pick), ("v", got_back)], [packed]
    )
    return (node_out, scores.reshape(1, 1, cands), node_grad)


def solution(mesh):
    in_specs = (
        P(("dom", "edge"), None),
        P("edge", None),
        P(),
        P(),
        P(("dom", "edge"), None),
        P(("dom", "edge")),
        P("dom", "edge", None, None),
        P("dom", "edge", None),
        P("dom", "edge", None, None, None),
        P("dom", "edge", None, None),
        P("dom", "edge"),
        P("dom", "edge", None),
        P("edge", None),
        P(),
    )
    out_specs = (P(("dom", "edge"), None), P("dom", "edge", None), P(("dom", "edge"), None))
    return jax.shard_map(local, mesh=mesh, in_specs=in_specs, out_specs=out_specs, check_vma=False)
```

```python
import functools

import jax
import jax.numpy as jnp
from jax import lax
from jax.experimental import pallas as pl
from jax.experimental.pallas import tpu as pltpu
from jax.sharding import PartitionSpec as P

F32 = jnp.float32
BF16 = jnp.bfloat16
LOG2_E = 1.4426950408889634
DEAD = 64.0
VMEM = pl.BlockSpec(memory_space=pltpu.VMEM)
SPACES = {
    "v": VMEM,
    "s": pl.BlockSpec(memory_space=pltpu.SMEM),
    "f": pl.BlockSpec(memory_space=pl.ANY),
}


def dot(a, b, dims=((1,), (0,))):
    return lax.dot_general(a, b, (dims, ((), ())), preferred_element_type=F32)


def call(kernel, outs, ins, scratch=(), vmem_mib=48):
    fetched = [i for i, (space, _) in enumerate(ins) if space == "f"]

    def body(*refs):
        refs = list(refs)
        local_count = len(fetched) + 1
        own, (held, sems) = refs[:-local_count], (refs[-local_count:-1], refs[-1])
        copies = []
        for n, i in enumerate(fetched):
            copies.append(pltpu.make_async_copy(own[i], held[n], sems.at[n]))
            copies[-1].start()
            own[i] = held[n]

        def ready():
            for copy in copies:
                copy.wait()

        kernel(ready, *own)

    return pl.pallas_call(
        body,
        out_shape=outs,
        in_specs=[SPACES[space] for space, _ in ins],
        out_specs=jax.tree.map(lambda _: VMEM, outs),
        scratch_shapes=list(scratch)
        + [pltpu.VMEM(ins[i][1].shape, ins[i][1].dtype) for i in fetched]
        + [pltpu.SemaphoreType.DMA((max(1, len(fetched)),))],
        compiler_params=pltpu.CompilerParams(vmem_limit_bytes=vmem_mib * 1024 * 1024),
    )(*[array for _, array in ins])


def halo_kernel(ready, count_ref, rows_ref, feats_ref, out_ref):
    doms, block = rows_ref.shape
    at = lax.broadcasted_iota(jnp.int32, (1, block), 1)
    ready()
    pieces = [
        jnp.where(at < count_ref[:, s : s + 1], rows_ref[s : s + 1, :], -1) for s in range(doms)
    ]
    flat = jnp.concatenate(pieces, axis=1)
    total = doms * block
    nodes = feats_ref.shape[0]
    pick = (lax.broadcasted_iota(jnp.int32, (nodes, total), 0) == flat).astype(F32).astype(BF16)
    rows = dot(pick, feats_ref[...], ((0,), (0,)))
    first = lax.broadcasted_iota(jnp.int32, (16, total), 0) == 0
    dead = jnp.where(first & (flat < 0), 1.0, 0.0).astype(BF16)
    mark_at = (lax.broadcasted_iota(jnp.int32, (16, 128), 0) == 0) & (
        lax.broadcasted_iota(jnp.int32, (16, 128), 1) == 0
    )
    mark = jnp.where(mark_at, DEAD, 0.0).astype(BF16)
    out_ref[:, :128] = (rows[:, :128] + dot(dead, mark, ((0,), (0,)))).astype(BF16)
    out_ref[:, 128:] = rows[:, 128:].astype(BF16)


def block_diagonal(vectors):
    heads, size = vectors.shape
    wide = jnp.concatenate([vectors] * heads, axis=1)
    lane_head = lax.broadcasted_iota(jnp.int32, wide.shape, 1) // size
    wide = jnp.where(lane_head == lax.broadcasted_iota(jnp.int32, wide.shape, 0), wide, 0.0)
    high = wide.astype(BF16).astype(F32)
    middle = (wide - high).astype(BF16).astype(F32)
    low = (wide - high - middle).astype(BF16).astype(F32)
    return jnp.concatenate([high, middle, low, jnp.zeros_like(wide)], axis=0).astype(BF16)


def prepare_kernel(
    ready,
    live_ref,
    neigh_ref,
    degree_ref,
    src_ref,
    dst_ref,
    ends_ref,
    cand_ref,
    labels_ref,
    out_w_ref,
    gat_ref,
    mlp_ref,
    count_ref,
    factor_ref,
    diag_src_ref,
    diag_dst_ref,
    pick_ref,
    gather_ref,
    scatter_ref,
    known_ref,
    weight_ref,
    gat_own_ref,
    *mlp_own_refs,
):
    ready()
    nodes, table = count_ref.shape
    slots = neigh_ref.shape[0]
    ids = neigh_ref[...]
    ids = jnp.where(lax.broadcasted_iota(jnp.int32, ids.shape, 0) < degree_ref[...], ids, -1)
    for base in range(0, table, nodes):
        at = base + lax.broadcasted_iota(jnp.int32, (nodes, nodes), 0)
        total = jnp.zeros((nodes, nodes), F32)
        if base == 0:
            total = (at == lax.broadcasted_iota(jnp.int32, (nodes, nodes), 1)).astype(F32)
        for j in range(slots):
            total = total + (at == ids[j : j + 1, :]).astype(F32)
        total = total.T
        power = jnp.where(total > 1, 2.0, total)
        power = jnp.where(total > 2, 4.0, power)
        power = jnp.where(total > 5, 8.0, power)
        power = jnp.where(total > 13, 16.0, power)
        count_ref[:, base : base + nodes] = total
        factor_ref[0, :, base : base + nodes] = power.astype(BF16)
        factor_ref[1, :, base : base + nodes] = (total - power).astype(BF16)
    diag_src_ref[...] = block_diagonal(src_ref[...])
    diag_dst_ref[...] = block_diagonal(dst_ref[...])
    ends = ends_ref.shape[1]
    node_at = lax.broadcasted_iota(jnp.int32, (nodes, ends), 0)
    pick_ref[...] = (node_at == ends_ref[...]).astype(F32).astype(BF16)
    cands = cand_ref.shape[1]
    slot_at = lax.broadcasted_iota(jnp.int32, (ends, cands), 0)
    for i in range(2):
        one_hot = (slot_at == cand_ref[i : i + 1, :]).astype(F32)
        scatter_ref[i] = one_hot.astype(BF16)
        gather_ref[i] = one_hot.T.astype(BF16)
    live = (lax.broadcasted_iota(jnp.int32, (1, cands), 1) < live_ref[0, 0]).astype(F32)
    known = jnp.concatenate([live, labels_ref[...].astype(F32), jnp.zeros((126, cands), F32)], axis=0)
    known_ref[...] = known.T
    weight_ref[...] = out_w_ref[...]
    gat_own_ref[...] = gat_ref[...]
    depth = mlp_own_refs[0].shape[0]
    for i, ref in enumerate(mlp_own_refs):
        ref[...] = mlp_ref[i * depth : (i + 1) * depth, :]


def shard_row(i, shards):
    depth = shards[0].shape[0]
    parts = len(shards) // lax.axis_size("edge")
    at = (lax.axis_index("edge") ^ (i // parts)) * parts + i % parts
    return pl.multiple_of(at * depth, depth)


def shard_dots(rows_ref, shards, whole_ref=None):
    depth = shards[0].shape[0]
    if depth % 128:
        for i, shard in enumerate(shards):
            whole_ref[pl.ds(shard_row(i, shards), depth), :] = shard[...]
        return dot(rows_ref[...], whole_ref[...])
    total = None
    for i, shard in enumerate(shards):
        cols = pl.ds(shard_row(i, shards), depth)
        part = dot(rows_ref[:, cols], shard[...])
        total = part if total is None else total + part
    return total


def attend_kernel(
    shard_count,
    ready,
    own_ref,
    got_ref,
    count_ref,
    factor_ref,
    diag_src_ref,
    diag_dst_ref,
    pick_ref,
    *rest,
):
    shards = rest[:shard_count]
    out_ref, send_ref, proj_ref, stage_ref, rows_ref, bias_ref, mix_ref, whole_ref = rest[-8:]
    ready()
    nodes, width = own_ref.shape
    table = proj_ref.shape[0]
    heads = diag_src_ref.shape[0] // 4
    size = width // heads
    rows_ref[:nodes, :] = own_ref[...]
    rows_ref[nodes:, :] = got_ref[...]
    proj_ref[...] = shard_dots(rows_ref, shards, whole_ref).astype(BF16)
    parts = dot(diag_src_ref[...], proj_ref[...], ((1,), (1,)))
    src = parts[:heads] + parts[heads : 2 * heads] + parts[2 * heads : 3 * heads]
    src = src.astype(BF16).astype(F32) * LOG2_E
    parts = dot(proj_ref[:nodes, :], diag_dst_ref[...], ((1,), (1,)))
    dst = parts[:, :heads] + parts[:, heads : 2 * heads] + parts[:, 2 * heads : 3 * heads]
    dst = dst * LOG2_E
    first_lane = (lax.broadcasted_iota(jnp.int32, (16, 128), 1) == 0).astype(F32).astype(BF16)
    mark = dot(first_lane, rows_ref[nodes:, :128], ((1,), (1,)))[:1]
    hide = jnp.where(mark < DEAD / 2, 0.0, -jnp.inf)
    hide = jnp.concatenate([jnp.zeros((1, nodes), F32), hide], axis=1)
    bias_ref[...] = jnp.where(count_ref[...] > 0, hide, -jnp.inf)
    chunk = 32
    for h in range(heads):
        for r in range(0, nodes, chunk):
            here = slice(r, r + chunk)
            logit = dst[here, h : h + 1] + src[h : h + 1, :]
            logit = jnp.maximum(logit, 0.2 * logit) + bias_ref[here, :]
            terms = jnp.exp2(logit - jnp.max(logit, axis=1, keepdims=True))
            running = jnp.sum(count_ref[here, :] * terms, axis=1, keepdims=True)
            weight = (terms * (1.0 / running)).astype(BF16)
            mix_ref[h % 2, here, :] = weight * factor_ref[0, here, :]
            mix_ref[h % 2, nodes + r : nodes + r + chunk, :] = weight * factor_ref[1, here, :]
        both = dot(mix_ref[h % 2], proj_ref[:, h * size : (h + 1) * size])
        total = both[:nodes] + both[nodes:]
        total = jnp.where(total > 0, total, jnp.exp(jnp.minimum(total, 0.0)) - 1.0)
        out_ref[:, h * size : (h + 1) * size] = total.astype(BF16)
    pack_rows(dot(pick_ref[...], out_ref[...], ((0,), (0,))), stage_ref, send_ref)


def pack_rows(rows, stage_ref, out_ref):
    slots, width = rows.shape
    pieces = width // 128
    for c in range(pieces):
        stage_ref[pl.ds(c, slots, stride=pieces), :] = rows[:, c * 128 : (c + 1) * 128]
    out_ref[...] = stage_ref[...].astype(BF16)


def unpack_rows(ref, stage_ref, pieces):
    stage_ref[...] = ref[...].astype(F32)
    slots = ref.shape[0] // pieces
    parts = [stage_ref[pl.ds(c, slots, stride=pieces), :] for c in range(pieces)]
    return jnp.concatenate(parts, axis=1).astype(BF16)


def score_kernel(
    shard_count, ready, got_ref, gather_ref, scatter_ref, known_ref, out_w_ref, *rest
):
    shards = rest[:shard_count]
    scores_ref, back_ref, pair_ref, stage_ref, sum_ref, grad_ref = rest[shard_count:]
    ready()
    cands = known_ref.shape[0]
    depth = shards[0].shape[0]
    slots, width = grad_ref.shape[1:]
    rows = unpack_rows(got_ref, stage_ref, width // 128)
    for i in range(2):
        pair_ref[:, i * width : (i + 1) * width] = dot(gather_ref[i], rows).astype(BF16)
    pre_act = shard_dots(pair_ref, shards)
    out_w = out_w_ref[...]
    live = known_ref[:, :1]
    gate = jax.nn.sigmoid(pre_act)
    score = jnp.sum(pre_act * gate * out_w, axis=1, keepdims=True) * live
    scores_ref[...] = jnp.broadcast_to(score, (cands, 128)).T[:1]
    grad_score = (jax.nn.sigmoid(score) - known_ref[:, 1:2]) * live
    grad_pre = (grad_score * out_w * (gate * (1.0 + pre_act * (1.0 - gate)))).astype(BF16)
    for i in range(2):
        total = dot(scatter_ref[i], grad_pre)
        high = total.astype(BF16)
        sum_ref[i, :slots, :] = high
        sum_ref[i, slots:, :] = (total - high.astype(F32)).astype(BF16)
    for i, shard in enumerate(shards):
        row = shard_row(i, shards)
        half = row // width
        col = pl.multiple_of(row % width, depth)
        both = dot(sum_ref[half], shard[...], ((1,), (1,)))
        grad_ref[half, :, pl.ds(col, depth)] = both[:slots] + both[slots:]
    pack_rows(grad_ref[0] + grad_ref[1], stage_ref, back_ref)


def scatter_kernel(ready, pick_ref, got_ref, out_ref, stage_ref):
    ready()
    rows = unpack_rows(got_ref, stage_ref, out_ref.shape[1] // 128)
    out_ref[...] = dot(pick_ref[...], rows)


def swap(array, axis, k):
    count = lax.axis_size(axis)
    return lax.ppermute(array, axis, [(i, i ^ k) for i in range(count)])


def across(shard, edge_count):
    return [shard] + [swap(shard, "edge", 2 * k) for k in range(1, edge_count // 2)]


def from_core(shards):
    return [one for shard in shards for one in (shard, swap(shard, "edge", 1))]


def local(
    node_feats,
    gat_weight,
    attn_src,
    attn_dst,
    neighbours,
    degree,
    halo_rows,
    halo_count,
    endpoint_rows,
    cand_ends,
    cand_count,
    labels,
    mlp_weight,
    out_weight,
):
    nodes, width = node_feats.shape
    dom_count = lax.axis_size("dom")
    edge_count = lax.axis_size("edge")
    block = halo_rows.shape[-1]
    cands = labels.shape[-1]
    hidden = out_weight.shape[0]
    halo = dom_count * block
    table = nodes + halo
    slots = dom_count * edge_count * endpoint_rows.shape[-1]
    pieces = width // 128
    everyone = ("dom", "edge")
    shape = jax.ShapeDtypeStruct

    heads = attn_src.shape[0]
    parts = 2 if mlp_weight.shape[0] % 256 == 0 else 1
    gat_across = across(gat_weight, edge_count)
    send_rows = call(
        halo_kernel,
        shape((halo, width), BF16),
        [("f", halo_count[0]), ("f", halo_rows[0, 0]), ("f", node_feats)],
        vmem_mib=60,
    )
    gat_across = lax.optimization_barrier((*gat_across, send_rows))[: len(gat_across)]
    got_rows = lax.all_to_all(send_rows, "dom", split_axis=0, concat_axis=0, tiled=True)
    mlp_parts = jnp.split(lax.optimization_barrier((mlp_weight, send_rows))[0], parts)
    mlp_across = [across(mlp_parts[0], edge_count)]
    gat_shards = from_core(gat_across)
    for part in mlp_parts[1:]:
        part = lax.optimization_barrier((part, *gat_across))[0]
        mlp_across.append(across(part, edge_count))
    prepared = call(
        prepare_kernel,
        (
            shape((nodes, table), F32),
            shape((2, nodes, table), BF16),
            shape((4 * heads, width), BF16),
            shape((4 * heads, width), BF16),
            shape((nodes, slots), BF16),
            shape((2, cands, slots), BF16),
            shape((2, slots, cands), BF16),
            shape((cands, 128), F32),
            shape((1, hidden), F32),
            shape(gat_weight.shape, BF16),
        )
        + (shape(mlp_parts[0].shape, BF16),) * parts,
        [
            ("s", cand_count),
            ("f", neighbours.T),
            ("f", degree.reshape(1, nodes)),
            ("f", attn_src),
            ("f", attn_dst),
            ("f", endpoint_rows.reshape(1, slots)),
            ("f", cand_ends[0, 0]),
            ("f", labels[0]),
            ("f", out_weight.reshape(1, hidden)),
            ("f", gat_weight),
            ("f", mlp_weight),
        ],
    )
    counts, factors, diag_src, diag_dst, pick, gather, scatter, known, out_row, *own = prepared
    gat_shards[0] = own[0]
    packed = pltpu.VMEM((slots * pieces, 128), F32)
    node_out, send_ends = call(
        functools.partial(attend_kernel, edge_count),
        (shape((nodes, width), BF16), shape((slots * pieces, 128), BF16)),
        [
            ("v", node_feats),
            ("v", got_rows),
            ("v", counts),
            ("v", factors),
            ("v", diag_src),
            ("v", diag_dst),
            ("v", pick),
        ]
        + [("v", w) for w in gat_shards],
        [
            pltpu.VMEM((table, width), BF16),
            packed,
            pltpu.VMEM((table, width), BF16),
            pltpu.VMEM((nodes, table), F32),
            pltpu.VMEM((2, 2 * nodes, table), BF16),
            pltpu.VMEM((width if width // edge_count % 128 else 16, width), BF16),
        ],
    )
    mlp_across[-1] = lax.optimization_barrier((send_ends, *mlp_across[-1]))[1:]
    for part in mlp_across[:-1]:
        part[0] = lax.optimization_barrier((part[0], *gat_across))[0]
    mlp_found = [from_core(part) for part in mlp_across]
    for found, held in zip(mlp_found, own[1:]):
        found[0] = held
    mlp_shards = [found[e] for e in range(edge_count) for found in mlp_found]
    got_ends = lax.all_to_all(send_ends, everyone, split_axis=0, concat_axis=0, tiled=True)
    scores, send_back = call(
        functools.partial(score_kernel, len(mlp_shards)),
        (shape((1, cands), F32), shape((slots * pieces, 128), BF16)),
        [
            ("v", got_ends),
            ("v", gather),
            ("v", scatter),
            ("v", known),
            ("v", out_row),
        ]
        + [("v", w) for w in mlp_shards],
        [
            pltpu.VMEM((cands, 2 * width), BF16),
            packed,
            pltpu.VMEM((2, 2 * slots, hidden), BF16),
            pltpu.VMEM((2, slots, width), F32),
        ],
    )
    got_back = lax.all_to_all(send_back, everyone, split_axis=0, concat_axis=0, tiled=True)
    node_grad = call(
        scatter_kernel, shape((nodes, width), F32), [("v", pick), ("v", got_back)], [packed]
    )
    return (node_out, scores.reshape(1, 1, cands), node_grad)


def solution(mesh):
    in_specs = (
        P(("dom", "edge"), None),
        P("edge", None),
        P(),
        P(),
        P(("dom", "edge"), None),
        P(("dom", "edge")),
        P("dom", "edge", None, None),
        P("dom", "edge", None),
        P("dom", "edge", None, None, None),
        P("dom", "edge", None, None),
        P("dom", "edge"),
        P("dom", "edge", None),
        P("edge", None),
        P(),
    )
    out_specs = (P(("dom", "edge"), None), P("dom", "edge", None), P(("dom", "edge"), None))
    return jax.shard_map(local, mesh=mesh, in_specs=in_specs, out_specs=out_specs, check_vma=False)
```

```python
import functools

import jax
import jax.numpy as jnp
from jax import lax
from jax.experimental import pallas as pl
from jax.experimental.pallas import tpu as pltpu
from jax.sharding import PartitionSpec as P

F32 = jnp.float32
BF16 = jnp.bfloat16
LOG2_E = 1.4426950408889634
DEAD = 64.0
VMEM = pl.BlockSpec(memory_space=pltpu.VMEM)
SPACES = {
    "v": VMEM,
    "s": pl.BlockSpec(memory_space=pltpu.SMEM),
    "f": pl.BlockSpec(memory_space=pl.ANY),
}


def dot(a, b, dims=((1,), (0,))):
    return lax.dot_general(a, b, (dims, ((), ())), preferred_element_type=F32)


def call(kernel, outs, ins, scratch=(), vmem_mib=20):
    fetched = [i for i, (space, _) in enumerate(ins) if space == "f"]

    def body(*refs):
        refs = list(refs)
        local_count = len(fetched) + 1
        own, (held, sems) = refs[:-local_count], (refs[-local_count:-1], refs[-1])
        copies = []
        for n, i in enumerate(fetched):
            copies.append(pltpu.make_async_copy(own[i], held[n], sems.at[n]))
            copies[-1].start()
            own[i] = held[n]

        def ready():
            for copy in copies:
                copy.wait()

        kernel(ready, *own)

    return pl.pallas_call(
        body,
        out_shape=outs,
        in_specs=[SPACES[space] for space, _ in ins],
        out_specs=jax.tree.map(lambda _: VMEM, outs),
        scratch_shapes=list(scratch)
        + [pltpu.VMEM(ins[i][1].shape, ins[i][1].dtype) for i in fetched]
        + [pltpu.SemaphoreType.DMA((max(1, len(fetched)),))],
        compiler_params=pltpu.CompilerParams(vmem_limit_bytes=vmem_mib * 1024 * 1024),
    )(*[array for _, array in ins])


def halo_kernel(ready, count_ref, rows_ref, feats_ref, out_ref):
    doms, block = rows_ref.shape
    at = lax.broadcasted_iota(jnp.int32, (1, block), 1)
    ready()
    pieces = [
        jnp.where(at < count_ref[:, s : s + 1], rows_ref[s : s + 1, :], -1) for s in range(doms)
    ]
    flat = jnp.concatenate(pieces, axis=1)
    total = doms * block
    nodes = feats_ref.shape[0]
    pick = (lax.broadcasted_iota(jnp.int32, (nodes, total), 0) == flat).astype(F32).astype(BF16)
    rows = dot(pick, feats_ref[...], ((0,), (0,)))
    first = lax.broadcasted_iota(jnp.int32, (16, total), 0) == 0
    dead = jnp.where(first & (flat < 0), 1.0, 0.0).astype(BF16)
    mark_at = (lax.broadcasted_iota(jnp.int32, (16, 128), 0) == 0) & (
        lax.broadcasted_iota(jnp.int32, (16, 128), 1) == 0
    )
    mark = jnp.where(mark_at, DEAD, 0.0).astype(BF16)
    out_ref[:, :128] = (rows[:, :128] + dot(dead, mark, ((0,), (0,)))).astype(BF16)
    out_ref[:, 128:] = rows[:, 128:].astype(BF16)


def block_diagonal(vectors):
    heads, size = vectors.shape
    wide = jnp.concatenate([vectors] * heads, axis=1)
    lane_head = lax.broadcasted_iota(jnp.int32, wide.shape, 1) // size
    wide = jnp.where(lane_head == lax.broadcasted_iota(jnp.int32, wide.shape, 0), wide, 0.0)
    high = wide.astype(BF16).astype(F32)
    middle = (wide - high).astype(BF16).astype(F32)
    low = (wide - high - middle).astype(BF16).astype(F32)
    return jnp.concatenate([high, middle, low, jnp.zeros_like(wide)], axis=0).astype(BF16)


def prepare_kernel(
    ready,
    live_ref,
    neigh_ref,
    degree_ref,
    src_ref,
    dst_ref,
    ends_ref,
    cand_ref,
    labels_ref,
    out_w_ref,
    gat_ref,
    mlp_ref,
    count_ref,
    factor_ref,
    diag_src_ref,
    diag_dst_ref,
    pick_ref,
    gather_ref,
    scatter_ref,
    known_ref,
    weight_ref,
    gat_own_ref,
    mlp_own_ref,
):
    ready()
    nodes, table = count_ref.shape
    slots = neigh_ref.shape[0]
    ids = neigh_ref[...]
    ids = jnp.where(lax.broadcasted_iota(jnp.int32, ids.shape, 0) < degree_ref[...], ids, -1)
    for base in range(0, table, nodes):
        at = base + lax.broadcasted_iota(jnp.int32, (nodes, nodes), 0)
        total = jnp.zeros((nodes, nodes), F32)
        if base == 0:
            total = (at == lax.broadcasted_iota(jnp.int32, (nodes, nodes), 1)).astype(F32)
        for j in range(slots):
            total = total + (at == ids[j : j + 1, :]).astype(F32)
        total = total.T
        power = jnp.where(total > 1, 2.0, total)
        power = jnp.where(total > 2, 4.0, power)
        power = jnp.where(total > 5, 8.0, power)
        power = jnp.where(total > 13, 16.0, power)
        count_ref[:, base : base + nodes] = total
        factor_ref[0, :, base : base + nodes] = power.astype(BF16)
        factor_ref[1, :, base : base + nodes] = (total - power).astype(BF16)
    diag_src_ref[...] = block_diagonal(src_ref[...])
    diag_dst_ref[...] = block_diagonal(dst_ref[...])
    ends = ends_ref.shape[1]
    node_at = lax.broadcasted_iota(jnp.int32, (nodes, ends), 0)
    pick_ref[...] = (node_at == ends_ref[...]).astype(F32).astype(BF16)
    cands = cand_ref.shape[1]
    slot_at = lax.broadcasted_iota(jnp.int32, (ends, cands), 0)
    for i in range(2):
        one_hot = (slot_at == cand_ref[i : i + 1, :]).astype(F32)
        scatter_ref[i] = one_hot.astype(BF16)
        gather_ref[i] = one_hot.T.astype(BF16)
    live = (lax.broadcasted_iota(jnp.int32, (1, cands), 1) < live_ref[0, 0]).astype(F32)
    known = jnp.concatenate([live, labels_ref[...].astype(F32), jnp.zeros((126, cands), F32)], axis=0)
    known_ref[...] = known.T
    weight_ref[...] = out_w_ref[...]
    gat_own_ref[...] = gat_ref[...]
    mlp_own_ref[...] = mlp_ref[...]


def shard_row(i, shards):
    depth = shards[0].shape[0]
    return pl.multiple_of((lax.axis_index("edge") ^ i) * depth, depth)


def shard_dots(rows_ref, shards, whole_ref=None):
    depth = shards[0].shape[0]
    if depth % 128:
        for i, shard in enumerate(shards):
            whole_ref[pl.ds(shard_row(i, shards), depth), :] = shard[...]
        return dot(rows_ref[...], whole_ref[...])
    total = None
    for i, shard in enumerate(shards):
        cols = pl.ds(shard_row(i, shards), depth)
        part = dot(rows_ref[:, cols], shard[...])
        total = part if total is None else total + part
    return total


def attend_kernel(
    shard_count,
    ready,
    own_ref,
    got_ref,
    count_ref,
    factor_ref,
    diag_src_ref,
    diag_dst_ref,
    pick_ref,
    *rest,
):
    shards = rest[:shard_count]
    out_ref, send_ref, proj_ref, stage_ref, rows_ref, bias_ref, mix_ref, whole_ref = rest[-8:]
    ready()
    nodes, width = own_ref.shape
    table = proj_ref.shape[0]
    heads = diag_src_ref.shape[0] // 4
    size = width // heads
    rows_ref[:nodes, :] = own_ref[...]
    rows_ref[nodes:, :] = got_ref[...]
    proj_ref[...] = shard_dots(rows_ref, shards, whole_ref).astype(BF16)
    parts = dot(diag_src_ref[...], proj_ref[...], ((1,), (1,)))
    src = parts[:heads] + parts[heads : 2 * heads] + parts[2 * heads : 3 * heads]
    src = src.astype(BF16).astype(F32) * LOG2_E
    parts = dot(proj_ref[:nodes, :], diag_dst_ref[...], ((1,), (1,)))
    dst = parts[:, :heads] + parts[:, heads : 2 * heads] + parts[:, 2 * heads : 3 * heads]
    dst = dst * LOG2_E
    first_lane = (lax.broadcasted_iota(jnp.int32, (16, 128), 1) == 0).astype(F32).astype(BF16)
    mark = dot(first_lane, rows_ref[nodes:, :128], ((1,), (1,)))[:1]
    hide = jnp.where(mark < DEAD / 2, 0.0, -jnp.inf)
    hide = jnp.concatenate([jnp.zeros((1, nodes), F32), hide], axis=1)
    bias_ref[...] = jnp.where(count_ref[...] > 0, hide, -jnp.inf)
    chunk = 32
    for h in range(heads):
        for r in range(0, nodes, chunk):
            here = slice(r, r + chunk)
            logit = dst[here, h : h + 1] + src[h : h + 1, :]
            logit = jnp.maximum(logit, 0.2 * logit) + bias_ref[here, :]
            terms = jnp.exp2(logit - jnp.max(logit, axis=1, keepdims=True))
            running = jnp.sum(count_ref[here, :] * terms, axis=1, keepdims=True)
            weight = (terms * (1.0 / running)).astype(BF16)
            mix_ref[h % 2, here, :] = weight * factor_ref[0, here, :]
            mix_ref[h % 2, nodes + r : nodes + r + chunk, :] = weight * factor_ref[1, here, :]
        both = dot(mix_ref[h % 2], proj_ref[:, h * size : (h + 1) * size])
        total = both[:nodes] + both[nodes:]
        total = jnp.where(total > 0, total, jnp.exp(jnp.minimum(total, 0.0)) - 1.0)
        out_ref[:, h * size : (h + 1) * size] = total.astype(BF16)
    pack_rows(dot(pick_ref[...], out_ref[...], ((0,), (0,))), stage_ref, send_ref)


def pack_rows(rows, stage_ref, out_ref):
    slots, width = rows.shape
    pieces = width // 128
    for c in range(pieces):
        stage_ref[pl.ds(c, slots, stride=pieces), :] = rows[:, c * 128 : (c + 1) * 128]
    out_ref[...] = stage_ref[...].astype(BF16)


def unpack_rows(ref, stage_ref, pieces):
    stage_ref[...] = ref[...].astype(F32)
    slots = ref.shape[0] // pieces
    parts = [stage_ref[pl.ds(c, slots, stride=pieces), :] for c in range(pieces)]
    return jnp.concatenate(parts, axis=1).astype(BF16)


def score_kernel(
    shard_count, ready, got_ref, gather_ref, scatter_ref, known_ref, out_w_ref, *rest
):
    shards = rest[:shard_count]
    scores_ref, back_ref, pair_ref, stage_ref, sum_ref, grad_ref = rest[shard_count:]
    ready()
    cands = known_ref.shape[0]
    depth = shards[0].shape[0]
    slots, width = grad_ref.shape[1:]
    rows = unpack_rows(got_ref, stage_ref, width // 128)
    for i in range(2):
        pair_ref[:, i * width : (i + 1) * width] = dot(gather_ref[i], rows).astype(BF16)
    pre_act = shard_dots(pair_ref, shards)
    out_w = out_w_ref[...]
    live = known_ref[:, :1]
    gate = jax.nn.sigmoid(pre_act)
    score = jnp.sum(pre_act * gate * out_w, axis=1, keepdims=True) * live
    scores_ref[...] = jnp.broadcast_to(score, (cands, 128)).T[:1]
    grad_score = (jax.nn.sigmoid(score) - known_ref[:, 1:2]) * live
    grad_pre = (grad_score * out_w * (gate * (1.0 + pre_act * (1.0 - gate)))).astype(BF16)
    for i in range(2):
        total = dot(scatter_ref[i], grad_pre)
        high = total.astype(BF16)
        sum_ref[i, :slots, :] = high
        sum_ref[i, slots:, :] = (total - high.astype(F32)).astype(BF16)
    for i, shard in enumerate(shards):
        row = shard_row(i, shards)
        half = row // width
        col = pl.multiple_of(row % width, depth)
        both = dot(sum_ref[half], shard[...], ((1,), (1,)))
        grad_ref[half, :, pl.ds(col, depth)] = both[:slots] + both[slots:]
    pack_rows(grad_ref[0] + grad_ref[1], stage_ref, back_ref)


def scatter_kernel(ready, pick_ref, got_ref, out_ref, stage_ref):
    ready()
    rows = unpack_rows(got_ref, stage_ref, out_ref.shape[1] // 128)
    out_ref[...] = dot(pick_ref[...], rows)


def swap(array, axis, k):
    count = lax.axis_size(axis)
    return lax.ppermute(array, axis, [(i, i ^ k) for i in range(count)])


def across(shard, edge_count):
    return [shard] + [swap(shard, "edge", 2 * k) for k in range(1, edge_count // 2)]


def from_core(shards):
    return [one for shard in shards for one in (shard, swap(shard, "edge", 1))]


def local(
    node_feats,
    gat_weight,
    attn_src,
    attn_dst,
    neighbours,
    degree,
    halo_rows,
    halo_count,
    endpoint_rows,
    cand_ends,
    cand_count,
    labels,
    mlp_weight,
    out_weight,
):
    nodes, width = node_feats.shape
    dom_count = lax.axis_size("dom")
    edge_count = lax.axis_size("edge")
    block = halo_rows.shape[-1]
    cands = labels.shape[-1]
    hidden = out_weight.shape[0]
    halo = dom_count * block
    table = nodes + halo
    slots = dom_count * edge_count * endpoint_rows.shape[-1]
    pieces = width // 128
    everyone = ("dom", "edge")
    shape = jax.ShapeDtypeStruct

    heads = attn_src.shape[0]
    gat_across = across(gat_weight, edge_count)
    send_rows = call(
        halo_kernel,
        shape((halo, width), BF16),
        [("f", halo_count[0]), ("f", halo_rows[0, 0]), ("f", node_feats)],
        vmem_mib=60,
    )
    gat_across = lax.optimization_barrier((*gat_across, send_rows))[: len(gat_across)]
    got_rows = lax.all_to_all(send_rows, "dom", split_axis=0, concat_axis=0, tiled=True)
    mlp_across = across(lax.optimization_barrier((mlp_weight, send_rows))[0], edge_count)
    gat_shards = from_core(gat_across)
    prepared = call(
        prepare_kernel,
        (
            shape((nodes, table), F32),
            shape((2, nodes, table), BF16),
            shape((4 * heads, width), BF16),
            shape((4 * heads, width), BF16),
            shape((nodes, slots), BF16),
            shape((2, cands, slots), BF16),
            shape((2, slots, cands), BF16),
            shape((cands, 128), F32),
            shape((1, hidden), F32),
            shape(gat_weight.shape, BF16),
            shape(mlp_weight.shape, BF16),
        ),
        [
            ("s", cand_count),
            ("f", neighbours.T),
            ("f", degree.reshape(1, nodes)),
            ("f", attn_src),
            ("f", attn_dst),
            ("f", endpoint_rows.reshape(1, slots)),
            ("f", cand_ends[0, 0]),
            ("f", labels[0]),
            ("f", out_weight.reshape(1, hidden)),
            ("f", gat_weight),
            ("f", mlp_weight),
        ],
    )
    counts, factors, diag_src, diag_dst, pick, gather, scatter, known, out_row, *own = prepared
    gat_shards[0] = own[0]
    packed = pltpu.VMEM((slots * pieces, 128), F32)
    node_out, send_ends = call(
        functools.partial(attend_kernel, edge_count),
        (shape((nodes, width), BF16), shape((slots * pieces, 128), BF16)),
        [
            ("v", node_feats),
            ("v", got_rows),
            ("v", counts),
            ("v", factors),
            ("v", diag_src),
            ("v", diag_dst),
            ("v", pick),
        ]
        + [("v", w) for w in gat_shards],
        [
            pltpu.VMEM((table, width), BF16),
            packed,
            pltpu.VMEM((table, width), BF16),
            pltpu.VMEM((nodes, table), F32),
            pltpu.VMEM((2, 2 * nodes, table), BF16),
            pltpu.VMEM((width if width // edge_count % 128 else 16, width), BF16),
        ],
    )
    mlp_across = lax.optimization_barrier((send_ends, *mlp_across))[1:]
    mlp_shards = from_core(mlp_across)
    mlp_shards[0] = own[1]
    got_ends = lax.all_to_all(send_ends, everyone, split_axis=0, concat_axis=0, tiled=True)
    scores, send_back = call(
        functools.partial(score_kernel, edge_count),
        (shape((1, cands), F32), shape((slots * pieces, 128), BF16)),
        [
            ("v", got_ends),
            ("v", gather),
            ("v", scatter),
            ("v", known),
            ("v", out_row),
        ]
        + [("v", w) for w in mlp_shards],
        [
            pltpu.VMEM((cands, 2 * width), BF16),
            packed,
            pltpu.VMEM((2, 2 * slots, hidden), BF16),
            pltpu.VMEM((2, slots, width), F32),
        ],
    )
    got_back = lax.all_to_all(send_back, everyone, split_axis=0, concat_axis=0, tiled=True)
    node_grad = call(
        scatter_kernel, shape((nodes, width), F32), [("v", pick), ("v", got_back)], [packed]
    )
    return (node_out, scores.reshape(1, 1, cands), node_grad)


def solution(mesh):
    in_specs = (
        P(("dom", "edge"), None),
        P("edge", None),
        P(),
        P(),
        P(("dom", "edge"), None),
        P(("dom", "edge")),
        P("dom", "edge", None, None),
        P("dom", "edge", None),
        P("dom", "edge", None, None, None),
        P("dom", "edge", None, None),
        P("dom", "edge"),
        P("dom", "edge", None),
        P("edge", None),
        P(),
    )
    out_specs = (P(("dom", "edge"), None), P("dom", "edge", None), P(("dom", "edge"), None))
    return jax.shard_map(local, mesh=mesh, in_specs=in_specs, out_specs=out_specs, check_vma=False)
```

```python
import functools

import jax
import jax.numpy as jnp
from jax import lax
from jax.experimental import pallas as pl
from jax.experimental.pallas import tpu as pltpu
from jax.sharding import PartitionSpec as P

F32 = jnp.float32
BF16 = jnp.bfloat16
LOG2_E = 1.4426950408889634
DEAD = 64.0
VMEM = pl.BlockSpec(memory_space=pltpu.VMEM)
SPACES = {
    "v": VMEM,
    "s": pl.BlockSpec(memory_space=pltpu.SMEM),
    "f": pl.BlockSpec(memory_space=pl.ANY),
}


def dot(a, b, dims=((1,), (0,))):
    return lax.dot_general(a, b, (dims, ((), ())), preferred_element_type=F32)


def call(kernel, outs, ins, scratch=(), vmem_mib=20):
    fetched = [i for i, (space, _) in enumerate(ins) if space == "f"]

    def body(*refs):
        refs = list(refs)
        local_count = len(fetched) + 1
        own, (held, sems) = refs[:-local_count], (refs[-local_count:-1], refs[-1])
        copies = []
        for n, i in enumerate(fetched):
            copies.append(pltpu.make_async_copy(own[i], held[n], sems.at[n]))
            copies[-1].start()
            own[i] = held[n]

        def ready():
            for copy in copies:
                copy.wait()

        kernel(ready, *own)

    return pl.pallas_call(
        body,
        out_shape=outs,
        in_specs=[SPACES[space] for space, _ in ins],
        out_specs=jax.tree.map(lambda _: VMEM, outs),
        scratch_shapes=list(scratch)
        + [pltpu.VMEM(ins[i][1].shape, ins[i][1].dtype) for i in fetched]
        + [pltpu.SemaphoreType.DMA((max(1, len(fetched)),))],
        compiler_params=pltpu.CompilerParams(vmem_limit_bytes=vmem_mib * 1024 * 1024),
    )(*[array for _, array in ins])


def halo_kernel(ready, count_ref, rows_ref, feats_ref, out_ref):
    doms, block = rows_ref.shape
    at = lax.broadcasted_iota(jnp.int32, (1, block), 1)
    ready()
    pieces = [
        jnp.where(at < count_ref[:, s : s + 1], rows_ref[s : s + 1, :], -1) for s in range(doms)
    ]
    flat = jnp.concatenate(pieces, axis=1)
    total = doms * block
    nodes = feats_ref.shape[0]
    pick = (lax.broadcasted_iota(jnp.int32, (nodes, total), 0) == flat).astype(F32).astype(BF16)
    rows = dot(pick, feats_ref[...], ((0,), (0,)))
    first = lax.broadcasted_iota(jnp.int32, (16, total), 0) == 0
    dead = jnp.where(first & (flat < 0), 1.0, 0.0).astype(BF16)
    mark_at = (lax.broadcasted_iota(jnp.int32, (16, 128), 0) == 0) & (
        lax.broadcasted_iota(jnp.int32, (16, 128), 1) == 0
    )
    mark = jnp.where(mark_at, DEAD, 0.0).astype(BF16)
    out_ref[:, :128] = (rows[:, :128] + dot(dead, mark, ((0,), (0,)))).astype(BF16)
    out_ref[:, 128:] = rows[:, 128:].astype(BF16)


def block_diagonal(vectors):
    heads, size = vectors.shape
    wide = jnp.concatenate([vectors] * heads, axis=1)
    lane_head = lax.broadcasted_iota(jnp.int32, wide.shape, 1) // size
    wide = jnp.where(lane_head == lax.broadcasted_iota(jnp.int32, wide.shape, 0), wide, 0.0)
    high = wide.astype(BF16).astype(F32)
    middle = (wide - high).astype(BF16).astype(F32)
    low = (wide - high - middle).astype(BF16).astype(F32)
    return jnp.concatenate([high, middle, low, jnp.zeros_like(wide)], axis=0).astype(BF16)


def prepare_kernel(
    ready,
    live_ref,
    neigh_ref,
    degree_ref,
    src_ref,
    dst_ref,
    ends_ref,
    cand_ref,
    labels_ref,
    out_w_ref,
    count_ref,
    power_ref,
    diag_src_ref,
    diag_dst_ref,
    pick_ref,
    scatter_ref,
    known_ref,
    weight_ref,
):
    ready()
    nodes, table = count_ref.shape
    slots = neigh_ref.shape[0]
    ids = neigh_ref[...]
    ids = jnp.where(lax.broadcasted_iota(jnp.int32, ids.shape, 0) < degree_ref[...], ids, -1)
    for base in range(0, table, nodes):
        at = base + lax.broadcasted_iota(jnp.int32, (nodes, nodes), 0)
        total = jnp.zeros((nodes, nodes), F32)
        if base == 0:
            total = (at == lax.broadcasted_iota(jnp.int32, (nodes, nodes), 1)).astype(F32)
        for j in range(slots):
            total = total + (at == ids[j : j + 1, :]).astype(F32)
        total = total.T
        power = jnp.where(total > 1, 2.0, total)
        power = jnp.where(total > 2, 4.0, power)
        power = jnp.where(total > 5, 8.0, power)
        power = jnp.where(total > 13, 16.0, power)
        count_ref[:, base : base + nodes] = total.astype(BF16)
        power_ref[:, base : base + nodes] = power.astype(BF16)
    diag_src_ref[...] = block_diagonal(src_ref[...])
    diag_dst_ref[...] = block_diagonal(dst_ref[...])
    ends = ends_ref.shape[1]
    node_at = lax.broadcasted_iota(jnp.int32, (nodes, ends), 0)
    pick_ref[...] = (node_at == ends_ref[...]).astype(F32).astype(BF16)
    cands = cand_ref.shape[1]
    slot_at = lax.broadcasted_iota(jnp.int32, (ends, cands), 0)
    for i in range(2):
        scatter_ref[i] = (slot_at == cand_ref[i : i + 1, :]).astype(F32).astype(BF16)
    live = (lax.broadcasted_iota(jnp.int32, (1, cands), 1) < live_ref[0, 0]).astype(F32)
    known = jnp.concatenate([live, labels_ref[...].astype(F32), jnp.zeros((126, cands), F32)], axis=0)
    known_ref[...] = known.T.astype(BF16)
    weight_ref[...] = out_w_ref[...]


def shard_row(i, shards):
    depth = shards[0].shape[0]
    return pl.multiple_of((lax.axis_index("edge") ^ i) * depth, depth)


def shard_dots(rows_ref, shards, whole_ref=None):
    depth = shards[0].shape[0]
    if depth % 128:
        for i, shard in enumerate(shards):
            whole_ref[pl.ds(shard_row(i, shards), depth), :] = shard[...]
        return dot(rows_ref[...], whole_ref[...])
    total = None
    for i, shard in enumerate(shards):
        cols = pl.ds(shard_row(i, shards), depth)
        part = dot(rows_ref[:, cols], shard[...])
        total = part if total is None else total + part
    return total


def attend_kernel(
    shard_count,
    ready,
    own_ref,
    got_ref,
    count_ref,
    power_ref,
    diag_src_ref,
    diag_dst_ref,
    pick_ref,
    *rest,
):
    shards = rest[:shard_count]
    out_ref, send_ref, proj_ref, stage_ref, rows_ref, bias_ref, mix_ref, whole_ref = rest[-8:]
    ready()
    nodes, width = own_ref.shape
    table = proj_ref.shape[0]
    heads = diag_src_ref.shape[0] // 4
    size = width // heads
    rows_ref[:nodes, :] = own_ref[...]
    rows_ref[nodes:, :] = got_ref[...]
    proj_ref[...] = shard_dots(rows_ref, shards, whole_ref).astype(BF16)
    parts = dot(diag_src_ref[...], proj_ref[...], ((1,), (1,)))
    src = parts[:heads] + parts[heads : 2 * heads] + parts[2 * heads : 3 * heads]
    src = src.astype(BF16).astype(F32) * LOG2_E
    parts = dot(proj_ref[:nodes, :], diag_dst_ref[...], ((1,), (1,)))
    dst = parts[:, :heads] + parts[:, heads : 2 * heads] + parts[:, 2 * heads : 3 * heads]
    dst = dst * LOG2_E
    first_lane = (lax.broadcasted_iota(jnp.int32, (16, 128), 1) == 0).astype(F32).astype(BF16)
    mark = dot(first_lane, rows_ref[nodes:, :128], ((1,), (1,)))[:1]
    hide = jnp.where(mark < DEAD / 2, 0.0, -jnp.inf)
    hide = jnp.concatenate([jnp.zeros((1, nodes), F32), hide], axis=1)
    bias_ref[...] = jnp.where(count_ref[...] > 0, hide, -jnp.inf)
    chunk = 32
    for h in range(heads):
        for r in range(0, nodes, chunk):
            here = slice(r, r + chunk)
            logit = dst[here, h : h + 1] + src[h : h + 1, :]
            logit = jnp.maximum(logit, 0.2 * logit) + bias_ref[here, :]
            terms = jnp.exp2(logit - jnp.max(logit, axis=1, keepdims=True))
            count = count_ref[here, :]
            power = power_ref[here, :]
            running = jnp.sum(count.astype(F32) * terms, axis=1, keepdims=True)
            weight = (terms * (1.0 / running)).astype(BF16)
            mix_ref[h % 2, here, :] = weight * power
            mix_ref[h % 2, nodes + r : nodes + r + chunk, :] = weight * (count - power)
        both = dot(mix_ref[h % 2], proj_ref[:, h * size : (h + 1) * size])
        total = both[:nodes] + both[nodes:]
        total = jnp.where(total > 0, total, jnp.exp(jnp.minimum(total, 0.0)) - 1.0)
        out_ref[:, h * size : (h + 1) * size] = total.astype(BF16)
    pack_rows(dot(pick_ref[...], out_ref[...], ((0,), (0,))), stage_ref, send_ref)


def pack_rows(rows, stage_ref, out_ref):
    slots, width = rows.shape
    pieces = width // 128
    for c in range(pieces):
        stage_ref[pl.ds(c, slots, stride=pieces), :] = rows[:, c * 128 : (c + 1) * 128]
    out_ref[...] = stage_ref[...].astype(BF16)


def unpack_rows(ref, stage_ref, pieces):
    stage_ref[...] = ref[...].astype(F32)
    slots = ref.shape[0] // pieces
    parts = [stage_ref[pl.ds(c, slots, stride=pieces), :] for c in range(pieces)]
    return jnp.concatenate(parts, axis=1).astype(BF16)


def score_kernel(
    shard_count, ready, got_ref, scatter_ref, known_ref, out_w_ref, *rest
):
    shards = rest[:shard_count]
    scores_ref, back_ref, pair_ref, stage_ref, sum_ref, grad_ref = rest[shard_count:]
    ready()
    cands = known_ref.shape[0]
    depth = shards[0].shape[0]
    slots, width = grad_ref.shape[1:]
    rows = unpack_rows(got_ref, stage_ref, width // 128)
    for i in range(2):
        pair_ref[:, i * width : (i + 1) * width] = dot(
            scatter_ref[i], rows, ((0,), (0,))
        ).astype(BF16)
    pre_act = shard_dots(pair_ref, shards)
    out_w = out_w_ref[...]
    live = known_ref[:, :1].astype(F32)
    gate = jax.nn.sigmoid(pre_act)
    score = jnp.sum(pre_act * gate * out_w, axis=1, keepdims=True) * live
    scores_ref[...] = jnp.broadcast_to(score, (cands, 128)).T[:1]
    grad_score = (jax.nn.sigmoid(score) - known_ref[:, 1:2].astype(F32)) * live
    grad_pre = (grad_score * out_w * (gate * (1.0 + pre_act * (1.0 - gate)))).astype(BF16)
    for i in range(2):
        total = dot(scatter_ref[i], grad_pre)
        high = total.astype(BF16)
        sum_ref[i, :slots, :] = high
        sum_ref[i, slots:, :] = (total - high.astype(F32)).astype(BF16)
    for i, shard in enumerate(shards):
        row = shard_row(i, shards)
        half = row // width
        col = pl.multiple_of(row % width, depth)
        both = dot(sum_ref[half], shard[...], ((1,), (1,)))
        grad_ref[half, :, pl.ds(col, depth)] = both[:slots] + both[slots:]
    pack_rows(grad_ref[0] + grad_ref[1], stage_ref, back_ref)


def scatter_kernel(ready, pick_ref, got_ref, out_ref, stage_ref):
    ready()
    rows = unpack_rows(got_ref, stage_ref, out_ref.shape[1] // 128)
    out_ref[...] = dot(pick_ref[...], rows)


def swap(array, axis, k):
    count = lax.axis_size(axis)
    return lax.ppermute(array, axis, [(i, i ^ k) for i in range(count)])


def across(shard, edge_count):
    return [shard] + [swap(shard, "edge", 2 * k) for k in range(1, edge_count // 2)]


def from_core(shards):
    return [one for shard in shards for one in (shard, swap(shard, "edge", 1))]


def local(
    node_feats,
    gat_weight,
    attn_src,
    attn_dst,
    neighbours,
    degree,
    halo_rows,
    halo_count,
    endpoint_rows,
    cand_ends,
    cand_count,
    labels,
    mlp_weight,
    out_weight,
):
    nodes, width = node_feats.shape
    dom_count = lax.axis_size("dom")
    edge_count = lax.axis_size("edge")
    block = halo_rows.shape[-1]
    cands = labels.shape[-1]
    hidden = out_weight.shape[0]
    halo = dom_count * block
    table = nodes + halo
    slots = dom_count * edge_count * endpoint_rows.shape[-1]
    pieces = width // 128
    everyone = ("dom", "edge")
    shape = jax.ShapeDtypeStruct

    heads = attn_src.shape[0]
    gat_across = across(gat_weight, edge_count)
    send_rows = call(
        halo_kernel,
        shape((halo, width), BF16),
        [("f", halo_count[0]), ("f", halo_rows[0, 0]), ("f", node_feats)],
        vmem_mib=60,
    )
    gat_across = lax.optimization_barrier((*gat_across, send_rows))[: len(gat_across)]
    got_rows = lax.all_to_all(send_rows, "dom", split_axis=0, concat_axis=0, tiled=True)
    mlp_across = across(lax.optimization_barrier((mlp_weight, send_rows))[0], edge_count)
    gat_shards = from_core(gat_across)
    prepared = call(
        prepare_kernel,
        (
            shape((nodes, table), BF16),
            shape((nodes, table), BF16),
            shape((4 * heads, width), BF16),
            shape((4 * heads, width), BF16),
            shape((nodes, slots), BF16),
            shape((2, slots, cands), BF16),
            shape((cands, 128), BF16),
            shape((1, hidden), F32),
        ),
        [
            ("s", cand_count),
            ("f", neighbours.T),
            ("f", degree.reshape(1, nodes)),
            ("f", attn_src),
            ("f", attn_dst),
            ("f", endpoint_rows.reshape(1, slots)),
            ("f", cand_ends[0, 0]),
            ("f", labels[0]),
            ("f", out_weight.reshape(1, hidden)),
        ],
    )
    counts, powers, diag_src, diag_dst, pick, scatter, known, out_row = prepared
    packed = pltpu.VMEM((slots * pieces, 128), F32)
    node_out, send_ends = call(
        functools.partial(attend_kernel, edge_count),
        (shape((nodes, width), BF16), shape((slots * pieces, 128), BF16)),
        [
            ("v", node_feats),
            ("v", got_rows),
            ("v", counts),
            ("v", powers),
            ("v", diag_src),
            ("v", diag_dst),
            ("v", pick),
        ]
        + [("v", w) for w in gat_shards],
        [
            pltpu.VMEM((table, width), BF16),
            packed,
            pltpu.VMEM((table, width), BF16),
            pltpu.VMEM((nodes, table), F32),
            pltpu.VMEM((2, 2 * nodes, table), BF16),
            pltpu.VMEM((width if width // edge_count % 128 else 16, width), BF16),
        ],
    )
    mlp_across = lax.optimization_barrier((send_ends, *mlp_across))[1:]
    mlp_shards = from_core(mlp_across)
    got_ends = lax.all_to_all(send_ends, everyone, split_axis=0, concat_axis=0, tiled=True)
    scores, send_back = call(
        functools.partial(score_kernel, edge_count),
        (shape((1, cands), F32), shape((slots * pieces, 128), BF16)),
        [
            ("v", got_ends),
            ("v", scatter),
            ("v", known),
            ("v", out_row),
        ]
        + [("v", w) for w in mlp_shards],
        [
            pltpu.VMEM((cands, 2 * width), BF16),
            packed,
            pltpu.VMEM((2, 2 * slots, hidden), BF16),
            pltpu.VMEM((2, slots, width), F32),
        ],
    )
    got_back = lax.all_to_all(send_back, everyone, split_axis=0, concat_axis=0, tiled=True)
    node_grad = call(
        scatter_kernel, shape((nodes, width), F32), [("v", pick), ("v", got_back)], [packed]
    )
    return (node_out, scores.reshape(1, 1, cands), node_grad)


def solution(mesh):
    in_specs = (
        P(("dom", "edge"), None),
        P("edge", None),
        P(),
        P(),
        P(("dom", "edge"), None),
        P(("dom", "edge")),
        P("dom", "edge", None, None),
        P("dom", "edge", None),
        P("dom", "edge", None, None, None),
        P("dom", "edge", None, None),
        P("dom", "edge"),
        P("dom", "edge", None),
        P("edge", None),
        P(),
    )
    out_specs = (P(("dom", "edge"), None), P("dom", "edge", None), P(("dom", "edge"), None))
    return jax.shard_map(local, mesh=mesh, in_specs=in_specs, out_specs=out_specs, check_vma=False)
```

```python
import functools

import jax
import jax.numpy as jnp
from jax import lax
from jax.experimental import pallas as pl
from jax.experimental.pallas import tpu as pltpu
from jax.sharding import PartitionSpec as P

F32 = jnp.float32
BF16 = jnp.bfloat16
LOG2_E = 1.4426950408889634
DEAD = 64.0
VMEM = pl.BlockSpec(memory_space=pltpu.VMEM)
SPACES = {
    "v": VMEM,
    "s": pl.BlockSpec(memory_space=pltpu.SMEM),
    "f": pl.BlockSpec(memory_space=pl.ANY),
}


def dot(a, b, dims=((1,), (0,))):
    return lax.dot_general(a, b, (dims, ((), ())), preferred_element_type=F32)


def call(kernel, outs, ins, scratch=(), vmem_mib=20):
    fetched = [i for i, (space, _) in enumerate(ins) if space == "f"]

    def body(*refs):
        refs = list(refs)
        local_count = len(fetched) + 1
        own, (held, sems) = refs[:-local_count], (refs[-local_count:-1], refs[-1])
        copies = []
        for n, i in enumerate(fetched):
            copies.append(pltpu.make_async_copy(own[i], held[n], sems.at[n]))
            copies[-1].start()
            own[i] = held[n]

        def ready():
            for copy in copies:
                copy.wait()

        kernel(ready, *own)

    return pl.pallas_call(
        body,
        out_shape=outs,
        in_specs=[SPACES[space] for space, _ in ins],
        out_specs=jax.tree.map(lambda _: VMEM, outs),
        scratch_shapes=list(scratch)
        + [pltpu.VMEM(ins[i][1].shape, ins[i][1].dtype) for i in fetched]
        + [pltpu.SemaphoreType.DMA((max(1, len(fetched)),))],
        compiler_params=pltpu.CompilerParams(vmem_limit_bytes=vmem_mib * 1024 * 1024),
    )(*[array for _, array in ins])


def halo_kernel(ready, count_ref, rows_ref, feats_ref, out_ref):
    doms, block = rows_ref.shape
    at = lax.broadcasted_iota(jnp.int32, (1, block), 1)
    ready()
    pieces = [
        jnp.where(at < count_ref[:, s : s + 1], rows_ref[s : s + 1, :], -1) for s in range(doms)
    ]
    flat = jnp.concatenate(pieces, axis=1)
    total = doms * block
    nodes = feats_ref.shape[0]
    pick = (lax.broadcasted_iota(jnp.int32, (nodes, total), 0) == flat).astype(F32).astype(BF16)
    rows = dot(pick, feats_ref[...], ((0,), (0,)))
    first = lax.broadcasted_iota(jnp.int32, (16, total), 0) == 0
    dead = jnp.where(first & (flat < 0), 1.0, 0.0).astype(BF16)
    mark_at = (lax.broadcasted_iota(jnp.int32, (16, 128), 0) == 0) & (
        lax.broadcasted_iota(jnp.int32, (16, 128), 1) == 0
    )
    mark = jnp.where(mark_at, DEAD, 0.0).astype(BF16)
    out_ref[:, :128] = (rows[:, :128] + dot(dead, mark, ((0,), (0,)))).astype(BF16)
    out_ref[:, 128:] = rows[:, 128:].astype(BF16)


def block_diagonal(vectors):
    heads, size = vectors.shape
    wide = jnp.concatenate([vectors] * heads, axis=1)
    lane_head = lax.broadcasted_iota(jnp.int32, wide.shape, 1) // size
    wide = jnp.where(lane_head == lax.broadcasted_iota(jnp.int32, wide.shape, 0), wide, 0.0)
    high = wide.astype(BF16).astype(F32)
    middle = (wide - high).astype(BF16).astype(F32)
    low = (wide - high - middle).astype(BF16).astype(F32)
    return jnp.concatenate([high, middle, low, jnp.zeros_like(wide)], axis=0).astype(BF16)


def prepare_kernel(
    table,
    ready,
    live_ref,
    neigh_ref,
    degree_ref,
    src_ref,
    dst_ref,
    ends_ref,
    cand_ref,
    labels_ref,
    out_w_ref,
    for_attend_ref,
    for_score_ref,
    pick_ref,
):
    ready()
    nodes, ends = pick_ref.shape
    heads, size = src_ref.shape
    slots = neigh_ref.shape[0]
    ids = neigh_ref[...]
    ids = jnp.where(lax.broadcasted_iota(jnp.int32, ids.shape, 0) < degree_ref[...], ids, -1)
    for base in range(0, table, nodes):
        at = base + lax.broadcasted_iota(jnp.int32, (nodes, nodes), 0)
        total = jnp.zeros((nodes, nodes), F32)
        if base == 0:
            total = (at == lax.broadcasted_iota(jnp.int32, (nodes, nodes), 1)).astype(F32)
        for j in range(slots):
            total = total + (at == ids[j : j + 1, :]).astype(F32)
        total = total.T
        power = jnp.where(total > 1, 2.0, total)
        power = jnp.where(total > 2, 4.0, power)
        power = jnp.where(total > 5, 8.0, power)
        power = jnp.where(total > 13, 16.0, power)
        for_attend_ref[:nodes, base : base + nodes] = total.astype(BF16)
        for_attend_ref[:nodes, table + base : table + base + nodes] = power.astype(BF16)
    node_at = lax.broadcasted_iota(jnp.int32, (nodes, ends), 0)
    pick = (node_at == ends_ref[...]).astype(F32).astype(BF16)
    pick_ref[...] = pick
    for_attend_ref[:nodes, 2 * table : 2 * table + ends] = pick
    for_attend_ref[nodes : nodes + 4 * heads, : heads * size] = block_diagonal(src_ref[...])
    for_attend_ref[nodes + 4 * heads :, : heads * size] = block_diagonal(dst_ref[...])
    cands = cand_ref.shape[1]
    hidden = out_w_ref.shape[1]
    slot_at = lax.broadcasted_iota(jnp.int32, (ends, cands), 0)
    for i in range(2):
        one_hot = (slot_at == cand_ref[i : i + 1, :]).astype(F32).astype(BF16)
        for_score_ref[:ends, i * cands : (i + 1) * cands] = one_hot
    live = (lax.broadcasted_iota(jnp.int32, (1, cands), 1) < live_ref[0, 0]).astype(F32)
    known = jnp.concatenate([live, labels_ref[...].astype(F32), jnp.zeros((14, cands), F32)], axis=0)
    for_score_ref[ends : ends + 16, :cands] = known.astype(BF16)
    high = out_w_ref[...].astype(BF16).astype(F32)
    middle = (out_w_ref[...] - high).astype(BF16).astype(F32)
    low = out_w_ref[...] - high - middle
    whole = jnp.concatenate([high, middle, low, jnp.zeros((13, hidden), F32)], axis=0)
    for_score_ref[ends + 16 :, :hidden] = whole.astype(BF16)


def shard_row(i, shards):
    depth = shards[0].shape[0]
    return pl.multiple_of((lax.axis_index("edge") ^ i) * depth, depth)


def shard_dots(rows_ref, shards, whole_ref=None):
    depth = shards[0].shape[0]
    if depth % 128:
        for i, shard in enumerate(shards):
            whole_ref[pl.ds(shard_row(i, shards), depth), :] = shard[...]
        return dot(rows_ref[...], whole_ref[...])
    total = None
    for i, shard in enumerate(shards):
        cols = pl.ds(shard_row(i, shards), depth)
        part = dot(rows_ref[:, cols], shard[...])
        total = part if total is None else total + part
    return total


def attend_kernel(shard_count, heads, slots, ready, own_ref, got_ref, known_ref, *rest):
    shards = rest[:shard_count]
    out_ref, send_ref, proj_ref, stage_ref, rows_ref, bias_ref, mix_ref, whole_ref = rest[-8:]
    ready()
    nodes, width = own_ref.shape
    table = proj_ref.shape[0]
    size = width // heads
    diag_src_ref = known_ref.at[nodes : nodes + 4 * heads, :width]
    diag_dst_ref = known_ref.at[nodes + 4 * heads :, :width]
    count_ref = known_ref.at[:nodes, :table]
    power_ref = known_ref.at[:nodes, table : 2 * table]
    pick_ref = known_ref.at[:nodes, 2 * table : 2 * table + slots]
    rows_ref[:nodes, :] = own_ref[...]
    rows_ref[nodes:, :] = got_ref[...]
    proj_ref[...] = shard_dots(rows_ref, shards, whole_ref).astype(BF16)
    parts = dot(diag_src_ref[...], proj_ref[...], ((1,), (1,)))
    src = parts[:heads] + parts[heads : 2 * heads] + parts[2 * heads : 3 * heads]
    src = src.astype(BF16).astype(F32) * LOG2_E
    parts = dot(proj_ref[:nodes, :], diag_dst_ref[...], ((1,), (1,)))
    dst = parts[:, :heads] + parts[:, heads : 2 * heads] + parts[:, 2 * heads : 3 * heads]
    dst = dst * LOG2_E
    first_lane = (lax.broadcasted_iota(jnp.int32, (16, 128), 1) == 0).astype(F32).astype(BF16)
    mark = dot(first_lane, rows_ref[nodes:, :128], ((1,), (1,)))[:1]
    hide = jnp.where(mark < DEAD / 2, 0.0, -jnp.inf)
    hide = jnp.concatenate([jnp.zeros((1, nodes), F32), hide], axis=1)
    bias_ref[...] = jnp.where(count_ref[...] > 0, hide, -jnp.inf)
    chunk = 32
    for h in range(heads):
        for r in range(0, nodes, chunk):
            here = slice(r, r + chunk)
            logit = dst[here, h : h + 1] + src[h : h + 1, :]
            logit = jnp.maximum(logit, 0.2 * logit) + bias_ref[here, :]
            terms = jnp.exp2(logit - jnp.max(logit, axis=1, keepdims=True))
            count = count_ref[here, :]
            power = power_ref[here, :]
            running = jnp.sum(count.astype(F32) * terms, axis=1, keepdims=True)
            weight = (terms * (1.0 / running)).astype(BF16)
            mix_ref[h % 2, here, :] = weight * power
            mix_ref[h % 2, nodes + r : nodes + r + chunk, :] = weight * (count - power)
        both = dot(mix_ref[h % 2], proj_ref[:, h * size : (h + 1) * size])
        total = both[:nodes] + both[nodes:]
        total = jnp.where(total > 0, total, jnp.exp(jnp.minimum(total, 0.0)) - 1.0)
        out_ref[:, h * size : (h + 1) * size] = total.astype(BF16)
    pack_rows(dot(pick_ref[...], out_ref[...], ((0,), (0,))), stage_ref, send_ref)


def pack_rows(rows, stage_ref, out_ref):
    slots, width = rows.shape
    pieces = width // 128
    for c in range(pieces):
        stage_ref[pl.ds(c, slots, stride=pieces), :] = rows[:, c * 128 : (c + 1) * 128]
    out_ref[...] = stage_ref[...].astype(BF16)


def unpack_rows(ref, stage_ref, pieces):
    stage_ref[...] = ref[...].astype(F32)
    slots = ref.shape[0] // pieces
    parts = [stage_ref[pl.ds(c, slots, stride=pieces), :] for c in range(pieces)]
    return jnp.concatenate(parts, axis=1).astype(BF16)


def score_kernel(shard_count, cands, ready, got_ref, known_ref, *rest):
    shards = rest[:shard_count]
    scores_ref, back_ref, pair_ref, stage_ref, sum_ref, grad_ref = rest[shard_count:]
    ready()
    depth, hidden = shards[0].shape
    slots, width = grad_ref.shape[1:]
    picks = [known_ref[:slots, i * cands : (i + 1) * cands] for i in range(2)]
    known = known_ref[slots : slots + 16, :cands].astype(F32).T
    live, label = known[:, :1], known[:, 1:2]
    out_w = known_ref[slots + 16 :, :hidden].astype(F32)
    out_w = out_w[:1] + out_w[1:2] + out_w[2:3]
    rows = unpack_rows(got_ref, stage_ref, width // 128)
    for i in range(2):
        pair_ref[:, i * width : (i + 1) * width] = dot(
            picks[i], rows, ((0,), (0,))
        ).astype(BF16)
    pre_act = shard_dots(pair_ref, shards)
    gate = jax.nn.sigmoid(pre_act)
    score = jnp.sum(pre_act * gate * out_w, axis=1, keepdims=True) * live
    scores_ref[...] = jnp.broadcast_to(score, (cands, 128)).T[:1]
    grad_score = (jax.nn.sigmoid(score) - label) * live
    grad_pre = (grad_score * out_w * (gate * (1.0 + pre_act * (1.0 - gate)))).astype(BF16)
    for i in range(2):
        total = dot(picks[i], grad_pre)
        high = total.astype(BF16)
        sum_ref[i, :slots, :] = high
        sum_ref[i, slots:, :] = (total - high.astype(F32)).astype(BF16)
    for i, shard in enumerate(shards):
        row = shard_row(i, shards)
        half = row // width
        col = pl.multiple_of(row % width, depth)
        both = dot(sum_ref[half], shard[...], ((1,), (1,)))
        grad_ref[half, :, pl.ds(col, depth)] = both[:slots] + both[slots:]
    pack_rows(grad_ref[0] + grad_ref[1], stage_ref, back_ref)


def scatter_kernel(ready, pick_ref, got_ref, out_ref, stage_ref):
    ready()
    rows = unpack_rows(got_ref, stage_ref, out_ref.shape[1] // 128)
    out_ref[...] = dot(pick_ref[...], rows)


def swap(array, axis, k):
    count = lax.axis_size(axis)
    return lax.ppermute(array, axis, [(i, i ^ k) for i in range(count)])


def across(shard, edge_count):
    return [shard] + [swap(shard, "edge", 2 * k) for k in range(1, edge_count // 2)]


def from_core(shards):
    return [one for shard in shards for one in (shard, swap(shard, "edge", 1))]


def local(
    node_feats,
    gat_weight,
    attn_src,
    attn_dst,
    neighbours,
    degree,
    halo_rows,
    halo_count,
    endpoint_rows,
    cand_ends,
    cand_count,
    labels,
    mlp_weight,
    out_weight,
):
    nodes, width = node_feats.shape
    dom_count = lax.axis_size("dom")
    edge_count = lax.axis_size("edge")
    block = halo_rows.shape[-1]
    cands = labels.shape[-1]
    hidden = out_weight.shape[0]
    halo = dom_count * block
    table = nodes + halo
    slots = dom_count * edge_count * endpoint_rows.shape[-1]
    pieces = width // 128
    everyone = ("dom", "edge")
    shape = jax.ShapeDtypeStruct

    heads = attn_src.shape[0]
    send_rows = call(
        halo_kernel,
        shape((halo, width), BF16),
        [("f", halo_count[0]), ("f", halo_rows[0, 0]), ("f", node_feats)],
        vmem_mib=60,
    )
    got_rows = lax.all_to_all(send_rows, "dom", split_axis=0, concat_axis=0, tiled=True)
    gat_shards = from_core(across(gat_weight, edge_count))
    mlp_shards = from_core(across(mlp_weight, edge_count))
    lanes = -(-max(2 * table + slots, width) // 128) * 128
    for_attend, for_score, pick = call(
        functools.partial(prepare_kernel, table),
        (
            shape((nodes + 8 * heads, lanes), BF16),
            shape((slots + 32, max(2 * cands, hidden)), BF16),
            shape((nodes, slots), BF16),
        ),
        [
            ("s", cand_count),
            ("f", neighbours.T),
            ("f", degree.reshape(1, nodes)),
            ("f", attn_src),
            ("f", attn_dst),
            ("f", endpoint_rows.reshape(1, slots)),
            ("f", cand_ends[0, 0]),
            ("f", labels[0]),
            ("f", out_weight.reshape(1, hidden)),
        ],
        vmem_mib=60,
    )
    packed = pltpu.VMEM((slots * pieces, 128), F32)
    node_out, send_ends = call(
        functools.partial(attend_kernel, edge_count, heads, slots),
        (shape((nodes, width), BF16), shape((slots * pieces, 128), BF16)),
        [("v", node_feats), ("v", got_rows), ("v", for_attend)] + [("v", w) for w in gat_shards],
        [
            pltpu.VMEM((table, width), BF16),
            packed,
            pltpu.VMEM((table, width), BF16),
            pltpu.VMEM((nodes, table), F32),
            pltpu.VMEM((2, 2 * nodes, table), BF16),
            pltpu.VMEM((width if width // edge_count % 128 else 16, width), BF16),
        ],
    )
    got_ends = lax.all_to_all(send_ends, everyone, split_axis=0, concat_axis=0, tiled=True)
    scores, send_back = call(
        functools.partial(score_kernel, edge_count, cands),
        (shape((1, cands), F32), shape((slots * pieces, 128), BF16)),
        [("v", got_ends), ("v", for_score)]
        + [("v", w) for w in mlp_shards],
        [
            pltpu.VMEM((cands, 2 * width), BF16),
            packed,
            pltpu.VMEM((2, 2 * slots, hidden), BF16),
            pltpu.VMEM((2, slots, width), F32),
        ],
    )
    got_back = lax.all_to_all(send_back, everyone, split_axis=0, concat_axis=0, tiled=True)
    node_grad = call(
        scatter_kernel, shape((nodes, width), F32), [("v", pick), ("v", got_back)], [packed]
    )
    return (node_out, scores.reshape(1, 1, cands), node_grad)


def solution(mesh):
    in_specs = (
        P(("dom", "edge"), None),
        P("edge", None),
        P(),
        P(),
        P(("dom", "edge"), None),
        P(("dom", "edge")),
        P("dom", "edge", None, None),
        P("dom", "edge", None),
        P("dom", "edge", None, None, None),
        P("dom", "edge", None, None),
        P("dom", "edge"),
        P("dom", "edge", None),
        P("edge", None),
        P(),
    )
    out_specs = (P(("dom", "edge"), None), P("dom", "edge", None), P(("dom", "edge"), None))
    return jax.shard_map(local, mesh=mesh, in_specs=in_specs, out_specs=out_specs, check_vma=False)
```

```python
import functools

import jax
import jax.numpy as jnp
from jax import lax
from jax.experimental import pallas as pl
from jax.experimental.pallas import tpu as pltpu
from jax.sharding import PartitionSpec as P

F32 = jnp.float32
BF16 = jnp.bfloat16
LOG2_E = 1.4426950408889634
DEAD = 64.0
VMEM = pl.BlockSpec(memory_space=pltpu.VMEM)
SPACES = {
    "v": VMEM,
    "s": pl.BlockSpec(memory_space=pltpu.SMEM),
    "f": pl.BlockSpec(memory_space=pl.ANY),
    "any": pl.BlockSpec(memory_space=pl.ANY),
}


def dot(a, b, dims=((1,), (0,))):
    return lax.dot_general(a, b, (dims, ((), ())), preferred_element_type=F32)


def call(kernel, outs, ins, scratch=(), vmem_mib=20, out_space="v"):
    fetched = [i for i, (space, _) in enumerate(ins) if space == "f"]

    def body(*refs):
        refs = list(refs)
        local_count = len(fetched) + 1
        own, (held, sems) = refs[:-local_count], (refs[-local_count:-1], refs[-1])
        copies = []
        for n, i in enumerate(fetched):
            copies.append(pltpu.make_async_copy(own[i], held[n], sems.at[n]))
            copies[-1].start()
            own[i] = held[n]

        def ready():
            for copy in copies:
                copy.wait()

        kernel(ready, *own)

    return pl.pallas_call(
        body,
        out_shape=outs,
        in_specs=[SPACES[space] for space, _ in ins],
        out_specs=jax.tree.map(lambda _: SPACES[out_space], outs),
        scratch_shapes=list(scratch)
        + [pltpu.VMEM(ins[i][1].shape, ins[i][1].dtype) for i in fetched]
        + [pltpu.SemaphoreType.DMA((max(1, len(fetched)),))],
        compiler_params=pltpu.CompilerParams(vmem_limit_bytes=vmem_mib * 1024 * 1024),
    )(*[array for _, array in ins])


def halo_kernel(
    ready, count_ref, rows_ref, feats_ref, out_ref, held_ref, done_ref, in_sems, out_sems
):
    chunks = in_sems.shape[0]
    wide = feats_ref.shape[1] // chunks
    cols = [pl.ds(i * wide, wide) for i in range(chunks)]
    loads = [
        pltpu.make_async_copy(feats_ref.at[:, c], held_ref.at[:, c], in_sems.at[i])
        for i, c in enumerate(cols)
    ]
    stores = [
        pltpu.make_async_copy(done_ref.at[:, c], out_ref.at[:, c], out_sems.at[i])
        for i, c in enumerate(cols)
    ]
    for load in loads:
        load.start()
    doms, block = rows_ref.shape
    total = doms * block
    nodes = feats_ref.shape[0]
    at = lax.broadcasted_iota(jnp.int32, (1, block), 1)
    ready()
    pieces = [
        jnp.where(at < count_ref[:, s : s + 1], rows_ref[s : s + 1, :], -1) for s in range(doms)
    ]
    flat = jnp.concatenate(pieces, axis=1)
    pick = (lax.broadcasted_iota(jnp.int32, (nodes, total), 0) == flat).astype(F32).astype(BF16)
    first = lax.broadcasted_iota(jnp.int32, (16, total), 0) == 0
    dead = jnp.where(first & (flat < 0), 1.0, 0.0).astype(BF16)
    mark_at = (lax.broadcasted_iota(jnp.int32, (16, wide), 0) == 0) & (
        lax.broadcasted_iota(jnp.int32, (16, wide), 1) == 0
    )
    mark = jnp.where(mark_at, DEAD, 0.0).astype(BF16)
    for i, c in enumerate(cols):
        loads[i].wait()
        rows = dot(pick, held_ref[:, c], ((0,), (0,)))
        if i == 0:
            rows = rows + dot(dead, mark, ((0,), (0,)))
        done_ref[:, c] = rows.astype(BF16)
        stores[i].start()
    for store in stores:
        store.wait()


def block_diagonal(vectors):
    heads, size = vectors.shape
    wide = jnp.concatenate([vectors] * heads, axis=1)
    lane_head = lax.broadcasted_iota(jnp.int32, wide.shape, 1) // size
    wide = jnp.where(lane_head == lax.broadcasted_iota(jnp.int32, wide.shape, 0), wide, 0.0)
    high = wide.astype(BF16).astype(F32)
    middle = (wide - high).astype(BF16).astype(F32)
    low = (wide - high - middle).astype(BF16).astype(F32)
    return jnp.concatenate([high, middle, low, jnp.zeros_like(wide)], axis=0).astype(BF16)


def prepare_kernel(
    table,
    ready,
    live_ref,
    neigh_ref,
    degree_ref,
    src_ref,
    dst_ref,
    ends_ref,
    cand_ref,
    labels_ref,
    out_w_ref,
    for_attend_ref,
    for_score_ref,
    pick_ref,
):
    ready()
    nodes, ends = pick_ref.shape
    heads, size = src_ref.shape
    slots = neigh_ref.shape[0]
    ids = neigh_ref[...]
    ids = jnp.where(lax.broadcasted_iota(jnp.int32, ids.shape, 0) < degree_ref[...], ids, -1)
    for base in range(0, table, nodes):
        at = base + lax.broadcasted_iota(jnp.int32, (nodes, nodes), 0)
        total = jnp.zeros((nodes, nodes), F32)
        if base == 0:
            total = (at == lax.broadcasted_iota(jnp.int32, (nodes, nodes), 1)).astype(F32)
        for j in range(slots):
            total = total + (at == ids[j : j + 1, :]).astype(F32)
        total = total.T
        power = jnp.where(total > 1, 2.0, total)
        power = jnp.where(total > 2, 4.0, power)
        power = jnp.where(total > 5, 8.0, power)
        power = jnp.where(total > 13, 16.0, power)
        for_attend_ref[:nodes, base : base + nodes] = total.astype(BF16)
        for_attend_ref[:nodes, table + base : table + base + nodes] = power.astype(BF16)
    node_at = lax.broadcasted_iota(jnp.int32, (nodes, ends), 0)
    pick = (node_at == ends_ref[...]).astype(F32).astype(BF16)
    pick_ref[...] = pick
    for_attend_ref[:nodes, 2 * table : 2 * table + ends] = pick
    for_attend_ref[nodes : nodes + 4 * heads, : heads * size] = block_diagonal(src_ref[...])
    for_attend_ref[nodes + 4 * heads :, : heads * size] = block_diagonal(dst_ref[...])
    cands = cand_ref.shape[1]
    hidden = out_w_ref.shape[1]
    slot_at = lax.broadcasted_iota(jnp.int32, (ends, cands), 0)
    for i in range(2):
        one_hot = (slot_at == cand_ref[i : i + 1, :]).astype(F32).astype(BF16)
        for_score_ref[:ends, i * cands : (i + 1) * cands] = one_hot
    live = (lax.broadcasted_iota(jnp.int32, (1, cands), 1) < live_ref[0, 0]).astype(F32)
    known = jnp.concatenate([live, labels_ref[...].astype(F32), jnp.zeros((14, cands), F32)], axis=0)
    for_score_ref[ends : ends + 16, :cands] = known.astype(BF16)
    high = out_w_ref[...].astype(BF16).astype(F32)
    middle = (out_w_ref[...] - high).astype(BF16).astype(F32)
    low = out_w_ref[...] - high - middle
    whole = jnp.concatenate([high, middle, low, jnp.zeros((13, hidden), F32)], axis=0)
    for_score_ref[ends + 16 :, :hidden] = whole.astype(BF16)


def shard_row(i, shards):
    depth = shards[0].shape[0]
    return pl.multiple_of((lax.axis_index("edge") ^ i) * depth, depth)


def shard_dots(rows_ref, shards, whole_ref=None):
    depth = shards[0].shape[0]
    if depth % 128:
        for i, shard in enumerate(shards):
            whole_ref[pl.ds(shard_row(i, shards), depth), :] = shard[...]
        return dot(rows_ref[...], whole_ref[...])
    total = None
    for i, shard in enumerate(shards):
        cols = pl.ds(shard_row(i, shards), depth)
        part = dot(rows_ref[:, cols], shard[...])
        total = part if total is None else total + part
    return total


def attend_kernel(shard_count, heads, slots, ready, own_ref, got_ref, known_ref, *rest):
    shards = rest[:shard_count]
    out_ref, send_ref, proj_ref, stage_ref, rows_ref, bias_ref, mix_ref, whole_ref = rest[-8:]
    ready()
    nodes, width = own_ref.shape
    table = proj_ref.shape[0]
    size = width // heads
    diag_src_ref = known_ref.at[nodes : nodes + 4 * heads, :width]
    diag_dst_ref = known_ref.at[nodes + 4 * heads :, :width]
    count_ref = known_ref.at[:nodes, :table]
    power_ref = known_ref.at[:nodes, table : 2 * table]
    pick_ref = known_ref.at[:nodes, 2 * table : 2 * table + slots]
    rows_ref[:nodes, :] = own_ref[...]
    rows_ref[nodes:, :] = got_ref[...]
    proj_ref[...] = shard_dots(rows_ref, shards, whole_ref).astype(BF16)
    parts = dot(diag_src_ref[...], proj_ref[...], ((1,), (1,)))
    src = parts[:heads] + parts[heads : 2 * heads] + parts[2 * heads : 3 * heads]
    src = src.astype(BF16).astype(F32) * LOG2_E
    parts = dot(proj_ref[:nodes, :], diag_dst_ref[...], ((1,), (1,)))
    dst = parts[:, :heads] + parts[:, heads : 2 * heads] + parts[:, 2 * heads : 3 * heads]
    dst = dst * LOG2_E
    first_lane = (lax.broadcasted_iota(jnp.int32, (16, 128), 1) == 0).astype(F32).astype(BF16)
    mark = dot(first_lane, rows_ref[nodes:, :128], ((1,), (1,)))[:1]
    hide = jnp.where(mark < DEAD / 2, 0.0, -jnp.inf)
    hide = jnp.concatenate([jnp.zeros((1, nodes), F32), hide], axis=1)
    bias_ref[...] = jnp.where(count_ref[...] > 0, hide, -jnp.inf)
    chunk = 32
    for h in range(heads):
        for r in range(0, nodes, chunk):
            here = slice(r, r + chunk)
            logit = dst[here, h : h + 1] + src[h : h + 1, :]
            logit = jnp.maximum(logit, 0.2 * logit) + bias_ref[here, :]
            terms = jnp.exp2(logit - jnp.max(logit, axis=1, keepdims=True))
            count = count_ref[here, :]
            power = power_ref[here, :]
            running = jnp.sum(count.astype(F32) * terms, axis=1, keepdims=True)
            weight = (terms * (1.0 / running)).astype(BF16)
            mix_ref[h % 2, here, :] = weight * power
            mix_ref[h % 2, nodes + r : nodes + r + chunk, :] = weight * (count - power)
        both = dot(mix_ref[h % 2], proj_ref[:, h * size : (h + 1) * size])
        total = both[:nodes] + both[nodes:]
        total = jnp.where(total > 0, total, jnp.exp(jnp.minimum(total, 0.0)) - 1.0)
        out_ref[:, h * size : (h + 1) * size] = total.astype(BF16)
    pack_rows(dot(pick_ref[...], out_ref[...], ((0,), (0,))), stage_ref, send_ref)


def pack_rows(rows, stage_ref, out_ref):
    slots, width = rows.shape
    pieces = width // 128
    for c in range(pieces):
        stage_ref[pl.ds(c, slots, stride=pieces), :] = rows[:, c * 128 : (c + 1) * 128]
    out_ref[...] = stage_ref[...].astype(BF16)


def unpack_rows(ref, stage_ref, pieces):
    stage_ref[...] = ref[...].astype(F32)
    slots = ref.shape[0] // pieces
    parts = [stage_ref[pl.ds(c, slots, stride=pieces), :] for c in range(pieces)]
    return jnp.concatenate(parts, axis=1).astype(BF16)


def score_kernel(shard_count, cands, ready, got_ref, known_ref, *rest):
    shards = rest[:shard_count]
    scores_ref, back_ref, rows_ref, stage_ref, sum_ref, grad_ref, part_ref = rest[shard_count:]
    ready()
    depth, hidden = shards[0].shape
    slots, width = grad_ref.shape[1:]
    picks = [known_ref[:slots, i * cands : (i + 1) * cands] for i in range(2)]
    known = known_ref[slots : slots + 16, :cands].astype(F32).T
    live, label = known[:, :1], known[:, 1:2]
    out_w = known_ref[slots + 16 :, :hidden].astype(F32)
    out_w = out_w[:1] + out_w[1:2] + out_w[2:3]
    rows = unpack_rows(got_ref, stage_ref, width // 128)
    if slots > cands:
        for i in range(2):
            pair = dot(picks[i], rows, ((0,), (0,)))
            rows_ref[:, i * width : (i + 1) * width] = pair.astype(BF16)
        pre_act = shard_dots(rows_ref, shards)
    else:
        rows_ref[...] = rows
        part_ref[...] = jnp.zeros_like(part_ref)
        for i, shard in enumerate(shards):
            row = shard_row(i, shards)
            cols = pl.ds(pl.multiple_of(row % width, depth), depth)
            part_ref[row // width] += dot(rows_ref[:, cols], shard[...])
        pre_act = None
        for i in range(2):
            rest = part_ref[i]
            for _ in range(3):
                high = rest.astype(BF16)
                rest = rest - high.astype(F32)
                term = dot(picks[i], high, ((0,), (0,)))
                pre_act = term if pre_act is None else pre_act + term
    gate = jax.nn.sigmoid(pre_act)
    score = jnp.sum(pre_act * gate * out_w, axis=1, keepdims=True) * live
    scores_ref[...] = jnp.broadcast_to(score, (cands, 128)).T[:1]
    grad_score = (jax.nn.sigmoid(score) - label) * live
    grad_pre = (grad_score * out_w * (gate * (1.0 + pre_act * (1.0 - gate)))).astype(BF16)
    for i in range(2):
        total = dot(picks[i], grad_pre)
        high = total.astype(BF16)
        sum_ref[i, :slots, :] = high
        sum_ref[i, slots:, :] = (total - high.astype(F32)).astype(BF16)
    for i, shard in enumerate(shards):
        row = shard_row(i, shards)
        half = row // width
        col = pl.multiple_of(row % width, depth)
        both = dot(sum_ref[half], shard[...], ((1,), (1,)))
        grad_ref[half, :, pl.ds(col, depth)] = both[:slots] + both[slots:]
    pack_rows(grad_ref[0] + grad_ref[1], stage_ref, back_ref)


def scatter_kernel(ready, pick_ref, got_ref, out_ref, stage_ref):
    ready()
    rows = unpack_rows(got_ref, stage_ref, out_ref.shape[1] // 128)
    out_ref[...] = dot(pick_ref[...], rows)


def swap(array, axis, k):
    count = lax.axis_size(axis)
    return lax.ppermute(array, axis, [(i, i ^ k) for i in range(count)])


def across(shard, edge_count):
    return [shard] + [swap(shard, "edge", 2 * k) for k in range(1, edge_count // 2)]


def from_core(shards):
    return [one for shard in shards for one in (shard, swap(shard, "edge", 1))]


def local(
    node_feats,
    gat_weight,
    attn_src,
    attn_dst,
    neighbours,
    degree,
    halo_rows,
    halo_count,
    endpoint_rows,
    cand_ends,
    cand_count,
    labels,
    mlp_weight,
    out_weight,
):
    nodes, width = node_feats.shape
    dom_count = lax.axis_size("dom")
    edge_count = lax.axis_size("edge")
    block = halo_rows.shape[-1]
    cands = labels.shape[-1]
    hidden = out_weight.shape[0]
    halo = dom_count * block
    table = nodes + halo
    slots = dom_count * edge_count * endpoint_rows.shape[-1]
    pieces = width // 128
    everyone = ("dom", "edge")
    shape = jax.ShapeDtypeStruct

    heads = attn_src.shape[0]
    send_rows = call(
        halo_kernel,
        shape((halo, width), BF16),
        [("f", halo_count[0]), ("f", halo_rows[0, 0]), ("any", node_feats)],
        [
            pltpu.VMEM((nodes, width), BF16),
            pltpu.VMEM((halo, width), BF16),
            pltpu.SemaphoreType.DMA((4,)),
            pltpu.SemaphoreType.DMA((4,)),
        ],
        vmem_mib=60,
        out_space="any",
    )
    got_rows = lax.all_to_all(send_rows, "dom", split_axis=0, concat_axis=0, tiled=True)
    gat_across = across(gat_weight, edge_count)
    mlp_across = across(mlp_weight, edge_count)
    lanes = -(-max(2 * table + slots, width) // 128) * 128
    for_attend, for_score, pick = call(
        functools.partial(prepare_kernel, table),
        (
            shape((nodes + 8 * heads, lanes), BF16),
            shape((slots + 32, max(2 * cands, hidden)), BF16),
            shape((nodes, slots), BF16),
        ),
        [
            ("s", cand_count),
            ("f", neighbours.T),
            ("f", degree.reshape(1, nodes)),
            ("f", attn_src),
            ("f", attn_dst),
            ("f", endpoint_rows.reshape(1, slots)),
            ("f", cand_ends[0, 0]),
            ("f", labels[0]),
            ("f", out_weight.reshape(1, hidden)),
        ],
        vmem_mib=60,
    )
    gat_across = lax.optimization_barrier((*gat_across, for_attend))[:-1]
    gat_shards = from_core(gat_across)
    packed = pltpu.VMEM((slots * pieces, 128), F32)
    node_out, send_ends = call(
        functools.partial(attend_kernel, edge_count, heads, slots),
        (shape((nodes, width), BF16), shape((slots * pieces, 128), BF16)),
        [("v", node_feats), ("v", got_rows), ("v", for_attend)] + [("v", w) for w in gat_shards],
        [
            pltpu.VMEM((table, width), BF16),
            packed,
            pltpu.VMEM((table, width), BF16),
            pltpu.VMEM((nodes, table), F32),
            pltpu.VMEM((2, 2 * nodes, table), BF16),
            pltpu.VMEM((width if width // edge_count % 128 else 16, width), BF16),
        ],
    )
    mlp_shards = from_core(lax.optimization_barrier((*mlp_across, send_ends))[:-1])
    got_ends = lax.all_to_all(send_ends, everyone, split_axis=0, concat_axis=0, tiled=True)
    scores, send_back = call(
        functools.partial(score_kernel, edge_count, cands),
        (shape((1, cands), F32), shape((slots * pieces, 128), BF16)),
        [("v", got_ends), ("v", for_score)]
        + [("v", w) for w in mlp_shards],
        [
            pltpu.VMEM((cands, 2 * width) if slots > cands else (slots, width), BF16),
            packed,
            pltpu.VMEM((2, 2 * slots, hidden), BF16),
            pltpu.VMEM((2, slots, width), F32),
            pltpu.VMEM((2, slots, hidden), F32),
        ],
    )
    got_back = lax.all_to_all(send_back, everyone, split_axis=0, concat_axis=0, tiled=True)
    node_grad = call(
        scatter_kernel, shape((nodes, width), F32), [("v", pick), ("v", got_back)], [packed]
    )
    return (node_out, scores.reshape(1, 1, cands), node_grad)


def solution(mesh):
    in_specs = (
        P(("dom", "edge"), None),
        P("edge", None),
        P(),
        P(),
        P(("dom", "edge"), None),
        P(("dom", "edge")),
        P("dom", "edge", None, None),
        P("dom", "edge", None),
        P("dom", "edge", None, None, None),
        P("dom", "edge", None, None),
        P("dom", "edge"),
        P("dom", "edge", None),
        P("edge", None),
        P(),
    )
    out_specs = (P(("dom", "edge"), None), P("dom", "edge", None), P(("dom", "edge"), None))
    return jax.shard_map(local, mesh=mesh, in_specs=in_specs, out_specs=out_specs, check_vma=False)
```

```python
import functools

import jax
import jax.numpy as jnp
from jax import lax
from jax.experimental import pallas as pl
from jax.experimental.pallas import tpu as pltpu
from jax.sharding import PartitionSpec as P

F32 = jnp.float32
BF16 = jnp.bfloat16
LOG2_E = 1.4426950408889634
DEAD = 64.0
VMEM = pl.BlockSpec(memory_space=pltpu.VMEM)
SPACES = {
    "v": VMEM,
    "s": pl.BlockSpec(memory_space=pltpu.SMEM),
    "f": pl.BlockSpec(memory_space=pl.ANY),
    "any": pl.BlockSpec(memory_space=pl.ANY),
}


def dot(a, b, dims=((1,), (0,))):
    return lax.dot_general(a, b, (dims, ((), ())), preferred_element_type=F32)


def call(kernel, outs, ins, scratch=(), vmem_mib=20, out_space="v"):
    fetched = [i for i, (space, _) in enumerate(ins) if space == "f"]

    def body(*refs):
        refs = list(refs)
        local_count = len(fetched) + 1
        own, (held, sems) = refs[:-local_count], (refs[-local_count:-1], refs[-1])
        copies = []
        for n, i in enumerate(fetched):
            copies.append(pltpu.make_async_copy(own[i], held[n], sems.at[n]))
            copies[-1].start()
            own[i] = held[n]

        def ready():
            for copy in copies:
                copy.wait()

        kernel(ready, *own)

    return pl.pallas_call(
        body,
        out_shape=outs,
        in_specs=[SPACES[space] for space, _ in ins],
        out_specs=jax.tree.map(lambda _: SPACES[out_space], outs),
        scratch_shapes=list(scratch)
        + [pltpu.VMEM(ins[i][1].shape, ins[i][1].dtype) for i in fetched]
        + [pltpu.SemaphoreType.DMA((max(1, len(fetched)),))],
        compiler_params=pltpu.CompilerParams(vmem_limit_bytes=vmem_mib * 1024 * 1024),
    )(*[array for _, array in ins])


def halo_kernel(ready, count_ref, rows_ref, feats_ref, out_ref):
    doms, block = rows_ref.shape
    at = lax.broadcasted_iota(jnp.int32, (1, block), 1)
    ready()
    pieces = [
        jnp.where(at < count_ref[:, s : s + 1], rows_ref[s : s + 1, :], -1) for s in range(doms)
    ]
    flat = jnp.concatenate(pieces, axis=1)
    total = doms * block
    nodes = feats_ref.shape[0]
    pick = (lax.broadcasted_iota(jnp.int32, (nodes, total), 0) == flat).astype(F32).astype(BF16)
    rows = dot(pick, feats_ref[...], ((0,), (0,)))
    first = lax.broadcasted_iota(jnp.int32, (16, total), 0) == 0
    dead = jnp.where(first & (flat < 0), 1.0, 0.0).astype(BF16)
    mark_at = (lax.broadcasted_iota(jnp.int32, (16, 128), 0) == 0) & (
        lax.broadcasted_iota(jnp.int32, (16, 128), 1) == 0
    )
    mark = jnp.where(mark_at, DEAD, 0.0).astype(BF16)
    out_ref[:, :128] = (rows[:, :128] + dot(dead, mark, ((0,), (0,)))).astype(BF16)
    out_ref[:, 128:] = rows[:, 128:].astype(BF16)


def three_parts(values):
    high = values.astype(BF16).astype(F32)
    middle = (values - high).astype(BF16).astype(F32)
    return jnp.concatenate([high, middle, values - high - middle], axis=0)


def block_diagonal(parts, heads):
    parts = parts.astype(F32)
    wide = jnp.concatenate([parts] * heads, axis=1)
    lane_head = lax.broadcasted_iota(jnp.int32, wide.shape, 1) // parts.shape[1]
    row_head = lax.broadcasted_iota(jnp.int32, wide.shape, 0) % heads
    wide = jnp.where(lane_head == row_head, wide, 0.0)
    return jnp.concatenate([wide, jnp.zeros((heads, wide.shape[1]), F32)], axis=0).astype(BF16)


def prepare_kernel(
    table,
    ready,
    live_ref,
    neigh_ref,
    degree_ref,
    src_ref,
    dst_ref,
    ends_ref,
    cand_ref,
    labels_ref,
    out_w_ref,
    for_attend_ref,
    for_score_ref,
    pick_ref,
):
    ready()
    nodes, ends = pick_ref.shape
    heads, size = src_ref.shape
    slots = neigh_ref.shape[0]
    ids = neigh_ref[...]
    ids = jnp.where(lax.broadcasted_iota(jnp.int32, ids.shape, 0) < degree_ref[...], ids, -1)
    for base in range(0, table, nodes):
        at = base + lax.broadcasted_iota(jnp.int32, (nodes, nodes), 0)
        total = jnp.zeros((nodes, nodes), F32)
        if base == 0:
            total = (at == lax.broadcasted_iota(jnp.int32, (nodes, nodes), 1)).astype(F32)
        for j in range(slots):
            total = total + (at == ids[j : j + 1, :]).astype(F32)
        total = total.T
        power = jnp.where(total > 1, 2.0, total)
        power = jnp.where(total > 2, 4.0, power)
        power = jnp.where(total > 5, 8.0, power)
        power = jnp.where(total > 13, 16.0, power)
        for_attend_ref[:, base : base + nodes] = total.astype(BF16)
        for_attend_ref[:, table + base : table + base + nodes] = power.astype(BF16)
    node_at = lax.broadcasted_iota(jnp.int32, (nodes, ends), 0)
    pick = (node_at == ends_ref[...]).astype(F32).astype(BF16)
    pick_ref[...] = pick
    first = 2 * table + size
    for_attend_ref[:, first : first + ends] = pick
    vectors = [three_parts(src_ref[...]), three_parts(dst_ref[...])]
    for_attend_ref[: 6 * heads, 2 * table : first] = jnp.concatenate(vectors, axis=0).astype(BF16)
    cands = cand_ref.shape[1]
    hidden = out_w_ref.shape[1]
    slot_at = lax.broadcasted_iota(jnp.int32, (ends, cands), 0)
    for i in range(2):
        one_hot = (slot_at == cand_ref[i : i + 1, :]).astype(F32).astype(BF16)
        for_score_ref[:ends, i * cands : (i + 1) * cands] = one_hot
    live = (lax.broadcasted_iota(jnp.int32, (1, cands), 1) < live_ref[0, 0]).astype(F32)
    known = jnp.concatenate([live, labels_ref[...].astype(F32), jnp.zeros((14, cands), F32)], axis=0)
    for_score_ref[ends : ends + 16, :cands] = known.astype(BF16)
    whole = jnp.concatenate([three_parts(out_w_ref[...]), jnp.zeros((13, hidden), F32)], axis=0)
    for_score_ref[ends + 16 :, :hidden] = whole.astype(BF16)


def shard_row(i, depth):
    return pl.multiple_of((lax.axis_index("edge") ^ i) * depth, depth)


def shard_dots(rows_ref, shards, whole_ref=None):
    depth = shards[0].shape[0]
    if depth % 128:
        for i, shard in enumerate(shards):
            whole_ref[pl.ds(shard_row(i, depth), depth), :] = shard[...]
        return dot(rows_ref[...], whole_ref[...])
    total = None
    for i, shard in enumerate(shards):
        cols = pl.ds(shard_row(i, depth), depth)
        part = dot(rows_ref[:, cols], shard[...])
        total = part if total is None else total + part
    return total


def attend_kernel(shard_count, heads, slots, ready, own_ref, got_ref, known_ref, *rest):
    shards = rest[:shard_count]
    out_ref, send_ref, proj_ref, stage_ref, rows_ref, bias_ref, mix_ref, whole_ref = rest[-8:]
    ready()
    nodes, width = own_ref.shape
    table = proj_ref.shape[0]
    size = width // heads
    count_ref = known_ref.at[:, :table]
    power_ref = known_ref.at[:, table : 2 * table]
    pick_ref = known_ref.at[:, 2 * table + size : 2 * table + size + slots]
    vectors = known_ref[: 6 * heads, 2 * table : 2 * table + size]
    diag_src = block_diagonal(vectors[: 3 * heads], heads)
    diag_dst = block_diagonal(vectors[3 * heads :], heads)
    rows_ref[:nodes, :] = own_ref[...]
    rows_ref[nodes:, :] = got_ref[...]
    proj_ref[...] = shard_dots(rows_ref, shards, whole_ref).astype(BF16)
    parts = dot(diag_src, proj_ref[...], ((1,), (1,)))
    src = parts[:heads] + parts[heads : 2 * heads] + parts[2 * heads : 3 * heads]
    src = src.astype(BF16).astype(F32) * LOG2_E
    parts = dot(proj_ref[:nodes, :], diag_dst, ((1,), (1,)))
    dst = parts[:, :heads] + parts[:, heads : 2 * heads] + parts[:, 2 * heads : 3 * heads]
    dst = dst * LOG2_E
    first_lane = (lax.broadcasted_iota(jnp.int32, (16, 128), 1) == 0).astype(F32).astype(BF16)
    mark = dot(first_lane, rows_ref[nodes:, :128], ((1,), (1,)))[:1]
    hide = jnp.where(mark < DEAD / 2, 0.0, -jnp.inf)
    hide = jnp.concatenate([jnp.zeros((1, nodes), F32), hide], axis=1)
    bias_ref[...] = jnp.where(count_ref[...] > 0, hide, -jnp.inf)
    chunk = 32
    for h in range(heads):
        for r in range(0, nodes, chunk):
            here = slice(r, r + chunk)
            logit = dst[here, h : h + 1] + src[h : h + 1, :]
            logit = jnp.maximum(logit, 0.2 * logit) + bias_ref[here, :]
            terms = jnp.exp2(logit - jnp.max(logit, axis=1, keepdims=True))
            count = count_ref[here, :]
            power = power_ref[here, :]
            running = jnp.sum(count.astype(F32) * terms, axis=1, keepdims=True)
            weight = (terms * (1.0 / running)).astype(BF16)
            mix_ref[h % 2, here, :] = weight * power
            mix_ref[h % 2, nodes + r : nodes + r + chunk, :] = weight * (count - power)
        both = dot(mix_ref[h % 2], proj_ref[:, h * size : (h + 1) * size])
        total = both[:nodes] + both[nodes:]
        total = jnp.where(total > 0, total, jnp.exp(jnp.minimum(total, 0.0)) - 1.0)
        out_ref[:, h * size : (h + 1) * size] = total.astype(BF16)
    pack_rows(dot(pick_ref[...], out_ref[...], ((0,), (0,))), stage_ref, send_ref)


def pack_rows(rows, stage_ref, out_ref):
    slots, width = rows.shape
    pieces = width // 128
    for c in range(pieces):
        stage_ref[pl.ds(c, slots, stride=pieces), :] = rows[:, c * 128 : (c + 1) * 128]
    out_ref[...] = stage_ref[...].astype(BF16)


def unpack_rows(ref, stage_ref, pieces):
    stage_ref[...] = ref[...].astype(F32)
    slots = ref.shape[0] // pieces
    parts = [stage_ref[pl.ds(c, slots, stride=pieces), :] for c in range(pieces)]
    return jnp.concatenate(parts, axis=1).astype(BF16)


def add_shards(rows_ref, indices, shards, part_ref):
    depth = shards[0].shape[0]
    span = rows_ref.shape[1]
    for i, shard in zip(indices, shards):
        row = shard_row(i, depth)
        cols = pl.ds(pl.multiple_of(row % span, depth), depth)
        part_ref[row // span] += dot(rows_ref[:, cols], shard[...])


def first_kernel(indices, cands, ready, got_ref, known_ref, *rest):
    shards = rest[:-3]
    rows_ref, part_ref, stage_ref = rest[-3:]
    ready()
    slots = known_ref.shape[0] - 32
    width = got_ref.shape[0] * 128 // slots
    rows = unpack_rows(got_ref, stage_ref, width // 128)
    if slots > cands:
        for i in range(2):
            pick = known_ref[:slots, i * cands : (i + 1) * cands]
            pair = dot(pick, rows, ((0,), (0,)))
            rows_ref[:, i * width : (i + 1) * width] = pair.astype(BF16)
    else:
        rows_ref[...] = rows
    part_ref[...] = jnp.zeros_like(part_ref)
    add_shards(rows_ref, indices, shards, part_ref)


def score_kernel(late, cands, ready, rows_ref, first_ref, known_ref, *rest):
    shards = rest[:-6]
    scores_ref, back_ref, stage_ref, sum_ref, grad_ref, part_ref = rest[-6:]
    ready()
    depth, hidden = shards[0].shape
    slots, width = grad_ref.shape[1:]
    picks = [known_ref[:slots, i * cands : (i + 1) * cands] for i in range(2)]
    known = known_ref[slots : slots + 16, :cands].astype(F32).T
    live, label = known[:, :1], known[:, 1:2]
    out_w = known_ref[slots + 16 :, :hidden].astype(F32)
    out_w = out_w[:1] + out_w[1:2] + out_w[2:3]
    part_ref[...] = first_ref[...]
    add_shards(rows_ref, late, [shards[i] for i in late], part_ref)
    if slots > cands:
        pre_act = part_ref[0]
    else:
        pre_act = None
        for i in range(2):
            rest = part_ref[i]
            for _ in range(3):
                high = rest.astype(BF16)
                rest = rest - high.astype(F32)
                term = dot(picks[i], high, ((0,), (0,)))
                pre_act = term if pre_act is None else pre_act + term
    gate = jax.nn.sigmoid(pre_act)
    score = jnp.sum(pre_act * gate * out_w, axis=1, keepdims=True) * live
    scores_ref[...] = jnp.broadcast_to(score, (cands, 128)).T[:1]
    grad_score = (jax.nn.sigmoid(score) - label) * live
    grad_pre = (grad_score * out_w * (gate * (1.0 + pre_act * (1.0 - gate)))).astype(BF16)
    for i in range(2):
        total = dot(picks[i], grad_pre)
        high = total.astype(BF16)
        sum_ref[i, :slots, :] = high
        sum_ref[i, slots:, :] = (total - high.astype(F32)).astype(BF16)
    for i, shard in enumerate(shards):
        row = shard_row(i, depth)
        half = row // width
        col = pl.multiple_of(row % width, depth)
        both = dot(sum_ref[half], shard[...], ((1,), (1,)))
        grad_ref[half, :, pl.ds(col, depth)] = both[:slots] + both[slots:]
    pack_rows(grad_ref[0] + grad_ref[1], stage_ref, back_ref)


def scatter_kernel(ready, pick_ref, got_ref, out_ref, stage_ref):
    ready()
    rows = unpack_rows(got_ref, stage_ref, out_ref.shape[1] // 128)
    out_ref[...] = dot(pick_ref[...], rows)


def swap(array, axis, k):
    count = lax.axis_size(axis)
    return lax.ppermute(array, axis, [(i, i ^ k) for i in range(count)])


def across(shard, edge_count):
    return [shard] + [swap(shard, "edge", 2 * k) for k in range(1, edge_count // 2)]


def from_core(shards):
    return [one for shard in shards for one in (shard, swap(shard, "edge", 1))]


def local(
    node_feats,
    gat_weight,
    attn_src,
    attn_dst,
    neighbours,
    degree,
    halo_rows,
    halo_count,
    endpoint_rows,
    cand_ends,
    cand_count,
    labels,
    mlp_weight,
    out_weight,
):
    nodes, width = node_feats.shape
    dom_count = lax.axis_size("dom")
    edge_count = lax.axis_size("edge")
    block = halo_rows.shape[-1]
    cands = labels.shape[-1]
    hidden = out_weight.shape[0]
    halo = dom_count * block
    table = nodes + halo
    slots = dom_count * edge_count * endpoint_rows.shape[-1]
    pieces = width // 128
    everyone = ("dom", "edge")
    shape = jax.ShapeDtypeStruct

    heads = attn_src.shape[0]
    send_rows = call(
        halo_kernel,
        shape((halo, width), BF16),
        [("f", halo_count[0]), ("f", halo_rows[0, 0]), ("f", node_feats)],
        vmem_mib=60,
    )
    got_rows = lax.all_to_all(send_rows, "dom", split_axis=0, concat_axis=0, tiled=True)
    gat_across = across(gat_weight, edge_count)
    mlp_across = across(mlp_weight, edge_count)
    lanes = -(-(2 * table + attn_src.shape[1] + slots) // 128) * 128
    for_attend, for_score, pick = call(
        functools.partial(prepare_kernel, table),
        (
            shape((nodes, lanes), BF16),
            shape((slots + 32, max(2 * cands, hidden)), BF16),
            shape((nodes, slots), BF16),
        ),
        [
            ("s", cand_count),
            ("f", neighbours.T),
            ("f", degree.reshape(1, nodes)),
            ("f", attn_src),
            ("f", attn_dst),
            ("f", endpoint_rows.reshape(1, slots)),
            ("f", cand_ends[0, 0]),
            ("f", labels[0]),
            ("f", out_weight.reshape(1, hidden)),
        ],
    )
    gat_across = lax.optimization_barrier((*gat_across, for_attend))[:-1]
    gat_shards = from_core(gat_across)
    packed = pltpu.VMEM((slots * pieces, 128), F32)
    node_out, send_ends = call(
        functools.partial(attend_kernel, edge_count, heads, slots),
        (shape((nodes, width), BF16), shape((slots * pieces, 128), BF16)),
        [("v", node_feats), ("v", got_rows), ("v", for_attend)] + [("v", w) for w in gat_shards],
        [
            pltpu.VMEM((table, width), BF16),
            packed,
            pltpu.VMEM((table, width), BF16),
            pltpu.VMEM((nodes, table), F32),
            pltpu.VMEM((2, 2 * nodes, table), BF16),
            pltpu.VMEM((width if width // edge_count % 128 else 16, width), BF16),
        ],
    )
    got_ends = lax.all_to_all(send_ends, everyone, split_axis=0, concat_axis=0, tiled=True)
    mlp_shards = [mlp_across[0], swap(mlp_across[0], "edge", 1)]
    tied = lax.optimization_barrier((*mlp_across[1:], got_ends))[:-1]
    for shard, held in zip(mlp_across[1:], tied):
        mlp_shards += [shard, swap(held, "edge", 1)]
    early = [i for i in range(edge_count) if i < 2 or i % 2 == 0]
    late = [i for i in range(edge_count) if i not in early]
    many = slots > cands
    rows, part = call(
        functools.partial(first_kernel, early, cands),
        (
            shape((cands, 2 * width) if many else (slots, width), BF16),
            shape((1, cands, hidden) if many else (2, slots, hidden), F32),
        ),
        [("v", got_ends), ("v", for_score)] + [("v", mlp_shards[i]) for i in early],
        [packed],
    )
    scores, send_back = call(
        functools.partial(score_kernel, late, cands),
        (shape((1, cands), F32), shape((slots * pieces, 128), BF16)),
        [("v", rows), ("v", part), ("v", for_score)] + [("v", w) for w in mlp_shards],
        [
            packed,
            pltpu.VMEM((2, 2 * slots, hidden), BF16),
            pltpu.VMEM((2, slots, width), F32),
            pltpu.VMEM(part.shape, F32),
        ],
    )
    got_back = lax.all_to_all(send_back, everyone, split_axis=0, concat_axis=0, tiled=True)
    node_grad = call(
        scatter_kernel, shape((nodes, width), F32), [("v", pick), ("v", got_back)], [packed]
    )
    return (node_out, scores.reshape(1, 1, cands), node_grad)


def solution(mesh):
    in_specs = (
        P(("dom", "edge"), None),
        P("edge", None),
        P(),
        P(),
        P(("dom", "edge"), None),
        P(("dom", "edge")),
        P("dom", "edge", None, None),
        P("dom", "edge", None),
        P("dom", "edge", None, None, None),
        P("dom", "edge", None, None),
        P("dom", "edge"),
        P("dom", "edge", None),
        P("edge", None),
        P(),
    )
    out_specs = (P(("dom", "edge"), None), P("dom", "edge", None), P(("dom", "edge"), None))
    return jax.shard_map(local, mesh=mesh, in_specs=in_specs, out_specs=out_specs, check_vma=False)
```

```python
import functools

import jax
import jax.numpy as jnp
from jax import lax
from jax.experimental import pallas as pl
from jax.experimental.pallas import tpu as pltpu
from jax.sharding import PartitionSpec as P

F32 = jnp.float32
BF16 = jnp.bfloat16
LOG2_E = 1.4426950408889634
DEAD = 64.0
VMEM = pl.BlockSpec(memory_space=pltpu.VMEM)
SPACES = {
    "v": VMEM,
    "s": pl.BlockSpec(memory_space=pltpu.SMEM),
    "f": pl.BlockSpec(memory_space=pl.ANY),
    "any": pl.BlockSpec(memory_space=pl.ANY),
}


def dot(a, b, dims=((1,), (0,))):
    return lax.dot_general(a, b, (dims, ((), ())), preferred_element_type=F32)


def call(kernel, outs, ins, scratch=(), vmem_mib=20, out_space="v"):
    fetched = [i for i, (space, _) in enumerate(ins) if space == "f"]

    def body(*refs):
        refs = list(refs)
        local_count = len(fetched) + 1
        own, (held, sems) = refs[:-local_count], (refs[-local_count:-1], refs[-1])
        copies = []
        for n, i in enumerate(fetched):
            copies.append(pltpu.make_async_copy(own[i], held[n], sems.at[n]))
            copies[-1].start()
            own[i] = held[n]

        def ready():
            for copy in copies:
                copy.wait()

        kernel(ready, *own)

    return pl.pallas_call(
        body,
        out_shape=outs,
        in_specs=[SPACES[space] for space, _ in ins],
        out_specs=jax.tree.map(lambda _: SPACES[out_space], outs),
        scratch_shapes=list(scratch)
        + [pltpu.VMEM(ins[i][1].shape, ins[i][1].dtype) for i in fetched]
        + [pltpu.SemaphoreType.DMA((max(1, len(fetched)),))],
        compiler_params=pltpu.CompilerParams(vmem_limit_bytes=vmem_mib * 1024 * 1024),
    )(*[array for _, array in ins])


def halo_kernel(ready, count_ref, rows_ref, feats_ref, out_ref):
    doms, block = rows_ref.shape
    at = lax.broadcasted_iota(jnp.int32, (1, block), 1)
    ready()
    pieces = [
        jnp.where(at < count_ref[:, s : s + 1], rows_ref[s : s + 1, :], -1) for s in range(doms)
    ]
    flat = jnp.concatenate(pieces, axis=1)
    total = doms * block
    nodes = feats_ref.shape[0]
    pick = (lax.broadcasted_iota(jnp.int32, (nodes, total), 0) == flat).astype(F32).astype(BF16)
    rows = dot(pick, feats_ref[...], ((0,), (0,)))
    first = lax.broadcasted_iota(jnp.int32, (16, total), 0) == 0
    dead = jnp.where(first & (flat < 0), 1.0, 0.0).astype(BF16)
    mark_at = (lax.broadcasted_iota(jnp.int32, (16, 128), 0) == 0) & (
        lax.broadcasted_iota(jnp.int32, (16, 128), 1) == 0
    )
    mark = jnp.where(mark_at, DEAD, 0.0).astype(BF16)
    out_ref[:, :128] = (rows[:, :128] + dot(dead, mark, ((0,), (0,)))).astype(BF16)
    out_ref[:, 128:] = rows[:, 128:].astype(BF16)


def three_parts(values):
    high = values.astype(BF16).astype(F32)
    middle = (values - high).astype(BF16).astype(F32)
    return jnp.concatenate([high, middle, values - high - middle], axis=0)


def block_diagonal(parts, heads):
    parts = parts.astype(F32)
    wide = jnp.concatenate([parts] * heads, axis=1)
    lane_head = lax.broadcasted_iota(jnp.int32, wide.shape, 1) // parts.shape[1]
    row_head = lax.broadcasted_iota(jnp.int32, wide.shape, 0) % heads
    wide = jnp.where(lane_head == row_head, wide, 0.0)
    return jnp.concatenate([wide, jnp.zeros((heads, wide.shape[1]), F32)], axis=0).astype(BF16)


def prepare_kernel(
    table,
    ready,
    live_ref,
    neigh_ref,
    degree_ref,
    src_ref,
    dst_ref,
    ends_ref,
    cand_ref,
    labels_ref,
    out_w_ref,
    mlp_ref,
    for_attend_ref,
    for_score_ref,
    pick_ref,
    *mlp_part_refs,
):
    ready()
    nodes, ends = pick_ref.shape
    heads, size = src_ref.shape
    slots = neigh_ref.shape[0]
    ids = neigh_ref[...]
    ids = jnp.where(lax.broadcasted_iota(jnp.int32, ids.shape, 0) < degree_ref[...], ids, -1)
    for base in range(0, table, nodes):
        at = base + lax.broadcasted_iota(jnp.int32, (nodes, nodes), 0)
        total = jnp.zeros((nodes, nodes), F32)
        if base == 0:
            total = (at == lax.broadcasted_iota(jnp.int32, (nodes, nodes), 1)).astype(F32)
        for j in range(slots):
            total = total + (at == ids[j : j + 1, :]).astype(F32)
        total = total.T
        power = jnp.where(total > 1, 2.0, total)
        power = jnp.where(total > 2, 4.0, power)
        power = jnp.where(total > 5, 8.0, power)
        power = jnp.where(total > 13, 16.0, power)
        for_attend_ref[:, base : base + nodes] = total.astype(BF16)
        for_attend_ref[:, table + base : table + base + nodes] = power.astype(BF16)
    node_at = lax.broadcasted_iota(jnp.int32, (nodes, ends), 0)
    pick = (node_at == ends_ref[...]).astype(F32).astype(BF16)
    pick_ref[...] = pick
    first = 2 * table + size
    for_attend_ref[:, first : first + ends] = pick
    vectors = [three_parts(src_ref[...]), three_parts(dst_ref[...])]
    for_attend_ref[: 6 * heads, 2 * table : first] = jnp.concatenate(vectors, axis=0).astype(BF16)
    cands = cand_ref.shape[1]
    hidden = out_w_ref.shape[1]
    slot_at = lax.broadcasted_iota(jnp.int32, (ends, cands), 0)
    for i in range(2):
        one_hot = (slot_at == cand_ref[i : i + 1, :]).astype(F32).astype(BF16)
        for_score_ref[:ends, i * cands : (i + 1) * cands] = one_hot
    live = (lax.broadcasted_iota(jnp.int32, (1, cands), 1) < live_ref[0, 0]).astype(F32)
    known = jnp.concatenate([live, labels_ref[...].astype(F32), jnp.zeros((14, cands), F32)], axis=0)
    for_score_ref[ends : ends + 16, :cands] = known.astype(BF16)
    whole = jnp.concatenate([three_parts(out_w_ref[...]), jnp.zeros((13, hidden), F32)], axis=0)
    for_score_ref[ends + 16 :, :hidden] = whole.astype(BF16)
    depth = mlp_part_refs[0].shape[0]
    for i, ref in enumerate(mlp_part_refs):
        ref[...] = mlp_ref[i * depth : (i + 1) * depth, :]


def shard_row(i, shards):
    depth = shards[0].shape[0]
    parts = len(shards) // lax.axis_size("edge")
    at = (lax.axis_index("edge") ^ (i // parts)) * parts + i % parts
    return pl.multiple_of(at * depth, depth)


def shard_dots(rows_ref, shards, whole_ref=None):
    depth = shards[0].shape[0]
    if depth % 128:
        for i, shard in enumerate(shards):
            whole_ref[pl.ds(shard_row(i, shards), depth), :] = shard[...]
        return dot(rows_ref[...], whole_ref[...])
    total = None
    for i, shard in enumerate(shards):
        cols = pl.ds(shard_row(i, shards), depth)
        part = dot(rows_ref[:, cols], shard[...])
        total = part if total is None else total + part
    return total


def attend_kernel(shard_count, heads, slots, ready, own_ref, got_ref, known_ref, *rest):
    shards = rest[:shard_count]
    out_ref, send_ref, proj_ref, stage_ref, rows_ref, bias_ref, mix_ref, whole_ref = rest[-8:]
    ready()
    nodes, width = own_ref.shape
    table = proj_ref.shape[0]
    size = width // heads
    count_ref = known_ref.at[:, :table]
    power_ref = known_ref.at[:, table : 2 * table]
    pick_ref = known_ref.at[:, 2 * table + size : 2 * table + size + slots]
    vectors = known_ref[: 6 * heads, 2 * table : 2 * table + size]
    diag_src = block_diagonal(vectors[: 3 * heads], heads)
    diag_dst = block_diagonal(vectors[3 * heads :], heads)
    rows_ref[:nodes, :] = own_ref[...]
    rows_ref[nodes:, :] = got_ref[...]
    proj_ref[...] = shard_dots(rows_ref, shards, whole_ref).astype(BF16)
    parts = dot(diag_src, proj_ref[...], ((1,), (1,)))
    src = parts[:heads] + parts[heads : 2 * heads] + parts[2 * heads : 3 * heads]
    src = src.astype(BF16).astype(F32) * LOG2_E
    parts = dot(proj_ref[:nodes, :], diag_dst, ((1,), (1,)))
    dst = parts[:, :heads] + parts[:, heads : 2 * heads] + parts[:, 2 * heads : 3 * heads]
    dst = dst * LOG2_E
    first_lane = (lax.broadcasted_iota(jnp.int32, (16, 128), 1) == 0).astype(F32).astype(BF16)
    mark = dot(first_lane, rows_ref[nodes:, :128], ((1,), (1,)))[:1]
    hide = jnp.where(mark < DEAD / 2, 0.0, -jnp.inf)
    hide = jnp.concatenate([jnp.zeros((1, nodes), F32), hide], axis=1)
    bias_ref[...] = jnp.where(count_ref[...] > 0, hide, -jnp.inf)
    chunk = 32
    for h in range(heads):
        for r in range(0, nodes, chunk):
            here = slice(r, r + chunk)
            logit = dst[here, h : h + 1] + src[h : h + 1, :]
            logit = jnp.maximum(logit, 0.2 * logit) + bias_ref[here, :]
            terms = jnp.exp2(logit - jnp.max(logit, axis=1, keepdims=True))
            count = count_ref[here, :]
            power = power_ref[here, :]
            running = jnp.sum(count.astype(F32) * terms, axis=1, keepdims=True)
            weight = (terms * (1.0 / running)).astype(BF16)
            mix_ref[h % 2, here, :] = weight * power
            mix_ref[h % 2, nodes + r : nodes + r + chunk, :] = weight * (count - power)
        both = dot(mix_ref[h % 2], proj_ref[:, h * size : (h + 1) * size])
        total = both[:nodes] + both[nodes:]
        total = jnp.where(total > 0, total, jnp.exp(jnp.minimum(total, 0.0)) - 1.0)
        out_ref[:, h * size : (h + 1) * size] = total.astype(BF16)
    pack_rows(dot(pick_ref[...], out_ref[...], ((0,), (0,))), stage_ref, send_ref)


def pack_rows(rows, stage_ref, out_ref):
    slots, width = rows.shape
    pieces = width // 128
    for c in range(pieces):
        stage_ref[pl.ds(c, slots, stride=pieces), :] = rows[:, c * 128 : (c + 1) * 128]
    out_ref[...] = stage_ref[...].astype(BF16)


def unpack_rows(ref, stage_ref, pieces):
    stage_ref[...] = ref[...].astype(F32)
    slots = ref.shape[0] // pieces
    parts = [stage_ref[pl.ds(c, slots, stride=pieces), :] for c in range(pieces)]
    return jnp.concatenate(parts, axis=1).astype(BF16)


def add_shards(rows_ref, shards, part_ref):
    depth = shards[0].shape[0]
    span = rows_ref.shape[1]
    for i, shard in enumerate(shards):
        row = shard_row(i, shards)
        cols = pl.ds(pl.multiple_of(row % span, depth), depth)
        part_ref[row // span] += dot(rows_ref[:, cols], shard[...])


def score_kernel(cands, ready, got_ref, known_ref, *rest):
    shards = rest[:-7]
    scores_ref, back_ref, stage_ref, sum_ref, grad_ref, part_ref, rows_ref = rest[-7:]
    ready()
    depth, hidden = shards[0].shape
    slots, width = grad_ref.shape[1:]
    picks = [known_ref[:slots, i * cands : (i + 1) * cands] for i in range(2)]
    known = known_ref[slots : slots + 16, :cands].astype(F32).T
    live, label = known[:, :1], known[:, 1:2]
    out_w = known_ref[slots + 16 :, :hidden].astype(F32)
    out_w = out_w[:1] + out_w[1:2] + out_w[2:3]
    rows = unpack_rows(got_ref, stage_ref, width // 128)
    if slots > cands:
        for i in range(2):
            pair = dot(picks[i], rows, ((0,), (0,)))
            rows_ref[:, i * width : (i + 1) * width] = pair.astype(BF16)
    else:
        rows_ref[...] = rows
    part_ref[...] = jnp.zeros_like(part_ref)
    add_shards(rows_ref, shards, part_ref)
    if slots > cands:
        pre_act = part_ref[0]
    else:
        pre_act = None
        for i in range(2):
            rest = part_ref[i]
            for _ in range(3):
                high = rest.astype(BF16)
                rest = rest - high.astype(F32)
                term = dot(picks[i], high, ((0,), (0,)))
                pre_act = term if pre_act is None else pre_act + term
    gate = jax.nn.sigmoid(pre_act)
    score = jnp.sum(pre_act * gate * out_w, axis=1, keepdims=True) * live
    scores_ref[...] = jnp.broadcast_to(score, (cands, 128)).T[:1]
    grad_score = (jax.nn.sigmoid(score) - label) * live
    grad_pre = (grad_score * out_w * (gate * (1.0 + pre_act * (1.0 - gate)))).astype(BF16)
    for i in range(2):
        total = dot(picks[i], grad_pre)
        high = total.astype(BF16)
        sum_ref[i, :slots, :] = high
        sum_ref[i, slots:, :] = (total - high.astype(F32)).astype(BF16)
    for i, shard in enumerate(shards):
        row = shard_row(i, shards)
        half = row // width
        col = pl.multiple_of(row % width, depth)
        both = dot(sum_ref[half], shard[...], ((1,), (1,)))
        grad_ref[half, :, pl.ds(col, depth)] = both[:slots] + both[slots:]
    pack_rows(grad_ref[0] + grad_ref[1], stage_ref, back_ref)


def scatter_kernel(ready, pick_ref, got_ref, out_ref, stage_ref):
    ready()
    rows = unpack_rows(got_ref, stage_ref, out_ref.shape[1] // 128)
    out_ref[...] = dot(pick_ref[...], rows)


def swap(array, axis, k):
    count = lax.axis_size(axis)
    return lax.ppermute(array, axis, [(i, i ^ k) for i in range(count)])


def across(shard, edge_count):
    return [shard] + [swap(shard, "edge", 2 * k) for k in range(1, edge_count // 2)]


def from_core(shards):
    return [one for shard in shards for one in (shard, swap(shard, "edge", 1))]


def local(
    node_feats,
    gat_weight,
    attn_src,
    attn_dst,
    neighbours,
    degree,
    halo_rows,
    halo_count,
    endpoint_rows,
    cand_ends,
    cand_count,
    labels,
    mlp_weight,
    out_weight,
):
    nodes, width = node_feats.shape
    dom_count = lax.axis_size("dom")
    edge_count = lax.axis_size("edge")
    block = halo_rows.shape[-1]
    cands = labels.shape[-1]
    hidden = out_weight.shape[0]
    halo = dom_count * block
    table = nodes + halo
    slots = dom_count * edge_count * endpoint_rows.shape[-1]
    pieces = width // 128
    everyone = ("dom", "edge")
    shape = jax.ShapeDtypeStruct

    heads = attn_src.shape[0]
    send_rows = call(
        halo_kernel,
        shape((halo, width), BF16),
        [("f", halo_count[0]), ("f", halo_rows[0, 0]), ("f", node_feats)],
        vmem_mib=60,
    )
    got_rows = lax.all_to_all(send_rows, "dom", split_axis=0, concat_axis=0, tiled=True)
    gat_across = across(gat_weight, edge_count)
    held_mlp = lax.optimization_barrier((mlp_weight, send_rows))[0]
    parts = 2 if mlp_weight.shape[0] % 256 == 0 else 1
    lanes = -(-(2 * table + attn_src.shape[1] + slots) // 128) * 128
    for_attend, for_score, pick, *mlp_parts = call(
        functools.partial(prepare_kernel, table),
        (
            shape((nodes, lanes), BF16),
            shape((slots + 32, max(2 * cands, hidden)), BF16),
            shape((nodes, slots), BF16),
        )
        + (shape((mlp_weight.shape[0] // parts, hidden), BF16),) * parts,
        [
            ("s", cand_count),
            ("f", neighbours.T),
            ("f", degree.reshape(1, nodes)),
            ("f", attn_src),
            ("f", attn_dst),
            ("f", endpoint_rows.reshape(1, slots)),
            ("f", cand_ends[0, 0]),
            ("f", labels[0]),
            ("f", out_weight.reshape(1, hidden)),
            ("f", held_mlp),
        ],
        vmem_mib=60,
    )
    gat_across = lax.optimization_barrier((*gat_across, for_attend))[:-1]
    gat_shards = from_core(gat_across)
    mlp_across = [across(part, edge_count) for part in mlp_parts]
    if parts > 1:
        got_rows, *mlp_across[0] = lax.optimization_barrier((got_rows, *mlp_across[0]))
    packed = pltpu.VMEM((slots * pieces, 128), F32)
    node_out, send_ends = call(
        functools.partial(attend_kernel, edge_count, heads, slots),
        (shape((nodes, width), BF16), shape((slots * pieces, 128), BF16)),
        [("v", node_feats), ("v", got_rows), ("v", for_attend)] + [("v", w) for w in gat_shards],
        [
            pltpu.VMEM((table, width), BF16),
            packed,
            pltpu.VMEM((table, width), BF16),
            pltpu.VMEM((nodes, table), F32),
            pltpu.VMEM((2, 2 * nodes, table), BF16),
            pltpu.VMEM((width if width // edge_count % 128 else 16, width), BF16),
        ],
    )
    mlp_across[-1] = lax.optimization_barrier((*mlp_across[-1], send_ends))[:-1]
    mlp_found = [from_core(part) for part in mlp_across]
    mlp_shards = [found[e] for e in range(edge_count) for found in mlp_found]
    got_ends = lax.all_to_all(send_ends, everyone, split_axis=0, concat_axis=0, tiled=True)
    many = slots > cands
    scores, send_back = call(
        functools.partial(score_kernel, cands),
        (shape((1, cands), F32), shape((slots * pieces, 128), BF16)),
        [("v", got_ends), ("v", for_score)] + [("v", w) for w in mlp_shards],
        [
            packed,
            pltpu.VMEM((2, 2 * slots, hidden), BF16),
            pltpu.VMEM((2, slots, width), F32),
            pltpu.VMEM((1, cands, hidden) if many else (2, slots, hidden), F32),
            pltpu.VMEM((cands, 2 * width) if many else (slots, width), BF16),
        ],
    )
    got_back = lax.all_to_all(send_back, everyone, split_axis=0, concat_axis=0, tiled=True)
    node_grad = call(
        scatter_kernel, shape((nodes, width), F32), [("v", pick), ("v", got_back)], [packed]
    )
    return (node_out, scores.reshape(1, 1, cands), node_grad)


def solution(mesh):
    in_specs = (
        P(("dom", "edge"), None),
        P("edge", None),
        P(),
        P(),
        P(("dom", "edge"), None),
        P(("dom", "edge")),
        P("dom", "edge", None, None),
        P("dom", "edge", None),
        P("dom", "edge", None, None, None),
        P("dom", "edge", None, None),
        P("dom", "edge"),
        P("dom", "edge", None),
        P("edge", None),
        P(),
    )
    out_specs = (P(("dom", "edge"), None), P("dom", "edge", None), P(("dom", "edge"), None))
    return jax.shard_map(local, mesh=mesh, in_specs=in_specs, out_specs=out_specs, check_vma=False)
```

```python
import functools

import jax
import jax.numpy as jnp
from jax import lax
from jax.experimental import pallas as pl
from jax.experimental.pallas import tpu as pltpu
from jax.sharding import PartitionSpec as P

F32 = jnp.float32
BF16 = jnp.bfloat16
LOG2_E = 1.4426950408889634
DEAD = 64.0
VMEM = pl.BlockSpec(memory_space=pltpu.VMEM)
SPACES = {
    "v": VMEM,
    "s": pl.BlockSpec(memory_space=pltpu.SMEM),
    "f": pl.BlockSpec(memory_space=pl.ANY),
    "any": pl.BlockSpec(memory_space=pl.ANY),
}


def dot(a, b, dims=((1,), (0,))):
    return lax.dot_general(a, b, (dims, ((), ())), preferred_element_type=F32)


def call(kernel, outs, ins, scratch=(), vmem_mib=20, out_space=None):
    out_space = out_space or jax.tree.map(lambda _: "v", outs)
    fetched = [i for i, (space, _) in enumerate(ins) if space == "f"]

    def body(*refs):
        refs = list(refs)
        local_count = len(fetched) + 1
        own, (held, sems) = refs[:-local_count], (refs[-local_count:-1], refs[-1])
        copies = []
        for n, i in enumerate(fetched):
            copies.append(pltpu.make_async_copy(own[i], held[n], sems.at[n]))
            copies[-1].start()
            own[i] = held[n]

        def ready():
            for copy in copies:
                copy.wait()

        kernel(ready, *own)

    return pl.pallas_call(
        body,
        out_shape=outs,
        in_specs=[SPACES[space] for space, _ in ins],
        out_specs=jax.tree.map(lambda space: SPACES[space], out_space),
        scratch_shapes=list(scratch)
        + [pltpu.VMEM(ins[i][1].shape, ins[i][1].dtype) for i in fetched]
        + [pltpu.SemaphoreType.DMA((max(1, len(fetched)),))],
        compiler_params=pltpu.CompilerParams(vmem_limit_bytes=vmem_mib * 1024 * 1024),
    )(*[array for _, array in ins])


def halo_kernel(ready, count_ref, rows_ref, feats_ref, mlp_ref, out_ref, held_ref, sem):
    hold = pltpu.make_async_copy(mlp_ref, held_ref, sem)
    hold.start()
    doms, block = rows_ref.shape
    at = lax.broadcasted_iota(jnp.int32, (1, block), 1)
    ready()
    pieces = [
        jnp.where(at < count_ref[:, s : s + 1], rows_ref[s : s + 1, :], -1) for s in range(doms)
    ]
    flat = jnp.concatenate(pieces, axis=1)
    total = doms * block
    nodes = feats_ref.shape[0]
    pick = (lax.broadcasted_iota(jnp.int32, (nodes, total), 0) == flat).astype(F32).astype(BF16)
    rows = dot(pick, feats_ref[...], ((0,), (0,)))
    first = lax.broadcasted_iota(jnp.int32, (16, total), 0) == 0
    dead = jnp.where(first & (flat < 0), 1.0, 0.0).astype(BF16)
    mark_at = (lax.broadcasted_iota(jnp.int32, (16, 128), 0) == 0) & (
        lax.broadcasted_iota(jnp.int32, (16, 128), 1) == 0
    )
    mark = jnp.where(mark_at, DEAD, 0.0).astype(BF16)
    out_ref[:, :128] = (rows[:, :128] + dot(dead, mark, ((0,), (0,)))).astype(BF16)
    out_ref[:, 128:] = rows[:, 128:].astype(BF16)
    hold.wait()


def three_parts(values):
    high = values.astype(BF16).astype(F32)
    middle = (values - high).astype(BF16).astype(F32)
    return jnp.concatenate([high, middle, values - high - middle], axis=0)


def block_diagonal(parts, heads):
    parts = parts.astype(F32)
    wide = jnp.concatenate([parts] * heads, axis=1)
    lane_head = lax.broadcasted_iota(jnp.int32, wide.shape, 1) // parts.shape[1]
    row_head = lax.broadcasted_iota(jnp.int32, wide.shape, 0) % heads
    wide = jnp.where(lane_head == row_head, wide, 0.0)
    return jnp.concatenate([wide, jnp.zeros((heads, wide.shape[1]), F32)], axis=0).astype(BF16)


def prepare_kernel(
    table,
    ready,
    live_ref,
    neigh_ref,
    degree_ref,
    src_ref,
    dst_ref,
    ends_ref,
    cand_ref,
    labels_ref,
    out_w_ref,
    for_attend_ref,
    for_score_ref,
    pick_ref,
):
    ready()
    nodes, ends = pick_ref.shape
    heads, size = src_ref.shape
    slots = neigh_ref.shape[0]
    ids = neigh_ref[...]
    ids = jnp.where(lax.broadcasted_iota(jnp.int32, ids.shape, 0) < degree_ref[...], ids, -1)
    for base in range(0, table, nodes):
        at = base + lax.broadcasted_iota(jnp.int32, (nodes, nodes), 0)
        total = jnp.zeros((nodes, nodes), F32)
        if base == 0:
            total = (at == lax.broadcasted_iota(jnp.int32, (nodes, nodes), 1)).astype(F32)
        for j in range(slots):
            total = total + (at == ids[j : j + 1, :]).astype(F32)
        total = total.T
        power = jnp.where(total > 1, 2.0, total)
        power = jnp.where(total > 2, 4.0, power)
        power = jnp.where(total > 5, 8.0, power)
        power = jnp.where(total > 13, 16.0, power)
        for_attend_ref[:, base : base + nodes] = total.astype(BF16)
        for_attend_ref[:, table + base : table + base + nodes] = power.astype(BF16)
    node_at = lax.broadcasted_iota(jnp.int32, (nodes, ends), 0)
    pick = (node_at == ends_ref[...]).astype(F32).astype(BF16)
    pick_ref[...] = pick
    first = 2 * table + size
    for_attend_ref[:, first : first + ends] = pick
    vectors = [three_parts(src_ref[...]), three_parts(dst_ref[...])]
    for_attend_ref[: 6 * heads, 2 * table : first] = jnp.concatenate(vectors, axis=0).astype(BF16)
    cands = cand_ref.shape[1]
    hidden = out_w_ref.shape[1]
    slot_at = lax.broadcasted_iota(jnp.int32, (ends, cands), 0)
    for i in range(2):
        one_hot = (slot_at == cand_ref[i : i + 1, :]).astype(F32).astype(BF16)
        for_score_ref[:ends, i * cands : (i + 1) * cands] = one_hot
    live = (lax.broadcasted_iota(jnp.int32, (1, cands), 1) < live_ref[0, 0]).astype(F32)
    known = jnp.concatenate([live, labels_ref[...].astype(F32), jnp.zeros((14, cands), F32)], axis=0)
    for_score_ref[ends : ends + 16, :cands] = known.astype(BF16)
    whole = jnp.concatenate([three_parts(out_w_ref[...]), jnp.zeros((13, hidden), F32)], axis=0)
    for_score_ref[ends + 16 :, :hidden] = whole.astype(BF16)


def shard_row(i, depth):
    return pl.multiple_of((lax.axis_index("edge") ^ i) * depth, depth)


def shard_dots(rows_ref, shards, whole_ref=None):
    depth = shards[0].shape[0]
    if depth % 128:
        for i, shard in enumerate(shards):
            whole_ref[pl.ds(shard_row(i, depth), depth), :] = shard[...]
        return dot(rows_ref[...], whole_ref[...])
    total = None
    for i, shard in enumerate(shards):
        cols = pl.ds(shard_row(i, depth), depth)
        part = dot(rows_ref[:, cols], shard[...])
        total = part if total is None else total + part
    return total


def attend_kernel(shard_count, heads, slots, ready, own_ref, got_ref, known_ref, *rest):
    shards = rest[:shard_count]
    out_ref, send_ref, proj_ref, stage_ref, rows_ref, bias_ref, mix_ref, whole_ref = rest[-8:]
    ready()
    nodes, width = own_ref.shape
    table = proj_ref.shape[0]
    size = width // heads
    count_ref = known_ref.at[:, :table]
    power_ref = known_ref.at[:, table : 2 * table]
    pick_ref = known_ref.at[:, 2 * table + size : 2 * table + size + slots]
    vectors = known_ref[: 6 * heads, 2 * table : 2 * table + size]
    diag_src = block_diagonal(vectors[: 3 * heads], heads)
    diag_dst = block_diagonal(vectors[3 * heads :], heads)
    rows_ref[:nodes, :] = own_ref[...]
    rows_ref[nodes:, :] = got_ref[...]
    proj_ref[...] = shard_dots(rows_ref, shards, whole_ref).astype(BF16)
    parts = dot(diag_src, proj_ref[...], ((1,), (1,)))
    src = parts[:heads] + parts[heads : 2 * heads] + parts[2 * heads : 3 * heads]
    src = src.astype(BF16).astype(F32) * LOG2_E
    parts = dot(proj_ref[:nodes, :], diag_dst, ((1,), (1,)))
    dst = parts[:, :heads] + parts[:, heads : 2 * heads] + parts[:, 2 * heads : 3 * heads]
    dst = dst * LOG2_E
    first_lane = (lax.broadcasted_iota(jnp.int32, (16, 128), 1) == 0).astype(F32).astype(BF16)
    mark = dot(first_lane, rows_ref[nodes:, :128], ((1,), (1,)))[:1]
    hide = jnp.where(mark < DEAD / 2, 0.0, -jnp.inf)
    hide = jnp.concatenate([jnp.zeros((1, nodes), F32), hide], axis=1)
    bias_ref[...] = jnp.where(count_ref[...] > 0, hide, -jnp.inf)
    chunk = 32
    for h in range(heads):
        for r in range(0, nodes, chunk):
            here = slice(r, r + chunk)
            logit = dst[here, h : h + 1] + src[h : h + 1, :]
            logit = jnp.maximum(logit, 0.2 * logit) + bias_ref[here, :]
            terms = jnp.exp2(logit - jnp.max(logit, axis=1, keepdims=True))
            count = count_ref[here, :]
            power = power_ref[here, :]
            running = jnp.sum(count.astype(F32) * terms, axis=1, keepdims=True)
            weight = (terms * (1.0 / running)).astype(BF16)
            mix_ref[h % 2, here, :] = weight * power
            mix_ref[h % 2, nodes + r : nodes + r + chunk, :] = weight * (count - power)
        both = dot(mix_ref[h % 2], proj_ref[:, h * size : (h + 1) * size])
        total = both[:nodes] + both[nodes:]
        total = jnp.where(total > 0, total, jnp.exp(jnp.minimum(total, 0.0)) - 1.0)
        out_ref[:, h * size : (h + 1) * size] = total.astype(BF16)
    pack_rows(dot(pick_ref[...], out_ref[...], ((0,), (0,))), stage_ref, send_ref)


def pack_rows(rows, stage_ref, out_ref):
    slots, width = rows.shape
    pieces = width // 128
    for c in range(pieces):
        stage_ref[pl.ds(c, slots, stride=pieces), :] = rows[:, c * 128 : (c + 1) * 128]
    out_ref[...] = stage_ref[...].astype(BF16)


def unpack_rows(ref, stage_ref, pieces):
    stage_ref[...] = ref[...].astype(F32)
    slots = ref.shape[0] // pieces
    parts = [stage_ref[pl.ds(c, slots, stride=pieces), :] for c in range(pieces)]
    return jnp.concatenate(parts, axis=1).astype(BF16)


def add_shards(rows_ref, indices, shards, part_ref):
    depth = shards[0].shape[0]
    span = rows_ref.shape[1]
    for i, shard in zip(indices, shards):
        row = shard_row(i, depth)
        cols = pl.ds(pl.multiple_of(row % span, depth), depth)
        part_ref[row // span] += dot(rows_ref[:, cols], shard[...])


def first_kernel(indices, cands, ready, got_ref, known_ref, *rest):
    shards = rest[:-3]
    rows_ref, part_ref, stage_ref = rest[-3:]
    ready()
    slots = known_ref.shape[0] - 32
    width = got_ref.shape[0] * 128 // slots
    rows = unpack_rows(got_ref, stage_ref, width // 128)
    if slots > cands:
        for i in range(2):
            pick = known_ref[:slots, i * cands : (i + 1) * cands]
            pair = dot(pick, rows, ((0,), (0,)))
            rows_ref[:, i * width : (i + 1) * width] = pair.astype(BF16)
    else:
        rows_ref[...] = rows
    part_ref[...] = jnp.zeros_like(part_ref)
    add_shards(rows_ref, indices, shards, part_ref)


def score_kernel(late, cands, ready, rows_ref, first_ref, known_ref, *rest):
    shards = rest[:-6]
    scores_ref, back_ref, stage_ref, sum_ref, grad_ref, part_ref = rest[-6:]
    ready()
    depth, hidden = shards[0].shape
    slots, width = grad_ref.shape[1:]
    picks = [known_ref[:slots, i * cands : (i + 1) * cands] for i in range(2)]
    known = known_ref[slots : slots + 16, :cands].astype(F32).T
    live, label = known[:, :1], known[:, 1:2]
    out_w = known_ref[slots + 16 :, :hidden].astype(F32)
    out_w = out_w[:1] + out_w[1:2] + out_w[2:3]
    part_ref[...] = first_ref[...]
    add_shards(rows_ref, late, [shards[i] for i in late], part_ref)
    if slots > cands:
        pre_act = part_ref[0]
    else:
        pre_act = None
        for i in range(2):
            rest = part_ref[i]
            for _ in range(3):
                high = rest.astype(BF16)
                rest = rest - high.astype(F32)
                term = dot(picks[i], high, ((0,), (0,)))
                pre_act = term if pre_act is None else pre_act + term
    gate = jax.nn.sigmoid(pre_act)
    score = jnp.sum(pre_act * gate * out_w, axis=1, keepdims=True) * live
    scores_ref[...] = jnp.broadcast_to(score, (cands, 128)).T[:1]
    grad_score = (jax.nn.sigmoid(score) - label) * live
    grad_pre = (grad_score * out_w * (gate * (1.0 + pre_act * (1.0 - gate)))).astype(BF16)
    for i in range(2):
        total = dot(picks[i], grad_pre)
        high = total.astype(BF16)
        sum_ref[i, :slots, :] = high
        sum_ref[i, slots:, :] = (total - high.astype(F32)).astype(BF16)
    for i, shard in enumerate(shards):
        row = shard_row(i, depth)
        half = row // width
        col = pl.multiple_of(row % width, depth)
        both = dot(sum_ref[half], shard[...], ((1,), (1,)))
        grad_ref[half, :, pl.ds(col, depth)] = both[:slots] + both[slots:]
    pack_rows(grad_ref[0] + grad_ref[1], stage_ref, back_ref)


def scatter_kernel(ready, pick_ref, got_ref, out_ref, stage_ref):
    ready()
    rows = unpack_rows(got_ref, stage_ref, out_ref.shape[1] // 128)
    out_ref[...] = dot(pick_ref[...], rows)


def swap(array, axis, k):
    count = lax.axis_size(axis)
    return lax.ppermute(array, axis, [(i, i ^ k) for i in range(count)])


def across(shard, edge_count):
    return [shard] + [swap(shard, "edge", 2 * k) for k in range(1, edge_count // 2)]


def from_core(shards):
    return [one for shard in shards for one in (shard, swap(shard, "edge", 1))]


def local(
    node_feats,
    gat_weight,
    attn_src,
    attn_dst,
    neighbours,
    degree,
    halo_rows,
    halo_count,
    endpoint_rows,
    cand_ends,
    cand_count,
    labels,
    mlp_weight,
    out_weight,
):
    nodes, width = node_feats.shape
    dom_count = lax.axis_size("dom")
    edge_count = lax.axis_size("edge")
    block = halo_rows.shape[-1]
    cands = labels.shape[-1]
    hidden = out_weight.shape[0]
    halo = dom_count * block
    table = nodes + halo
    slots = dom_count * edge_count * endpoint_rows.shape[-1]
    pieces = width // 128
    everyone = ("dom", "edge")
    shape = jax.ShapeDtypeStruct

    heads = attn_src.shape[0]
    send_rows, held_mlp = call(
        halo_kernel,
        (shape((halo, width), BF16), shape(mlp_weight.shape, BF16)),
        [
            ("f", halo_count[0]),
            ("f", halo_rows[0, 0]),
            ("f", node_feats),
            ("any", mlp_weight),
        ],
        [pltpu.SemaphoreType.DMA],
        vmem_mib=60,
        out_space=("v", "any"),
    )
    got_rows = lax.all_to_all(send_rows, "dom", split_axis=0, concat_axis=0, tiled=True)
    gat_across = across(gat_weight, edge_count)
    mlp_across = across(held_mlp, edge_count)
    lanes = -(-(2 * table + attn_src.shape[1] + slots) // 128) * 128
    for_attend, for_score, pick = call(
        functools.partial(prepare_kernel, table),
        (
            shape((nodes, lanes), BF16),
            shape((slots + 32, max(2 * cands, hidden)), BF16),
            shape((nodes, slots), BF16),
        ),
        [
            ("s", cand_count),
            ("f", neighbours.T),
            ("f", degree.reshape(1, nodes)),
            ("f", attn_src),
            ("f", attn_dst),
            ("f", endpoint_rows.reshape(1, slots)),
            ("f", cand_ends[0, 0]),
            ("f", labels[0]),
            ("f", out_weight.reshape(1, hidden)),
        ],
    )
    gat_across = lax.optimization_barrier((*gat_across, for_attend))[:-1]
    gat_shards = from_core(gat_across)
    packed = pltpu.VMEM((slots * pieces, 128), F32)
    node_out, send_ends = call(
        functools.partial(attend_kernel, edge_count, heads, slots),
        (shape((nodes, width), BF16), shape((slots * pieces, 128), BF16)),
        [("v", node_feats), ("v", got_rows), ("v", for_attend)] + [("v", w) for w in gat_shards],
        [
            pltpu.VMEM((table, width), BF16),
            packed,
            pltpu.VMEM((table, width), BF16),
            pltpu.VMEM((nodes, table), F32),
            pltpu.VMEM((2, 2 * nodes, table), BF16),
            pltpu.VMEM((width if width // edge_count % 128 else 16, width), BF16),
        ],
    )
    got_ends = lax.all_to_all(send_ends, everyone, split_axis=0, concat_axis=0, tiled=True)
    mlp_shards = [mlp_weight, swap(held_mlp, "edge", 1)]
    tied = lax.optimization_barrier((*mlp_across[1:], send_ends))[:-1]
    for shard, held in zip(mlp_across[1:], tied):
        mlp_shards += [shard, swap(held, "edge", 1)]
    early = [i for i in range(edge_count) if i < 2 or i % 2 == 0]
    late = [i for i in range(edge_count) if i not in early]
    many = slots > cands
    rows, part = call(
        functools.partial(first_kernel, early, cands),
        (
            shape((cands, 2 * width) if many else (slots, width), BF16),
            shape((1, cands, hidden) if many else (2, slots, hidden), F32),
        ),
        [("v", got_ends), ("v", for_score)] + [("v", mlp_shards[i]) for i in early],
        [packed],
    )
    scores, send_back = call(
        functools.partial(score_kernel, late, cands),
        (shape((1, cands), F32), shape((slots * pieces, 128), BF16)),
        [("v", rows), ("v", part), ("v", for_score)] + [("v", w) for w in mlp_shards],
        [
            packed,
            pltpu.VMEM((2, 2 * slots, hidden), BF16),
            pltpu.VMEM((2, slots, width), F32),
            pltpu.VMEM(part.shape, F32),
        ],
    )
    got_back = lax.all_to_all(send_back, everyone, split_axis=0, concat_axis=0, tiled=True)
    node_grad = call(
        scatter_kernel, shape((nodes, width), F32), [("v", pick), ("v", got_back)], [packed]
    )
    return (node_out, scores.reshape(1, 1, cands), node_grad)


def solution(mesh):
    in_specs = (
        P(("dom", "edge"), None),
        P("edge", None),
        P(),
        P(),
        P(("dom", "edge"), None),
        P(("dom", "edge")),
        P("dom", "edge", None, None),
        P("dom", "edge", None),
        P("dom", "edge", None, None, None),
        P("dom", "edge", None, None),
        P("dom", "edge"),
        P("dom", "edge", None),
        P("edge", None),
        P(),
    )
    out_specs = (P(("dom", "edge"), None), P("dom", "edge", None), P(("dom", "edge"), None))
    return jax.shard_map(local, mesh=mesh, in_specs=in_specs, out_specs=out_specs, check_vma=False)
```

```python
import functools

import jax
import jax.numpy as jnp
from jax import lax
from jax.experimental import pallas as pl
from jax.experimental.pallas import tpu as pltpu
from jax.sharding import PartitionSpec as P

F32 = jnp.float32
BF16 = jnp.bfloat16
LOG2_E = 1.4426950408889634
DEAD = 64.0
VMEM = pl.BlockSpec(memory_space=pltpu.VMEM)
SPACES = {
    "v": VMEM,
    "s": pl.BlockSpec(memory_space=pltpu.SMEM),
    "f": pl.BlockSpec(memory_space=pl.ANY),
    "any": pl.BlockSpec(memory_space=pl.ANY),
}


def dot(a, b, dims=((1,), (0,))):
    return lax.dot_general(a, b, (dims, ((), ())), preferred_element_type=F32)


def call(kernel, outs, ins, scratch=(), vmem_mib=20, out_space="v", cost=None):
    fetched = [i for i, (space, _) in enumerate(ins) if space == "f"]

    def body(*refs):
        refs = list(refs)
        local_count = len(fetched) + 1
        own, (held, sems) = refs[:-local_count], (refs[-local_count:-1], refs[-1])
        copies = []
        for n, i in enumerate(fetched):
            copies.append(pltpu.make_async_copy(own[i], held[n], sems.at[n]))
            copies[-1].start()
            own[i] = held[n]

        def ready():
            for copy in copies:
                copy.wait()

        kernel(ready, *own)

    return pl.pallas_call(
        body,
        out_shape=outs,
        in_specs=[SPACES[space] for space, _ in ins],
        out_specs=jax.tree.map(lambda _: SPACES[out_space], outs),
        scratch_shapes=list(scratch)
        + [pltpu.VMEM(ins[i][1].shape, ins[i][1].dtype) for i in fetched]
        + [pltpu.SemaphoreType.DMA((max(1, len(fetched)),))],
        cost_estimate=cost,
        compiler_params=pltpu.CompilerParams(vmem_limit_bytes=vmem_mib * 1024 * 1024),
    )(*[array for _, array in ins])


def halo_kernel(ready, count_ref, rows_ref, feats_ref, out_ref):
    doms, block = rows_ref.shape
    at = lax.broadcasted_iota(jnp.int32, (1, block), 1)
    ready()
    pieces = [
        jnp.where(at < count_ref[:, s : s + 1], rows_ref[s : s + 1, :], -1) for s in range(doms)
    ]
    flat = jnp.concatenate(pieces, axis=1)
    total = doms * block
    nodes = feats_ref.shape[0]
    pick = (lax.broadcasted_iota(jnp.int32, (nodes, total), 0) == flat).astype(F32).astype(BF16)
    rows = dot(pick, feats_ref[...], ((0,), (0,)))
    first = lax.broadcasted_iota(jnp.int32, (16, total), 0) == 0
    dead = jnp.where(first & (flat < 0), 1.0, 0.0).astype(BF16)
    mark_at = (lax.broadcasted_iota(jnp.int32, (16, 128), 0) == 0) & (
        lax.broadcasted_iota(jnp.int32, (16, 128), 1) == 0
    )
    mark = jnp.where(mark_at, DEAD, 0.0).astype(BF16)
    out_ref[:, :128] = (rows[:, :128] + dot(dead, mark, ((0,), (0,)))).astype(BF16)
    out_ref[:, 128:] = rows[:, 128:].astype(BF16)


def three_parts(values):
    high = values.astype(BF16).astype(F32)
    middle = (values - high).astype(BF16).astype(F32)
    return jnp.concatenate([high, middle, values - high - middle], axis=0)


def block_diagonal(parts, heads):
    parts = parts.astype(F32)
    wide = jnp.concatenate([parts] * heads, axis=1)
    lane_head = lax.broadcasted_iota(jnp.int32, wide.shape, 1) // parts.shape[1]
    row_head = lax.broadcasted_iota(jnp.int32, wide.shape, 0) % heads
    wide = jnp.where(lane_head == row_head, wide, 0.0)
    return jnp.concatenate([wide, jnp.zeros((heads, wide.shape[1]), F32)], axis=0).astype(BF16)


def prepare_kernel(
    table,
    ready,
    live_ref,
    neigh_ref,
    degree_ref,
    src_ref,
    dst_ref,
    ends_ref,
    cand_ref,
    labels_ref,
    out_w_ref,
    for_attend_ref,
    for_score_ref,
    pick_ref,
):
    ready()
    nodes, ends = pick_ref.shape
    heads, size = src_ref.shape
    slots = neigh_ref.shape[0]
    ids = neigh_ref[...]
    ids = jnp.where(lax.broadcasted_iota(jnp.int32, ids.shape, 0) < degree_ref[...], ids, -1)
    for base in range(0, table, nodes):
        at = base + lax.broadcasted_iota(jnp.int32, (nodes, nodes), 0)
        total = jnp.zeros((nodes, nodes), F32)
        if base == 0:
            total = (at == lax.broadcasted_iota(jnp.int32, (nodes, nodes), 1)).astype(F32)
        for j in range(slots):
            total = total + (at == ids[j : j + 1, :]).astype(F32)
        total = total.T
        power = jnp.where(total > 1, 2.0, total)
        power = jnp.where(total > 2, 4.0, power)
        power = jnp.where(total > 5, 8.0, power)
        power = jnp.where(total > 13, 16.0, power)
        for_attend_ref[:, base : base + nodes] = total.astype(BF16)
        for_attend_ref[:, table + base : table + base + nodes] = power.astype(BF16)
    node_at = lax.broadcasted_iota(jnp.int32, (nodes, ends), 0)
    pick = (node_at == ends_ref[...]).astype(F32).astype(BF16)
    pick_ref[...] = pick
    first = 2 * table + size
    for_attend_ref[:, first : first + ends] = pick
    vectors = [three_parts(src_ref[...]), three_parts(dst_ref[...])]
    for_attend_ref[: 6 * heads, 2 * table : first] = jnp.concatenate(vectors, axis=0).astype(BF16)
    cands = cand_ref.shape[1]
    hidden = out_w_ref.shape[1]
    slot_at = lax.broadcasted_iota(jnp.int32, (ends, cands), 0)
    for i in range(2):
        one_hot = (slot_at == cand_ref[i : i + 1, :]).astype(F32).astype(BF16)
        for_score_ref[:ends, i * cands : (i + 1) * cands] = one_hot
    live = (lax.broadcasted_iota(jnp.int32, (1, cands), 1) < live_ref[0, 0]).astype(F32)
    known = jnp.concatenate([live, labels_ref[...].astype(F32), jnp.zeros((14, cands), F32)], axis=0)
    for_score_ref[ends : ends + 16, :cands] = known.astype(BF16)
    whole = jnp.concatenate([three_parts(out_w_ref[...]), jnp.zeros((13, hidden), F32)], axis=0)
    for_score_ref[ends + 16 :, :hidden] = whole.astype(BF16)


def shard_row(i, depth):
    return pl.multiple_of((lax.axis_index("edge") ^ i) * depth, depth)


def shard_dots(rows_ref, shards, whole_ref=None):
    depth = shards[0].shape[0]
    if depth % 128:
        for i, shard in enumerate(shards):
            whole_ref[pl.ds(shard_row(i, depth), depth), :] = shard[...]
        return dot(rows_ref[...], whole_ref[...])
    total = None
    for i, shard in enumerate(shards):
        cols = pl.ds(shard_row(i, depth), depth)
        part = dot(rows_ref[:, cols], shard[...])
        total = part if total is None else total + part
    return total


def attend_kernel(shard_count, heads, slots, ready, own_ref, got_ref, known_ref, *rest):
    shards = rest[:shard_count]
    out_ref, send_ref, proj_ref, stage_ref, rows_ref, bias_ref, mix_ref, whole_ref = rest[-8:]
    ready()
    nodes, width = own_ref.shape
    table = proj_ref.shape[0]
    size = width // heads
    count_ref = known_ref.at[:, :table]
    power_ref = known_ref.at[:, table : 2 * table]
    pick_ref = known_ref.at[:, 2 * table + size : 2 * table + size + slots]
    vectors = known_ref[: 6 * heads, 2 * table : 2 * table + size]
    diag_src = block_diagonal(vectors[: 3 * heads], heads)
    diag_dst = block_diagonal(vectors[3 * heads :], heads)
    rows_ref[:nodes, :] = own_ref[...]
    rows_ref[nodes:, :] = got_ref[...]
    proj_ref[...] = shard_dots(rows_ref, shards, whole_ref).astype(BF16)
    parts = dot(diag_src, proj_ref[...], ((1,), (1,)))
    src = parts[:heads] + parts[heads : 2 * heads] + parts[2 * heads : 3 * heads]
    src = src.astype(BF16).astype(F32) * LOG2_E
    parts = dot(proj_ref[:nodes, :], diag_dst, ((1,), (1,)))
    dst = parts[:, :heads] + parts[:, heads : 2 * heads] + parts[:, 2 * heads : 3 * heads]
    dst = dst * LOG2_E
    first_lane = (lax.broadcasted_iota(jnp.int32, (16, 128), 1) == 0).astype(F32).astype(BF16)
    mark = dot(first_lane, rows_ref[nodes:, :128], ((1,), (1,)))[:1]
    hide = jnp.where(mark < DEAD / 2, 0.0, -jnp.inf)
    hide = jnp.concatenate([jnp.zeros((1, nodes), F32), hide], axis=1)
    bias_ref[...] = jnp.where(count_ref[...] > 0, hide, -jnp.inf)
    chunk = 32
    for h in range(heads):
        for r in range(0, nodes, chunk):
            here = slice(r, r + chunk)
            logit = dst[here, h : h + 1] + src[h : h + 1, :]
            logit = jnp.maximum(logit, 0.2 * logit) + bias_ref[here, :]
            terms = jnp.exp2(logit - jnp.max(logit, axis=1, keepdims=True))
            count = count_ref[here, :]
            power = power_ref[here, :]
            running = jnp.sum(count.astype(F32) * terms, axis=1, keepdims=True)
            weight = (terms * (1.0 / running)).astype(BF16)
            mix_ref[h % 2, here, :] = weight * power
            mix_ref[h % 2, nodes + r : nodes + r + chunk, :] = weight * (count - power)
        both = dot(mix_ref[h % 2], proj_ref[:, h * size : (h + 1) * size])
        total = both[:nodes] + both[nodes:]
        total = jnp.where(total > 0, total, jnp.exp(jnp.minimum(total, 0.0)) - 1.0)
        out_ref[:, h * size : (h + 1) * size] = total.astype(BF16)
    pack_rows(dot(pick_ref[...], out_ref[...], ((0,), (0,))), stage_ref, send_ref)


def pack_rows(rows, stage_ref, out_ref):
    slots, width = rows.shape
    pieces = width // 128
    for c in range(pieces):
        stage_ref[pl.ds(c, slots, stride=pieces), :] = rows[:, c * 128 : (c + 1) * 128]
    out_ref[...] = stage_ref[...].astype(BF16)


def unpack_rows(ref, stage_ref, pieces):
    stage_ref[...] = ref[...].astype(F32)
    slots = ref.shape[0] // pieces
    parts = [stage_ref[pl.ds(c, slots, stride=pieces), :] for c in range(pieces)]
    return jnp.concatenate(parts, axis=1).astype(BF16)


def add_shards(rows_ref, indices, shards, part_ref):
    depth = shards[0].shape[0]
    span = rows_ref.shape[1]
    for i, shard in zip(indices, shards):
        row = shard_row(i, depth)
        cols = pl.ds(pl.multiple_of(row % span, depth), depth)
        part_ref[row // span] += dot(rows_ref[:, cols], shard[...])


def first_kernel(indices, cands, ready, got_ref, known_ref, *rest):
    shards = rest[:-3]
    rows_ref, part_ref, stage_ref = rest[-3:]
    ready()
    slots = known_ref.shape[0] - 32
    width = got_ref.shape[0] * 128 // slots
    rows = unpack_rows(got_ref, stage_ref, width // 128)
    if slots > cands:
        for i in range(2):
            pick = known_ref[:slots, i * cands : (i + 1) * cands]
            pair = dot(pick, rows, ((0,), (0,)))
            rows_ref[:, i * width : (i + 1) * width] = pair.astype(BF16)
    else:
        rows_ref[...] = rows
    part_ref[...] = jnp.zeros_like(part_ref)
    add_shards(rows_ref, indices, shards, part_ref)


def score_kernel(late, cands, ready, rows_ref, first_ref, known_ref, *rest):
    shards = rest[:-6]
    scores_ref, back_ref, stage_ref, sum_ref, grad_ref, part_ref = rest[-6:]
    ready()
    depth, hidden = shards[0].shape
    slots, width = grad_ref.shape[1:]
    picks = [known_ref[:slots, i * cands : (i + 1) * cands] for i in range(2)]
    known = known_ref[slots : slots + 16, :cands].astype(F32).T
    live, label = known[:, :1], known[:, 1:2]
    out_w = known_ref[slots + 16 :, :hidden].astype(F32)
    out_w = out_w[:1] + out_w[1:2] + out_w[2:3]
    part_ref[...] = first_ref[...]
    add_shards(rows_ref, late, [shards[i] for i in late], part_ref)
    if slots > cands:
        pre_act = part_ref[0]
    else:
        pre_act = None
        for i in range(2):
            rest = part_ref[i]
            for _ in range(3):
                high = rest.astype(BF16)
                rest = rest - high.astype(F32)
                term = dot(picks[i], high, ((0,), (0,)))
                pre_act = term if pre_act is None else pre_act + term
    gate = jax.nn.sigmoid(pre_act)
    score = jnp.sum(pre_act * gate * out_w, axis=1, keepdims=True) * live
    scores_ref[...] = jnp.broadcast_to(score, (cands, 128)).T[:1]
    grad_score = (jax.nn.sigmoid(score) - label) * live
    grad_pre = (grad_score * out_w * (gate * (1.0 + pre_act * (1.0 - gate)))).astype(BF16)
    for i in range(2):
        total = dot(picks[i], grad_pre)
        high = total.astype(BF16)
        sum_ref[i, :slots, :] = high
        sum_ref[i, slots:, :] = (total - high.astype(F32)).astype(BF16)
    for i, shard in enumerate(shards):
        row = shard_row(i, depth)
        half = row // width
        col = pl.multiple_of(row % width, depth)
        both = dot(sum_ref[half], shard[...], ((1,), (1,)))
        grad_ref[half, :, pl.ds(col, depth)] = both[:slots] + both[slots:]
    pack_rows(grad_ref[0] + grad_ref[1], stage_ref, back_ref)


def scatter_kernel(ready, pick_ref, got_ref, out_ref, stage_ref):
    ready()
    rows = unpack_rows(got_ref, stage_ref, out_ref.shape[1] // 128)
    out_ref[...] = dot(pick_ref[...], rows)


def swap(array, axis, k):
    count = lax.axis_size(axis)
    return lax.ppermute(array, axis, [(i, i ^ k) for i in range(count)])


def across(shard, edge_count):
    return [shard] + [swap(shard, "edge", 2 * k) for k in range(1, edge_count // 2)]


def from_core(shards):
    return [one for shard in shards for one in (shard, swap(shard, "edge", 1))]


def local(
    node_feats,
    gat_weight,
    attn_src,
    attn_dst,
    neighbours,
    degree,
    halo_rows,
    halo_count,
    endpoint_rows,
    cand_ends,
    cand_count,
    labels,
    mlp_weight,
    out_weight,
):
    nodes, width = node_feats.shape
    dom_count = lax.axis_size("dom")
    edge_count = lax.axis_size("edge")
    block = halo_rows.shape[-1]
    cands = labels.shape[-1]
    hidden = out_weight.shape[0]
    halo = dom_count * block
    table = nodes + halo
    slots = dom_count * edge_count * endpoint_rows.shape[-1]
    pieces = width // 128
    everyone = ("dom", "edge")
    shape = jax.ShapeDtypeStruct

    heads = attn_src.shape[0]
    send_rows = call(
        halo_kernel,
        shape((halo, width), BF16),
        [("f", halo_count[0]), ("f", halo_rows[0, 0]), ("f", node_feats)],
        vmem_mib=60,
    )
    got_rows = lax.all_to_all(send_rows, "dom", split_axis=0, concat_axis=0, tiled=True)
    gat_across = across(gat_weight, edge_count)
    mlp_across = across(mlp_weight, edge_count)
    lanes = -(-(2 * table + attn_src.shape[1] + slots) // 128) * 128
    for_attend, for_score, pick = call(
        functools.partial(prepare_kernel, table),
        (
            shape((nodes, lanes), BF16),
            shape((slots + 32, max(2 * cands, hidden)), BF16),
            shape((nodes, slots), BF16),
        ),
        [
            ("s", cand_count),
            ("f", neighbours.T),
            ("f", degree.reshape(1, nodes)),
            ("f", attn_src),
            ("f", attn_dst),
            ("f", endpoint_rows.reshape(1, slots)),
            ("f", cand_ends[0, 0]),
            ("f", labels[0]),
            ("f", out_weight.reshape(1, hidden)),
        ],
        vmem_mib=60,
    )
    gat_across = lax.optimization_barrier((*gat_across, for_attend))[:-1]
    gat_shards = from_core(gat_across)
    packed = pltpu.VMEM((slots * pieces, 128), F32)
    node_out, send_ends = call(
        functools.partial(attend_kernel, edge_count, heads, slots),
        (shape((nodes, width), BF16), shape((slots * pieces, 128), BF16)),
        [("v", node_feats), ("v", got_rows), ("v", for_attend)] + [("v", w) for w in gat_shards],
        [
            pltpu.VMEM((table, width), BF16),
            packed,
            pltpu.VMEM((table, width), BF16),
            pltpu.VMEM((nodes, table), F32),
            pltpu.VMEM((2, 2 * nodes, table), BF16),
            pltpu.VMEM((width if width // edge_count % 128 else 16, width), BF16),
        ],
    )
    got_ends = lax.all_to_all(send_ends, everyone, split_axis=0, concat_axis=0, tiled=True)
    mlp_shards = [mlp_across[0], swap(mlp_across[0], "edge", 1)]
    tied = lax.optimization_barrier((*mlp_across[1:], send_ends))[:-1]
    for shard, held in zip(mlp_across[1:], tied):
        mlp_shards += [shard, swap(held, "edge", 1)]
    early = [i for i in range(edge_count) if i < 2 or i % 2 == 0]
    late = [i for i in range(edge_count) if i not in early]
    many = slots > cands
    rows, part = call(
        functools.partial(first_kernel, early, cands),
        (
            shape((cands, 2 * width) if many else (slots, width), BF16),
            shape((1, cands, hidden) if many else (2, slots, hidden), F32),
        ),
        [("v", got_ends), ("v", for_score)] + [("v", mlp_shards[i]) for i in early],
        [packed],
        cost=pl.CostEstimate(flops=20 * 10**9, bytes_accessed=60 * 10**6, transcendentals=0),
    )
    scores, send_back = call(
        functools.partial(score_kernel, late, cands),
        (shape((1, cands), F32), shape((slots * pieces, 128), BF16)),
        [("v", rows), ("v", part), ("v", for_score)] + [("v", w) for w in mlp_shards],
        [
            packed,
            pltpu.VMEM((2, 2 * slots, hidden), BF16),
            pltpu.VMEM((2, slots, width), F32),
            pltpu.VMEM(part.shape, F32),
        ],
    )
    got_back = lax.all_to_all(send_back, everyone, split_axis=0, concat_axis=0, tiled=True)
    node_grad = call(
        scatter_kernel, shape((nodes, width), F32), [("v", pick), ("v", got_back)], [packed]
    )
    return (node_out, scores.reshape(1, 1, cands), node_grad)


def solution(mesh):
    in_specs = (
        P(("dom", "edge"), None),
        P("edge", None),
        P(),
        P(),
        P(("dom", "edge"), None),
        P(("dom", "edge")),
        P("dom", "edge", None, None),
        P("dom", "edge", None),
        P("dom", "edge", None, None, None),
        P("dom", "edge", None, None),
        P("dom", "edge"),
        P("dom", "edge", None),
        P("edge", None),
        P(),
    )
    out_specs = (P(("dom", "edge"), None), P("dom", "edge", None), P(("dom", "edge"), None))
    return jax.shard_map(local, mesh=mesh, in_specs=in_specs, out_specs=out_specs, check_vma=False)
```

```python
import functools

import jax
import jax.numpy as jnp
from jax import lax
from jax.experimental import pallas as pl
from jax.experimental.pallas import tpu as pltpu
from jax.sharding import PartitionSpec as P

F32 = jnp.float32
BF16 = jnp.bfloat16
LOG2_E = 1.4426950408889634
DEAD = 64.0
VMEM = pl.BlockSpec(memory_space=pltpu.VMEM)
SPACES = {
    "v": VMEM,
    "s": pl.BlockSpec(memory_space=pltpu.SMEM),
    "f": pl.BlockSpec(memory_space=pl.ANY),
    "any": pl.BlockSpec(memory_space=pl.ANY),
}


def dot(a, b, dims=((1,), (0,))):
    return lax.dot_general(a, b, (dims, ((), ())), preferred_element_type=F32)


def call(kernel, outs, ins, scratch=(), vmem_mib=20, out_space="v", cost=None):
    fetched = [i for i, (space, _) in enumerate(ins) if space == "f"]

    def body(*refs):
        refs = list(refs)
        local_count = len(fetched) + 1
        own, (held, sems) = refs[:-local_count], (refs[-local_count:-1], refs[-1])
        copies = []
        for n, i in enumerate(fetched):
            copies.append(pltpu.make_async_copy(own[i], held[n], sems.at[n]))
            copies[-1].start()
            own[i] = held[n]

        def ready():
            for copy in copies:
                copy.wait()

        kernel(ready, *own)

    return pl.pallas_call(
        body,
        out_shape=outs,
        in_specs=[SPACES[space] for space, _ in ins],
        out_specs=jax.tree.map(lambda _: SPACES[out_space], outs),
        scratch_shapes=list(scratch)
        + [pltpu.VMEM(ins[i][1].shape, ins[i][1].dtype) for i in fetched]
        + [pltpu.SemaphoreType.DMA((max(1, len(fetched)),))],
        cost_estimate=cost,
        compiler_params=pltpu.CompilerParams(vmem_limit_bytes=vmem_mib * 1024 * 1024),
    )(*[array for _, array in ins])


def halo_kernel(ready, count_ref, rows_ref, feats_ref, out_ref):
    doms, block = rows_ref.shape
    at = lax.broadcasted_iota(jnp.int32, (1, block), 1)
    ready()
    pieces = [
        jnp.where(at < count_ref[:, s : s + 1], rows_ref[s : s + 1, :], -1) for s in range(doms)
    ]
    flat = jnp.concatenate(pieces, axis=1)
    total = doms * block
    nodes = feats_ref.shape[0]
    pick = (lax.broadcasted_iota(jnp.int32, (nodes, total), 0) == flat).astype(F32).astype(BF16)
    rows = dot(pick, feats_ref[...], ((0,), (0,)))
    first = lax.broadcasted_iota(jnp.int32, (16, total), 0) == 0
    dead = jnp.where(first & (flat < 0), 1.0, 0.0).astype(BF16)
    mark_at = (lax.broadcasted_iota(jnp.int32, (16, 128), 0) == 0) & (
        lax.broadcasted_iota(jnp.int32, (16, 128), 1) == 0
    )
    mark = jnp.where(mark_at, DEAD, 0.0).astype(BF16)
    out_ref[:, :128] = (rows[:, :128] + dot(dead, mark, ((0,), (0,)))).astype(BF16)
    out_ref[:, 128:] = rows[:, 128:].astype(BF16)


def three_parts(values):
    high = values.astype(BF16).astype(F32)
    middle = (values - high).astype(BF16).astype(F32)
    return jnp.concatenate([high, middle, values - high - middle], axis=0)


def block_diagonal(parts, heads):
    parts = parts.astype(F32)
    wide = jnp.concatenate([parts] * heads, axis=1)
    lane_head = lax.broadcasted_iota(jnp.int32, wide.shape, 1) // parts.shape[1]
    row_head = lax.broadcasted_iota(jnp.int32, wide.shape, 0) % heads
    wide = jnp.where(lane_head == row_head, wide, 0.0)
    return jnp.concatenate([wide, jnp.zeros((heads, wide.shape[1]), F32)], axis=0).astype(BF16)


def prepare_kernel(
    table,
    ready,
    live_ref,
    neigh_ref,
    degree_ref,
    src_ref,
    dst_ref,
    ends_ref,
    cand_ref,
    labels_ref,
    out_w_ref,
    for_attend_ref,
    for_score_ref,
    pick_ref,
):
    ready()
    nodes, ends = pick_ref.shape
    heads, size = src_ref.shape
    slots = neigh_ref.shape[0]
    ids = neigh_ref[...]
    ids = jnp.where(lax.broadcasted_iota(jnp.int32, ids.shape, 0) < degree_ref[...], ids, -1)
    for base in range(0, table, nodes):
        at = base + lax.broadcasted_iota(jnp.int32, (nodes, nodes), 0)
        total = jnp.zeros((nodes, nodes), F32)
        if base == 0:
            total = (at == lax.broadcasted_iota(jnp.int32, (nodes, nodes), 1)).astype(F32)
        for j in range(slots):
            total = total + (at == ids[j : j + 1, :]).astype(F32)
        total = total.T
        power = jnp.where(total > 1, 2.0, total)
        power = jnp.where(total > 2, 4.0, power)
        power = jnp.where(total > 5, 8.0, power)
        power = jnp.where(total > 13, 16.0, power)
        for_attend_ref[:, base : base + nodes] = total.astype(BF16)
        for_attend_ref[:, table + base : table + base + nodes] = power.astype(BF16)
    node_at = lax.broadcasted_iota(jnp.int32, (nodes, ends), 0)
    pick = (node_at == ends_ref[...]).astype(F32).astype(BF16)
    pick_ref[...] = pick
    first = 2 * table + size
    for_attend_ref[:, first : first + ends] = pick
    vectors = [three_parts(src_ref[...]), three_parts(dst_ref[...])]
    for_attend_ref[: 6 * heads, 2 * table : first] = jnp.concatenate(vectors, axis=0).astype(BF16)
    cands = cand_ref.shape[1]
    hidden = out_w_ref.shape[1]
    slot_at = lax.broadcasted_iota(jnp.int32, (ends, cands), 0)
    for i in range(2):
        one_hot = (slot_at == cand_ref[i : i + 1, :]).astype(F32).astype(BF16)
        for_score_ref[:ends, i * cands : (i + 1) * cands] = one_hot
    live = (lax.broadcasted_iota(jnp.int32, (1, cands), 1) < live_ref[0, 0]).astype(F32)
    known = jnp.concatenate([live, labels_ref[...].astype(F32), jnp.zeros((14, cands), F32)], axis=0)
    for_score_ref[ends : ends + 16, :cands] = known.astype(BF16)
    whole = jnp.concatenate([three_parts(out_w_ref[...]), jnp.zeros((13, hidden), F32)], axis=0)
    for_score_ref[ends + 16 : ends + 32, :hidden] = whole.astype(BF16)
    if ends <= cands:
        place = lax.broadcasted_iota(jnp.int32, (3 * ends, cands), 0) % ends
        stacked = [(place == cand_ref[i : i + 1, :]).astype(F32) for i in range(2)]
        for_score_ref[ends + 32 :, : 6 * ends] = jnp.concatenate(stacked, axis=0).T.astype(BF16)


def shard_row(i, depth):
    return pl.multiple_of((lax.axis_index("edge") ^ i) * depth, depth)


def shard_dots(rows_ref, shards, whole_ref=None):
    depth = shards[0].shape[0]
    if depth % 128:
        for i, shard in enumerate(shards):
            whole_ref[pl.ds(shard_row(i, depth), depth), :] = shard[...]
        return dot(rows_ref[...], whole_ref[...])
    total = None
    for i, shard in enumerate(shards):
        cols = pl.ds(shard_row(i, depth), depth)
        part = dot(rows_ref[:, cols], shard[...])
        total = part if total is None else total + part
    return total


def attend_kernel(shard_count, heads, slots, ready, own_ref, got_ref, known_ref, *rest):
    shards = rest[:shard_count]
    out_ref, send_ref, proj_ref, stage_ref, rows_ref, bias_ref, mix_ref, whole_ref = rest[-8:]
    ready()
    nodes, width = own_ref.shape
    table = proj_ref.shape[0]
    size = width // heads
    count_ref = known_ref.at[:, :table]
    power_ref = known_ref.at[:, table : 2 * table]
    pick_ref = known_ref.at[:, 2 * table + size : 2 * table + size + slots]
    vectors = known_ref[: 6 * heads, 2 * table : 2 * table + size]
    diag_src = block_diagonal(vectors[: 3 * heads], heads)
    diag_dst = block_diagonal(vectors[3 * heads :], heads)
    rows_ref[:nodes, :] = own_ref[...]
    rows_ref[nodes:, :] = got_ref[...]
    proj_ref[...] = shard_dots(rows_ref, shards, whole_ref).astype(BF16)
    parts = dot(diag_src, proj_ref[...], ((1,), (1,)))
    src = parts[:heads] + parts[heads : 2 * heads] + parts[2 * heads : 3 * heads]
    src = src.astype(BF16).astype(F32) * LOG2_E
    parts = dot(proj_ref[:nodes, :], diag_dst, ((1,), (1,)))
    dst = parts[:, :heads] + parts[:, heads : 2 * heads] + parts[:, 2 * heads : 3 * heads]
    dst = dst * LOG2_E
    first_lane = (lax.broadcasted_iota(jnp.int32, (16, 128), 1) == 0).astype(F32).astype(BF16)
    mark = dot(first_lane, rows_ref[nodes:, :128], ((1,), (1,)))[:1]
    hide = jnp.where(mark < DEAD / 2, 0.0, -jnp.inf)
    hide = jnp.concatenate([jnp.zeros((1, nodes), F32), hide], axis=1)
    bias_ref[...] = jnp.where(count_ref[...] > 0, hide, -jnp.inf)
    chunk = 32
    for h in range(heads):
        for r in range(0, nodes, chunk):
            here = slice(r, r + chunk)
            logit = dst[here, h : h + 1] + src[h : h + 1, :]
            logit = jnp.maximum(logit, 0.2 * logit) + bias_ref[here, :]
            terms = jnp.exp2(logit - jnp.max(logit, axis=1, keepdims=True))
            count = count_ref[here, :]
            power = power_ref[here, :]
            running = jnp.sum(count.astype(F32) * terms, axis=1, keepdims=True)
            weight = (terms * (1.0 / running)).astype(BF16)
            mix_ref[h % 2, here, :] = weight * power
            mix_ref[h % 2, nodes + r : nodes + r + chunk, :] = weight * (count - power)
        both = dot(mix_ref[h % 2], proj_ref[:, h * size : (h + 1) * size])
        total = both[:nodes] + both[nodes:]
        total = jnp.where(total > 0, total, jnp.exp(jnp.minimum(total, 0.0)) - 1.0)
        out_ref[:, h * size : (h + 1) * size] = total.astype(BF16)
    pack_rows(dot(pick_ref[...], out_ref[...], ((0,), (0,))), stage_ref, send_ref)


def pack_rows(rows, stage_ref, out_ref):
    slots, width = rows.shape
    pieces = width // 128
    for c in range(pieces):
        stage_ref[pl.ds(c, slots, stride=pieces), :] = rows[:, c * 128 : (c + 1) * 128]
    out_ref[...] = stage_ref[...].astype(BF16)


def unpack_rows(ref, stage_ref, pieces):
    stage_ref[...] = ref[...].astype(F32)
    slots = ref.shape[0] // pieces
    parts = [stage_ref[pl.ds(c, slots, stride=pieces), :] for c in range(pieces)]
    return jnp.concatenate(parts, axis=1).astype(BF16)


def add_shards(rows_ref, indices, shards, part_ref):
    depth = shards[0].shape[0]
    span = rows_ref.shape[1]
    for i, shard in zip(indices, shards):
        row = shard_row(i, depth)
        cols = pl.ds(pl.multiple_of(row % span, depth), depth)
        part_ref[row // span] += dot(rows_ref[:, cols], shard[...])


def first_kernel(indices, cands, slot_total, ready, got_ref, known_ref, *rest):
    shards = rest[:-3]
    rows_ref, part_ref, stage_ref = rest[-3:]
    ready()
    slots = slot_total
    width = got_ref.shape[0] * 128 // slots
    rows = unpack_rows(got_ref, stage_ref, width // 128)
    if slots > cands:
        for i in range(2):
            pick = known_ref[:slots, i * cands : (i + 1) * cands]
            pair = dot(pick, rows, ((0,), (0,)))
            rows_ref[:, i * width : (i + 1) * width] = pair.astype(BF16)
    else:
        rows_ref[...] = rows
    part_ref[...] = jnp.zeros_like(part_ref)
    add_shards(rows_ref, indices, shards, part_ref)


def score_kernel(late, cands, ready, rows_ref, first_ref, known_ref, *rest):
    shards = rest[:-6]
    scores_ref, back_ref, stage_ref, sum_ref, grad_ref, part_ref = rest[-6:]
    ready()
    depth, hidden = shards[0].shape
    slots, width = grad_ref.shape[1:]
    picks = [known_ref[:slots, i * cands : (i + 1) * cands] for i in range(2)]
    known = known_ref[slots : slots + 16, :cands].astype(F32).T
    live, label = known[:, :1], known[:, 1:2]
    out_w = known_ref[slots + 16 : slots + 32, :hidden].astype(F32)
    out_w = out_w[:1] + out_w[1:2] + out_w[2:3]
    part_ref[...] = first_ref[...]
    add_shards(rows_ref, late, [shards[i] for i in late], part_ref)
    if slots > cands:
        pre_act = part_ref[0]
    else:
        parts = []
        for i in range(2):
            rest = part_ref[i]
            for _ in range(3):
                parts.append(rest.astype(BF16))
                rest = rest - parts[-1].astype(F32)
        pre_act = dot(known_ref[slots + 32 :, : 6 * slots], jnp.concatenate(parts, axis=0))
    gate = jax.nn.sigmoid(pre_act)
    score = jnp.sum(pre_act * gate * out_w, axis=1, keepdims=True) * live
    scores_ref[...] = jnp.broadcast_to(score, (cands, 128)).T[:1]
    grad_score = (jax.nn.sigmoid(score) - label) * live
    grad_pre = (grad_score * out_w * (gate * (1.0 + pre_act * (1.0 - gate)))).astype(BF16)
    for i in range(2):
        total = dot(picks[i], grad_pre)
        high = total.astype(BF16)
        sum_ref[i, :slots, :] = high
        sum_ref[i, slots:, :] = (total - high.astype(F32)).astype(BF16)
    for i, shard in enumerate(shards):
        row = shard_row(i, depth)
        half = row // width
        col = pl.multiple_of(row % width, depth)
        both = dot(sum_ref[half], shard[...], ((1,), (1,)))
        grad_ref[half, :, pl.ds(col, depth)] = both[:slots] + both[slots:]
    pack_rows(grad_ref[0] + grad_ref[1], stage_ref, back_ref)


def scatter_kernel(ready, pick_ref, got_ref, out_ref, stage_ref):
    ready()
    rows = unpack_rows(got_ref, stage_ref, out_ref.shape[1] // 128)
    out_ref[...] = dot(pick_ref[...], rows)


def swap(array, axis, k):
    count = lax.axis_size(axis)
    return lax.ppermute(array, axis, [(i, i ^ k) for i in range(count)])


def across(shard, edge_count):
    return [shard] + [swap(shard, "edge", 2 * k) for k in range(1, edge_count // 2)]


def from_core(shards):
    return [one for shard in shards for one in (shard, swap(shard, "edge", 1))]


def local(
    node_feats,
    gat_weight,
    attn_src,
    attn_dst,
    neighbours,
    degree,
    halo_rows,
    halo_count,
    endpoint_rows,
    cand_ends,
    cand_count,
    labels,
    mlp_weight,
    out_weight,
):
    nodes, width = node_feats.shape
    dom_count = lax.axis_size("dom")
    edge_count = lax.axis_size("edge")
    block = halo_rows.shape[-1]
    cands = labels.shape[-1]
    hidden = out_weight.shape[0]
    halo = dom_count * block
    table = nodes + halo
    slots = dom_count * edge_count * endpoint_rows.shape[-1]
    pieces = width // 128
    everyone = ("dom", "edge")
    shape = jax.ShapeDtypeStruct

    heads = attn_src.shape[0]
    send_rows = call(
        halo_kernel,
        shape((halo, width), BF16),
        [("f", halo_count[0]), ("f", halo_rows[0, 0]), ("f", node_feats)],
        vmem_mib=60,
    )
    got_rows = lax.all_to_all(send_rows, "dom", split_axis=0, concat_axis=0, tiled=True)
    gat_across = across(gat_weight, edge_count)
    held_mlp = lax.optimization_barrier((mlp_weight, got_rows))[0]
    mlp_across = across(held_mlp, edge_count)
    lanes = -(-(2 * table + attn_src.shape[1] + slots) // 128) * 128
    for_attend, for_score, pick = call(
        functools.partial(prepare_kernel, table),
        (
            shape((nodes, lanes), BF16),
            shape((slots + 32, max(2 * cands, hidden)), BF16)
            if slots > cands
            else shape((slots + 32 + cands, max(2 * cands, hidden, 6 * slots)), BF16),
            shape((nodes, slots), BF16),
        ),
        [
            ("s", cand_count),
            ("f", neighbours.T),
            ("f", degree.reshape(1, nodes)),
            ("f", attn_src),
            ("f", attn_dst),
            ("f", endpoint_rows.reshape(1, slots)),
            ("f", cand_ends[0, 0]),
            ("f", labels[0]),
            ("f", out_weight.reshape(1, hidden)),
        ],
        vmem_mib=60,
    )
    gat_across = lax.optimization_barrier((*gat_across, for_attend))[:-1]
    gat_shards = from_core(gat_across)
    packed = pltpu.VMEM((slots * pieces, 128), F32)
    node_out, send_ends = call(
        functools.partial(attend_kernel, edge_count, heads, slots),
        (shape((nodes, width), BF16), shape((slots * pieces, 128), BF16)),
        [("v", node_feats), ("v", got_rows), ("v", for_attend)] + [("v", w) for w in gat_shards],
        [
            pltpu.VMEM((table, width), BF16),
            packed,
            pltpu.VMEM((table, width), BF16),
            pltpu.VMEM((nodes, table), F32),
            pltpu.VMEM((2, 2 * nodes, table), BF16),
            pltpu.VMEM((width if width // edge_count % 128 else 16, width), BF16),
        ],
    )
    got_ends = lax.all_to_all(send_ends, everyone, split_axis=0, concat_axis=0, tiled=True)
    tied = lax.optimization_barrier((*mlp_across, send_ends))[:-1]
    mlp_across[0] = mlp_weight
    mlp_shards = []
    for shard, held in zip(mlp_across, tied):
        mlp_shards += [shard, swap(held, "edge", 1)]
    early = list(range(0, edge_count, 2))
    late = list(range(1, edge_count, 2))
    many = slots > cands
    rows, part = call(
        functools.partial(first_kernel, early, cands, slots),
        (
            shape((cands, 2 * width) if many else (slots, width), BF16),
            shape((1, cands, hidden) if many else (2, slots, hidden), F32),
        ),
        [("v", got_ends), ("v", for_score)] + [("v", mlp_shards[i]) for i in early],
        [packed],
        cost=pl.CostEstimate(flops=20 * 10**9, bytes_accessed=60 * 10**6, transcendentals=0),
    )
    scores, send_back = call(
        functools.partial(score_kernel, late, cands),
        (shape((1, cands), F32), shape((slots * pieces, 128), BF16)),
        [("v", rows), ("v", part), ("v", for_score)] + [("v", w) for w in mlp_shards],
        [
            packed,
            pltpu.VMEM((2, 2 * slots, hidden), BF16),
            pltpu.VMEM((2, slots, width), F32),
            pltpu.VMEM(part.shape, F32),
        ],
    )
    got_back = lax.all_to_all(send_back, everyone, split_axis=0, concat_axis=0, tiled=True)
    node_grad = call(
        scatter_kernel, shape((nodes, width), F32), [("v", pick), ("v", got_back)], [packed]
    )
    return (node_out, scores.reshape(1, 1, cands), node_grad)


def solution(mesh):
    in_specs = (
        P(("dom", "edge"), None),
        P("edge", None),
        P(),
        P(),
        P(("dom", "edge"), None),
        P(("dom", "edge")),
        P("dom", "edge", None, None),
        P("dom", "edge", None),
        P("dom", "edge", None, None, None),
        P("dom", "edge", None, None),
        P("dom", "edge"),
        P("dom", "edge", None),
        P("edge", None),
        P(),
    )
    out_specs = (P(("dom", "edge"), None), P("dom", "edge", None), P(("dom", "edge"), None))
    return jax.shard_map(local, mesh=mesh, in_specs=in_specs, out_specs=out_specs, check_vma=False)
```

```python
import functools

import jax
import jax.numpy as jnp
from jax import lax
from jax.experimental import pallas as pl
from jax.experimental.pallas import tpu as pltpu
from jax.sharding import PartitionSpec as P

F32 = jnp.float32
BF16 = jnp.bfloat16
LOG2_E = 1.4426950408889634
DEAD = 64.0
VMEM = pl.BlockSpec(memory_space=pltpu.VMEM)
SPACES = {
    "v": VMEM,
    "s": pl.BlockSpec(memory_space=pltpu.SMEM),
    "f": pl.BlockSpec(memory_space=pl.ANY),
    "any": pl.BlockSpec(memory_space=pl.ANY),
}


def dot(a, b, dims=((1,), (0,))):
    return lax.dot_general(a, b, (dims, ((), ())), preferred_element_type=F32)


def call(kernel, outs, ins, scratch=(), vmem_mib=20, out_space="v", cost=None):
    fetched = [i for i, (space, _) in enumerate(ins) if space == "f"]

    def body(*refs):
        refs = list(refs)
        local_count = len(fetched) + 1
        own, (held, sems) = refs[:-local_count], (refs[-local_count:-1], refs[-1])
        copies = []
        for n, i in enumerate(fetched):
            copies.append(pltpu.make_async_copy(own[i], held[n], sems.at[n]))
            copies[-1].start()
            own[i] = held[n]

        def ready():
            for copy in copies:
                copy.wait()

        kernel(ready, *own)

    return pl.pallas_call(
        body,
        out_shape=outs,
        in_specs=[SPACES[space] for space, _ in ins],
        out_specs=jax.tree.map(lambda _: SPACES[out_space], outs),
        scratch_shapes=list(scratch)
        + [pltpu.VMEM(ins[i][1].shape, ins[i][1].dtype) for i in fetched]
        + [pltpu.SemaphoreType.DMA((max(1, len(fetched)),))],
        cost_estimate=cost,
        compiler_params=pltpu.CompilerParams(vmem_limit_bytes=vmem_mib * 1024 * 1024),
    )(*[array for _, array in ins])


def halo_kernel(ready, count_ref, rows_ref, feats_ref, out_ref):
    doms, block = rows_ref.shape
    at = lax.broadcasted_iota(jnp.int32, (1, block), 1)
    ready()
    pieces = [
        jnp.where(at < count_ref[:, s : s + 1], rows_ref[s : s + 1, :], -1) for s in range(doms)
    ]
    flat = jnp.concatenate(pieces, axis=1)
    total = doms * block
    nodes = feats_ref.shape[0]
    pick = (lax.broadcasted_iota(jnp.int32, (nodes, total), 0) == flat).astype(F32).astype(BF16)
    rows = dot(pick, feats_ref[...], ((0,), (0,)))
    first = lax.broadcasted_iota(jnp.int32, (16, total), 0) == 0
    dead = jnp.where(first & (flat < 0), 1.0, 0.0).astype(BF16)
    mark_at = (lax.broadcasted_iota(jnp.int32, (16, 128), 0) == 0) & (
        lax.broadcasted_iota(jnp.int32, (16, 128), 1) == 0
    )
    mark = jnp.where(mark_at, DEAD, 0.0).astype(BF16)
    out_ref[:, :128] = (rows[:, :128] + dot(dead, mark, ((0,), (0,)))).astype(BF16)
    out_ref[:, 128:] = rows[:, 128:].astype(BF16)


def three_parts(values):
    high = values.astype(BF16).astype(F32)
    middle = (values - high).astype(BF16).astype(F32)
    return jnp.concatenate([high, middle, values - high - middle], axis=0)


def block_diagonal(parts, heads):
    parts = parts.astype(F32)
    wide = jnp.concatenate([parts] * heads, axis=1)
    lane_head = lax.broadcasted_iota(jnp.int32, wide.shape, 1) // parts.shape[1]
    row_head = lax.broadcasted_iota(jnp.int32, wide.shape, 0) % heads
    wide = jnp.where(lane_head == row_head, wide, 0.0)
    return jnp.concatenate([wide, jnp.zeros((heads, wide.shape[1]), F32)], axis=0).astype(BF16)


def prepare_kernel(
    table,
    ready,
    live_ref,
    neigh_ref,
    degree_ref,
    src_ref,
    dst_ref,
    ends_ref,
    cand_ref,
    labels_ref,
    out_w_ref,
    for_attend_ref,
    for_score_ref,
    pick_ref,
):
    ready()
    nodes, ends = pick_ref.shape
    heads, size = src_ref.shape
    slots = neigh_ref.shape[0]
    ids = neigh_ref[...]
    ids = jnp.where(lax.broadcasted_iota(jnp.int32, ids.shape, 0) < degree_ref[...], ids, -1)
    for base in range(0, table, nodes):
        at = base + lax.broadcasted_iota(jnp.int32, (nodes, nodes), 0)
        total = jnp.zeros((nodes, nodes), F32)
        if base == 0:
            total = (at == lax.broadcasted_iota(jnp.int32, (nodes, nodes), 1)).astype(F32)
        for j in range(slots):
            total = total + (at == ids[j : j + 1, :]).astype(F32)
        total = total.T
        power = jnp.where(total > 1, 2.0, total)
        power = jnp.where(total > 2, 4.0, power)
        power = jnp.where(total > 5, 8.0, power)
        power = jnp.where(total > 13, 16.0, power)
        for_attend_ref[:, base : base + nodes] = total.astype(BF16)
        for_attend_ref[:, table + base : table + base + nodes] = power.astype(BF16)
    node_at = lax.broadcasted_iota(jnp.int32, (nodes, ends), 0)
    pick = (node_at == ends_ref[...]).astype(F32).astype(BF16)
    pick_ref[...] = pick
    first = 2 * table + size
    for_attend_ref[:, first : first + ends] = pick
    vectors = [three_parts(src_ref[...]), three_parts(dst_ref[...])]
    for_attend_ref[: 6 * heads, 2 * table : first] = jnp.concatenate(vectors, axis=0).astype(BF16)
    cands = cand_ref.shape[1]
    hidden = out_w_ref.shape[1]
    slot_at = lax.broadcasted_iota(jnp.int32, (ends, cands), 0)
    for i in range(2):
        one_hot = (slot_at == cand_ref[i : i + 1, :]).astype(F32).astype(BF16)
        for_score_ref[:ends, i * cands : (i + 1) * cands] = one_hot
    live = (lax.broadcasted_iota(jnp.int32, (1, cands), 1) < live_ref[0, 0]).astype(F32)
    known = jnp.concatenate([live, labels_ref[...].astype(F32), jnp.zeros((14, cands), F32)], axis=0)
    for_score_ref[ends : ends + 16, :cands] = known.astype(BF16)
    whole = jnp.concatenate([three_parts(out_w_ref[...]), jnp.zeros((13, hidden), F32)], axis=0)
    for_score_ref[ends + 16 :, :hidden] = whole.astype(BF16)


def shard_row(i, depth):
    return pl.multiple_of((lax.axis_index("edge") ^ i) * depth, depth)


def shard_dots(rows_ref, shards, whole_ref=None):
    depth = shards[0].shape[0]
    if depth % 128:
        for i, shard in enumerate(shards):
            whole_ref[pl.ds(shard_row(i, depth), depth), :] = shard[...]
        return dot(rows_ref[...], whole_ref[...])
    total = None
    for i, shard in enumerate(shards):
        cols = pl.ds(shard_row(i, depth), depth)
        part = dot(rows_ref[:, cols], shard[...])
        total = part if total is None else total + part
    return total


def attend_kernel(shard_count, heads, slots, ready, own_ref, got_ref, known_ref, *rest):
    shards = rest[:shard_count]
    out_ref, send_ref, proj_ref, stage_ref, rows_ref, bias_ref, mix_ref, whole_ref = rest[-8:]
    ready()
    nodes, width = own_ref.shape
    table = proj_ref.shape[0]
    size = width // heads
    count_ref = known_ref.at[:, :table]
    power_ref = known_ref.at[:, table : 2 * table]
    pick_ref = known_ref.at[:, 2 * table + size : 2 * table + size + slots]
    vectors = known_ref[: 6 * heads, 2 * table : 2 * table + size]
    diag_src = block_diagonal(vectors[: 3 * heads], heads)
    diag_dst = block_diagonal(vectors[3 * heads :], heads)
    rows_ref[:nodes, :] = own_ref[...]
    rows_ref[nodes:, :] = got_ref[...]
    proj_ref[...] = shard_dots(rows_ref, shards, whole_ref).astype(BF16)
    parts = dot(diag_src, proj_ref[...], ((1,), (1,)))
    src = parts[:heads] + parts[heads : 2 * heads] + parts[2 * heads : 3 * heads]
    src = src.astype(BF16).astype(F32) * LOG2_E
    parts = dot(proj_ref[:nodes, :], diag_dst, ((1,), (1,)))
    dst = parts[:, :heads] + parts[:, heads : 2 * heads] + parts[:, 2 * heads : 3 * heads]
    dst = dst * LOG2_E
    first_lane = (lax.broadcasted_iota(jnp.int32, (16, 128), 1) == 0).astype(F32).astype(BF16)
    mark = dot(first_lane, rows_ref[nodes:, :128], ((1,), (1,)))[:1]
    hide = jnp.where(mark < DEAD / 2, 0.0, -jnp.inf)
    hide = jnp.concatenate([jnp.zeros((1, nodes), F32), hide], axis=1)
    bias_ref[...] = jnp.where(count_ref[...] > 0, hide, -jnp.inf)
    chunk = 32
    for h in range(heads):
        for r in range(0, nodes, chunk):
            here = slice(r, r + chunk)
            logit = dst[here, h : h + 1] + src[h : h + 1, :]
            logit = jnp.maximum(logit, 0.2 * logit) + bias_ref[here, :]
            terms = jnp.exp2(logit - jnp.max(logit, axis=1, keepdims=True))
            count = count_ref[here, :]
            power = power_ref[here, :]
            running = jnp.sum(count.astype(F32) * terms, axis=1, keepdims=True)
            weight = (terms * (1.0 / running)).astype(BF16)
            mix_ref[h % 2, here, :] = weight * power
            mix_ref[h % 2, nodes + r : nodes + r + chunk, :] = weight * (count - power)
        both = dot(mix_ref[h % 2], proj_ref[:, h * size : (h + 1) * size])
        total = both[:nodes] + both[nodes:]
        total = jnp.where(total > 0, total, jnp.exp(jnp.minimum(total, 0.0)) - 1.0)
        out_ref[:, h * size : (h + 1) * size] = total.astype(BF16)
    pack_rows(dot(pick_ref[...], out_ref[...], ((0,), (0,))), stage_ref, send_ref)


def pack_rows(rows, stage_ref, out_ref):
    slots, width = rows.shape
    pieces = width // 128
    for c in range(pieces):
        stage_ref[pl.ds(c, slots, stride=pieces), :] = rows[:, c * 128 : (c + 1) * 128]
    out_ref[...] = stage_ref[...].astype(BF16)


def unpack_rows(ref, stage_ref, pieces):
    stage_ref[...] = ref[...].astype(F32)
    slots = ref.shape[0] // pieces
    parts = [stage_ref[pl.ds(c, slots, stride=pieces), :] for c in range(pieces)]
    return jnp.concatenate(parts, axis=1).astype(BF16)


def add_shards(rows_ref, indices, shards, part_ref):
    depth = shards[0].shape[0]
    span = rows_ref.shape[1]
    for i, shard in zip(indices, shards):
        row = shard_row(i, depth)
        cols = pl.ds(pl.multiple_of(row % span, depth), depth)
        part_ref[row // span] += dot(rows_ref[:, cols], shard[...])


def first_kernel(indices, cands, ready, got_ref, known_ref, *rest):
    shards = rest[:-3]
    rows_ref, part_ref, stage_ref = rest[-3:]
    ready()
    slots = known_ref.shape[0] - 32
    width = got_ref.shape[0] * 128 // slots
    rows = unpack_rows(got_ref, stage_ref, width // 128)
    if slots > cands:
        for i in range(2):
            pick = known_ref[:slots, i * cands : (i + 1) * cands]
            pair = dot(pick, rows, ((0,), (0,)))
            rows_ref[:, i * width : (i + 1) * width] = pair.astype(BF16)
    else:
        rows_ref[...] = rows
    part_ref[...] = jnp.zeros_like(part_ref)
    add_shards(rows_ref, indices, shards, part_ref)


def score_kernel(late, cands, ready, rows_ref, first_ref, known_ref, *rest):
    shards = rest[:-6]
    scores_ref, back_ref, stage_ref, sum_ref, grad_ref, part_ref = rest[-6:]
    ready()
    depth, hidden = shards[0].shape
    slots, width = grad_ref.shape[1:]
    picks = [known_ref[:slots, i * cands : (i + 1) * cands] for i in range(2)]
    known = known_ref[slots : slots + 16, :cands].astype(F32).T
    live, label = known[:, :1], known[:, 1:2]
    out_w = known_ref[slots + 16 :, :hidden].astype(F32)
    out_w = out_w[:1] + out_w[1:2] + out_w[2:3]
    part_ref[...] = first_ref[...]
    add_shards(rows_ref, late, [shards[i] for i in late], part_ref)
    if slots > cands:
        pre_act = part_ref[0]
    else:
        pre_act = None
        for i in range(2):
            rest = part_ref[i]
            for _ in range(3):
                high = rest.astype(BF16)
                rest = rest - high.astype(F32)
                term = dot(picks[i], high, ((0,), (0,)))
                pre_act = term if pre_act is None else pre_act + term
    gate = jax.nn.sigmoid(pre_act)
    score = jnp.sum(pre_act * gate * out_w, axis=1, keepdims=True) * live
    scores_ref[...] = jnp.broadcast_to(score, (cands, 128)).T[:1]
    grad_score = (jax.nn.sigmoid(score) - label) * live
    grad_pre = (grad_score * out_w * (gate * (1.0 + pre_act * (1.0 - gate)))).astype(BF16)
    for i in range(2):
        total = dot(picks[i], grad_pre)
        high = total.astype(BF16)
        sum_ref[i, :slots, :] = high
        sum_ref[i, slots:, :] = (total - high.astype(F32)).astype(BF16)
    for i, shard in enumerate(shards):
        row = shard_row(i, depth)
        half = row // width
        col = pl.multiple_of(row % width, depth)
        both = dot(sum_ref[half], shard[...], ((1,), (1,)))
        grad_ref[half, :, pl.ds(col, depth)] = both[:slots] + both[slots:]
    pack_rows(grad_ref[0] + grad_ref[1], stage_ref, back_ref)


def scatter_kernel(ready, pick_ref, got_ref, out_ref, stage_ref):
    ready()
    rows = unpack_rows(got_ref, stage_ref, out_ref.shape[1] // 128)
    out_ref[...] = dot(pick_ref[...], rows)


def swap(array, axis, k):
    count = lax.axis_size(axis)
    return lax.ppermute(array, axis, [(i, i ^ k) for i in range(count)])


def across(shard, edge_count):
    return [shard] + [swap(shard, "edge", 2 * k) for k in range(1, edge_count // 2)]


def from_core(shards):
    return [one for shard in shards for one in (shard, swap(shard, "edge", 1))]


def local(
    node_feats,
    gat_weight,
    attn_src,
    attn_dst,
    neighbours,
    degree,
    halo_rows,
    halo_count,
    endpoint_rows,
    cand_ends,
    cand_count,
    labels,
    mlp_weight,
    out_weight,
):
    nodes, width = node_feats.shape
    dom_count = lax.axis_size("dom")
    edge_count = lax.axis_size("edge")
    block = halo_rows.shape[-1]
    cands = labels.shape[-1]
    hidden = out_weight.shape[0]
    halo = dom_count * block
    table = nodes + halo
    slots = dom_count * edge_count * endpoint_rows.shape[-1]
    pieces = width // 128
    everyone = ("dom", "edge")
    shape = jax.ShapeDtypeStruct

    heads = attn_src.shape[0]
    send_rows = call(
        halo_kernel,
        shape((halo, width), BF16),
        [("f", halo_count[0]), ("f", halo_rows[0, 0]), ("f", node_feats)],
        vmem_mib=60,
    )
    got_rows = lax.all_to_all(send_rows, "dom", split_axis=0, concat_axis=0, tiled=True)
    gat_across = across(gat_weight, edge_count)
    mlp_across = across(mlp_weight, edge_count)
    lanes = -(-(2 * table + attn_src.shape[1] + slots) // 128) * 128
    for_attend, for_score, pick = call(
        functools.partial(prepare_kernel, table),
        (
            shape((nodes, lanes), BF16),
            shape((slots + 32, max(2 * cands, hidden)), BF16),
            shape((nodes, slots), BF16),
        ),
        [
            ("s", cand_count),
            ("f", neighbours.T),
            ("f", degree.reshape(1, nodes)),
            ("f", attn_src),
            ("f", attn_dst),
            ("f", endpoint_rows.reshape(1, slots)),
            ("f", cand_ends[0, 0]),
            ("f", labels[0]),
            ("f", out_weight.reshape(1, hidden)),
        ],
        vmem_mib=60,
    )
    gat_across = lax.optimization_barrier((*gat_across, for_attend))[:-1]
    gat_shards = from_core(gat_across)
    packed = pltpu.VMEM((slots * pieces, 128), F32)
    node_out, send_ends = call(
        functools.partial(attend_kernel, edge_count, heads, slots),
        (shape((nodes, width), BF16), shape((slots * pieces, 128), BF16)),
        [("v", node_feats), ("v", got_rows), ("v", for_attend)] + [("v", w) for w in gat_shards],
        [
            pltpu.VMEM((table, width), BF16),
            packed,
            pltpu.VMEM((table, width), BF16),
            pltpu.VMEM((nodes, table), F32),
            pltpu.VMEM((2, 2 * nodes, table), BF16),
            pltpu.VMEM((width if width // edge_count % 128 else 16, width), BF16),
        ],
    )
    got_ends = lax.all_to_all(send_ends, everyone, split_axis=0, concat_axis=0, tiled=True)
    tied = lax.optimization_barrier((*mlp_across, send_ends))[:-1]
    mlp_shards = []
    for shard, held in zip(mlp_across, tied):
        mlp_shards += [shard, swap(held, "edge", 1)]
    early = list(range(0, edge_count, 2))
    late = list(range(1, edge_count, 2))
    many = slots > cands
    rows, part = call(
        functools.partial(first_kernel, early, cands),
        (
            shape((cands, 2 * width) if many else (slots, width), BF16),
            shape((1, cands, hidden) if many else (2, slots, hidden), F32),
        ),
        [("v", got_ends), ("v", for_score)] + [("v", mlp_shards[i]) for i in early],
        [packed],
        cost=pl.CostEstimate(flops=20 * 10**9, bytes_accessed=60 * 10**6, transcendentals=0),
    )
    scores, send_back = call(
        functools.partial(score_kernel, late, cands),
        (shape((1, cands), F32), shape((slots * pieces, 128), BF16)),
        [("v", rows), ("v", part), ("v", for_score)] + [("v", w) for w in mlp_shards],
        [
            packed,
            pltpu.VMEM((2, 2 * slots, hidden), BF16),
            pltpu.VMEM((2, slots, width), F32),
            pltpu.VMEM(part.shape, F32),
        ],
    )
    got_back = lax.all_to_all(send_back, everyone, split_axis=0, concat_axis=0, tiled=True)
    node_grad = call(
        scatter_kernel, shape((nodes, width), F32), [("v", pick), ("v", got_back)], [packed]
    )
    return (node_out, scores.reshape(1, 1, cands), node_grad)


def solution(mesh):
    in_specs = (
        P(("dom", "edge"), None),
        P("edge", None),
        P(),
        P(),
        P(("dom", "edge"), None),
        P(("dom", "edge")),
        P("dom", "edge", None, None),
        P("dom", "edge", None),
        P("dom", "edge", None, None, None),
        P("dom", "edge", None, None),
        P("dom", "edge"),
        P("dom", "edge", None),
        P("edge", None),
        P(),
    )
    out_specs = (P(("dom", "edge"), None), P("dom", "edge", None), P(("dom", "edge"), None))
    return jax.shard_map(local, mesh=mesh, in_specs=in_specs, out_specs=out_specs, check_vma=False)
```

```python
import functools

import jax
import jax.numpy as jnp
from jax import lax
from jax.experimental import pallas as pl
from jax.experimental.pallas import tpu as pltpu
from jax.sharding import PartitionSpec as P

F32 = jnp.float32
BF16 = jnp.bfloat16
LOG2_E = 1.4426950408889634
DEAD = 64.0
VMEM = pl.BlockSpec(memory_space=pltpu.VMEM)
SPACES = {
    "v": VMEM,
    "s": pl.BlockSpec(memory_space=pltpu.SMEM),
    "f": pl.BlockSpec(memory_space=pl.ANY),
    "any": pl.BlockSpec(memory_space=pl.ANY),
}


def dot(a, b, dims=((1,), (0,))):
    return lax.dot_general(a, b, (dims, ((), ())), preferred_element_type=F32)


def call(kernel, outs, ins, scratch=(), vmem_mib=20, out_space="v", cost=None):
    fetched = [i for i, (space, _) in enumerate(ins) if space == "f"]

    def body(*refs):
        refs = list(refs)
        local_count = len(fetched) + 1
        own, (held, sems) = refs[:-local_count], (refs[-local_count:-1], refs[-1])
        copies = []
        for n, i in enumerate(fetched):
            copies.append(pltpu.make_async_copy(own[i], held[n], sems.at[n]))
            copies[-1].start()
            own[i] = held[n]

        def ready():
            for copy in copies:
                copy.wait()

        kernel(ready, *own)

    return pl.pallas_call(
        body,
        out_shape=outs,
        in_specs=[SPACES[space] for space, _ in ins],
        out_specs=jax.tree.map(lambda _: SPACES[out_space], outs),
        scratch_shapes=list(scratch)
        + [pltpu.VMEM(ins[i][1].shape, ins[i][1].dtype) for i in fetched]
        + [pltpu.SemaphoreType.DMA((max(1, len(fetched)),))],
        cost_estimate=cost,
        compiler_params=pltpu.CompilerParams(vmem_limit_bytes=vmem_mib * 1024 * 1024),
    )(*[array for _, array in ins])


def halo_kernel(ready, count_ref, rows_ref, feats_ref, out_ref):
    doms, block = rows_ref.shape
    at = lax.broadcasted_iota(jnp.int32, (1, block), 1)
    ready()
    pieces = [
        jnp.where(at < count_ref[:, s : s + 1], rows_ref[s : s + 1, :], -1) for s in range(doms)
    ]
    flat = jnp.concatenate(pieces, axis=1)
    total = doms * block
    nodes = feats_ref.shape[0]
    pick = (lax.broadcasted_iota(jnp.int32, (nodes, total), 0) == flat).astype(F32).astype(BF16)
    rows = dot(pick, feats_ref[...], ((0,), (0,)))
    first = lax.broadcasted_iota(jnp.int32, (16, total), 0) == 0
    dead = jnp.where(first & (flat < 0), 1.0, 0.0).astype(BF16)
    mark_at = (lax.broadcasted_iota(jnp.int32, (16, 128), 0) == 0) & (
        lax.broadcasted_iota(jnp.int32, (16, 128), 1) == 0
    )
    mark = jnp.where(mark_at, DEAD, 0.0).astype(BF16)
    out_ref[:, :128] = (rows[:, :128] + dot(dead, mark, ((0,), (0,)))).astype(BF16)
    out_ref[:, 128:] = rows[:, 128:].astype(BF16)


def three_parts(values):
    high = values.astype(BF16).astype(F32)
    middle = (values - high).astype(BF16).astype(F32)
    return jnp.concatenate([high, middle, values - high - middle], axis=0)


def block_diagonal(parts, heads):
    parts = parts.astype(F32)
    wide = jnp.concatenate([parts] * heads, axis=1)
    lane_head = lax.broadcasted_iota(jnp.int32, wide.shape, 1) // parts.shape[1]
    row_head = lax.broadcasted_iota(jnp.int32, wide.shape, 0) % heads
    wide = jnp.where(lane_head == row_head, wide, 0.0)
    return jnp.concatenate([wide, jnp.zeros((heads, wide.shape[1]), F32)], axis=0).astype(BF16)


def prepare_kernel(
    table,
    ready,
    live_ref,
    neigh_ref,
    degree_ref,
    src_ref,
    dst_ref,
    ends_ref,
    cand_ref,
    labels_ref,
    out_w_ref,
    for_attend_ref,
    for_score_ref,
    pick_ref,
):
    ready()
    nodes, ends = pick_ref.shape
    heads, size = src_ref.shape
    slots = neigh_ref.shape[0]
    ids = neigh_ref[...]
    ids = jnp.where(lax.broadcasted_iota(jnp.int32, ids.shape, 0) < degree_ref[...], ids, -1)
    for base in range(0, table, nodes):
        at = base + lax.broadcasted_iota(jnp.int32, (nodes, nodes), 0)
        total = jnp.zeros((nodes, nodes), F32)
        if base == 0:
            total = (at == lax.broadcasted_iota(jnp.int32, (nodes, nodes), 1)).astype(F32)
        for j in range(slots):
            total = total + (at == ids[j : j + 1, :]).astype(F32)
        total = total.T
        power = jnp.where(total > 1, 2.0, total)
        power = jnp.where(total > 2, 4.0, power)
        power = jnp.where(total > 5, 8.0, power)
        power = jnp.where(total > 13, 16.0, power)
        for_attend_ref[:, base : base + nodes] = total.astype(BF16)
        for_attend_ref[:, table + base : table + base + nodes] = power.astype(BF16)
    node_at = lax.broadcasted_iota(jnp.int32, (nodes, ends), 0)
    pick = (node_at == ends_ref[...]).astype(F32).astype(BF16)
    pick_ref[...] = pick
    first = 2 * table + size
    for_attend_ref[:, first : first + ends] = pick
    vectors = [three_parts(src_ref[...]), three_parts(dst_ref[...])]
    for_attend_ref[: 6 * heads, 2 * table : first] = jnp.concatenate(vectors, axis=0).astype(BF16)
    cands = cand_ref.shape[1]
    hidden = out_w_ref.shape[1]
    slot_at = lax.broadcasted_iota(jnp.int32, (ends, cands), 0)
    for i in range(2):
        one_hot = (slot_at == cand_ref[i : i + 1, :]).astype(F32).astype(BF16)
        for_score_ref[:ends, i * cands : (i + 1) * cands] = one_hot
    live = (lax.broadcasted_iota(jnp.int32, (1, cands), 1) < live_ref[0, 0]).astype(F32)
    known = jnp.concatenate([live, labels_ref[...].astype(F32), jnp.zeros((14, cands), F32)], axis=0)
    for_score_ref[ends : ends + 16, :cands] = known.astype(BF16)
    whole = jnp.concatenate([three_parts(out_w_ref[...]), jnp.zeros((13, hidden), F32)], axis=0)
    for_score_ref[ends + 16 :, :hidden] = whole.astype(BF16)


def shard_row(i, depth):
    return pl.multiple_of((lax.axis_index("edge") ^ i) * depth, depth)


def shard_dots(rows_ref, shards, whole_ref=None, arriving=None):
    depth = shards[0].shape[0]
    arriving = arriving or {}
    if depth % 128:
        for copy in arriving.values():
            copy.wait()
        for i, shard in enumerate(shards):
            whole_ref[pl.ds(shard_row(i, depth), depth), :] = shard[...]
        return dot(rows_ref[...], whole_ref[...])
    total = None
    for i, shard in enumerate(shards):
        cols = pl.ds(shard_row(i, depth), depth)
        if i in arriving:
            arriving[i].wait()
        part = dot(rows_ref[:, cols], shard[...])
        total = part if total is None else total + part
    return total


def second_hop(edge_count):
    return [i for i in range(edge_count) if i > 1 and i % 2]


def attend_kernel(shard_count, heads, slots, ready, own_ref, got_ref, known_ref, *rest):
    shards = list(rest[:shard_count])
    out_ref, send_ref, proj_ref, stage_ref, rows_ref, bias_ref, mix_ref, whole_ref = rest[shard_count:-2]
    late_ref, late_sems = rest[-2:]
    arriving = {}
    for j, i in enumerate(second_hop(shard_count)):
        arriving[i] = pltpu.make_async_copy(shards[i], late_ref.at[j], late_sems.at[j])
        arriving[i].start()
        shards[i] = late_ref.at[j]
    ready()
    nodes, width = own_ref.shape
    table = proj_ref.shape[0]
    size = width // heads
    count_ref = known_ref.at[:, :table]
    power_ref = known_ref.at[:, table : 2 * table]
    pick_ref = known_ref.at[:, 2 * table + size : 2 * table + size + slots]
    vectors = known_ref[: 6 * heads, 2 * table : 2 * table + size]
    diag_src = block_diagonal(vectors[: 3 * heads], heads)
    diag_dst = block_diagonal(vectors[3 * heads :], heads)
    rows_ref[:nodes, :] = own_ref[...]
    rows_ref[nodes:, :] = got_ref[...]
    proj_ref[...] = shard_dots(rows_ref, shards, whole_ref, arriving).astype(BF16)
    parts = dot(diag_src, proj_ref[...], ((1,), (1,)))
    src = parts[:heads] + parts[heads : 2 * heads] + parts[2 * heads : 3 * heads]
    src = src.astype(BF16).astype(F32) * LOG2_E
    parts = dot(proj_ref[:nodes, :], diag_dst, ((1,), (1,)))
    dst = parts[:, :heads] + parts[:, heads : 2 * heads] + parts[:, 2 * heads : 3 * heads]
    dst = dst * LOG2_E
    first_lane = (lax.broadcasted_iota(jnp.int32, (16, 128), 1) == 0).astype(F32).astype(BF16)
    mark = dot(first_lane, rows_ref[nodes:, :128], ((1,), (1,)))[:1]
    hide = jnp.where(mark < DEAD / 2, 0.0, -jnp.inf)
    hide = jnp.concatenate([jnp.zeros((1, nodes), F32), hide], axis=1)
    bias_ref[...] = jnp.where(count_ref[...] > 0, hide, -jnp.inf)
    chunk = 32
    for h in range(heads):
        for r in range(0, nodes, chunk):
            here = slice(r, r + chunk)
            logit = dst[here, h : h + 1] + src[h : h + 1, :]
            logit = jnp.maximum(logit, 0.2 * logit) + bias_ref[here, :]
            terms = jnp.exp2(logit - jnp.max(logit, axis=1, keepdims=True))
            count = count_ref[here, :]
            power = power_ref[here, :]
            running = jnp.sum(count.astype(F32) * terms, axis=1, keepdims=True)
            weight = (terms * (1.0 / running)).astype(BF16)
            mix_ref[h % 2, here, :] = weight * power
            mix_ref[h % 2, nodes + r : nodes + r + chunk, :] = weight * (count - power)
        both = dot(mix_ref[h % 2], proj_ref[:, h * size : (h + 1) * size])
        total = both[:nodes] + both[nodes:]
        total = jnp.where(total > 0, total, jnp.exp(jnp.minimum(total, 0.0)) - 1.0)
        out_ref[:, h * size : (h + 1) * size] = total.astype(BF16)
    pack_rows(dot(pick_ref[...], out_ref[...], ((0,), (0,))), stage_ref, send_ref)


def pack_rows(rows, stage_ref, out_ref):
    slots, width = rows.shape
    pieces = width // 128
    for c in range(pieces):
        stage_ref[pl.ds(c, slots, stride=pieces), :] = rows[:, c * 128 : (c + 1) * 128]
    out_ref[...] = stage_ref[...].astype(BF16)


def unpack_rows(ref, stage_ref, pieces):
    stage_ref[...] = ref[...].astype(F32)
    slots = ref.shape[0] // pieces
    parts = [stage_ref[pl.ds(c, slots, stride=pieces), :] for c in range(pieces)]
    return jnp.concatenate(parts, axis=1).astype(BF16)


def add_shards(rows_ref, indices, shards, part_ref):
    depth = shards[0].shape[0]
    span = rows_ref.shape[1]
    for i, shard in zip(indices, shards):
        row = shard_row(i, depth)
        cols = pl.ds(pl.multiple_of(row % span, depth), depth)
        part_ref[row // span] += dot(rows_ref[:, cols], shard[...])


def first_kernel(indices, cands, ready, got_ref, known_ref, *rest):
    shards = rest[:-3]
    rows_ref, part_ref, stage_ref = rest[-3:]
    ready()
    slots = known_ref.shape[0] - 32
    width = got_ref.shape[0] * 128 // slots
    rows = unpack_rows(got_ref, stage_ref, width // 128)
    if slots > cands:
        for i in range(2):
            pick = known_ref[:slots, i * cands : (i + 1) * cands]
            pair = dot(pick, rows, ((0,), (0,)))
            rows_ref[:, i * width : (i + 1) * width] = pair.astype(BF16)
    else:
        rows_ref[...] = rows
    part_ref[...] = jnp.zeros_like(part_ref)
    add_shards(rows_ref, indices, shards, part_ref)


def score_kernel(late, cands, ready, rows_ref, first_ref, known_ref, *rest):
    shards = rest[:-6]
    scores_ref, back_ref, stage_ref, sum_ref, grad_ref, part_ref = rest[-6:]
    ready()
    depth, hidden = shards[0].shape
    slots, width = grad_ref.shape[1:]
    picks = [known_ref[:slots, i * cands : (i + 1) * cands] for i in range(2)]
    known = known_ref[slots : slots + 16, :cands].astype(F32).T
    live, label = known[:, :1], known[:, 1:2]
    out_w = known_ref[slots + 16 :, :hidden].astype(F32)
    out_w = out_w[:1] + out_w[1:2] + out_w[2:3]
    part_ref[...] = first_ref[...]
    add_shards(rows_ref, late, [shards[i] for i in late], part_ref)
    if slots > cands:
        pre_act = part_ref[0]
    else:
        pre_act = None
        for i in range(2):
            rest = part_ref[i]
            for _ in range(3):
                high = rest.astype(BF16)
                rest = rest - high.astype(F32)
                term = dot(picks[i], high, ((0,), (0,)))
                pre_act = term if pre_act is None else pre_act + term
    gate = jax.nn.sigmoid(pre_act)
    score = jnp.sum(pre_act * gate * out_w, axis=1, keepdims=True) * live
    scores_ref[...] = jnp.broadcast_to(score, (cands, 128)).T[:1]
    grad_score = (jax.nn.sigmoid(score) - label) * live
    grad_pre = (grad_score * out_w * (gate * (1.0 + pre_act * (1.0 - gate)))).astype(BF16)
    for i in range(2):
        total = dot(picks[i], grad_pre)
        high = total.astype(BF16)
        sum_ref[i, :slots, :] = high
        sum_ref[i, slots:, :] = (total - high.astype(F32)).astype(BF16)
    for i, shard in enumerate(shards):
        row = shard_row(i, depth)
        half = row // width
        col = pl.multiple_of(row % width, depth)
        both = dot(sum_ref[half], shard[...], ((1,), (1,)))
        grad_ref[half, :, pl.ds(col, depth)] = both[:slots] + both[slots:]
    pack_rows(grad_ref[0] + grad_ref[1], stage_ref, back_ref)


def scatter_kernel(ready, pick_ref, got_ref, out_ref, stage_ref):
    ready()
    rows = unpack_rows(got_ref, stage_ref, out_ref.shape[1] // 128)
    out_ref[...] = dot(pick_ref[...], rows)


def swap(array, axis, k):
    count = lax.axis_size(axis)
    return lax.ppermute(array, axis, [(i, i ^ k) for i in range(count)])


def across(shard, edge_count):
    return [shard] + [swap(shard, "edge", 2 * k) for k in range(1, edge_count // 2)]


def from_core(shards):
    return [one for shard in shards for one in (shard, swap(shard, "edge", 1))]


def local(
    node_feats,
    gat_weight,
    attn_src,
    attn_dst,
    neighbours,
    degree,
    halo_rows,
    halo_count,
    endpoint_rows,
    cand_ends,
    cand_count,
    labels,
    mlp_weight,
    out_weight,
):
    nodes, width = node_feats.shape
    dom_count = lax.axis_size("dom")
    edge_count = lax.axis_size("edge")
    block = halo_rows.shape[-1]
    cands = labels.shape[-1]
    hidden = out_weight.shape[0]
    halo = dom_count * block
    table = nodes + halo
    slots = dom_count * edge_count * endpoint_rows.shape[-1]
    pieces = width // 128
    everyone = ("dom", "edge")
    shape = jax.ShapeDtypeStruct

    heads = attn_src.shape[0]
    send_rows = call(
        halo_kernel,
        shape((halo, width), BF16),
        [("f", halo_count[0]), ("f", halo_rows[0, 0]), ("f", node_feats)],
        vmem_mib=60,
    )
    got_rows = lax.all_to_all(send_rows, "dom", split_axis=0, concat_axis=0, tiled=True)
    gat_across = across(gat_weight, edge_count)
    mlp_across = across(mlp_weight, edge_count)
    lanes = -(-(2 * table + attn_src.shape[1] + slots) // 128) * 128
    for_attend, for_score, pick = call(
        functools.partial(prepare_kernel, table),
        (
            shape((nodes, lanes), BF16),
            shape((slots + 32, max(2 * cands, hidden)), BF16),
            shape((nodes, slots), BF16),
        ),
        [
            ("s", cand_count),
            ("f", neighbours.T),
            ("f", degree.reshape(1, nodes)),
            ("f", attn_src),
            ("f", attn_dst),
            ("f", endpoint_rows.reshape(1, slots)),
            ("f", cand_ends[0, 0]),
            ("f", labels[0]),
            ("f", out_weight.reshape(1, hidden)),
        ],
        vmem_mib=60,
    )
    gat_across = lax.optimization_barrier((*gat_across, for_attend))[:-1]
    gat_shards = from_core(gat_across)
    packed = pltpu.VMEM((slots * pieces, 128), F32)
    late_count = max(1, len(second_hop(edge_count)))
    node_out, send_ends = call(
        functools.partial(attend_kernel, edge_count, heads, slots),
        (shape((nodes, width), BF16), shape((slots * pieces, 128), BF16)),
        [("v", node_feats), ("v", got_rows), ("v", for_attend)]
        + [("any" if i in second_hop(edge_count) else "v", w) for i, w in enumerate(gat_shards)],
        [
            pltpu.VMEM((table, width), BF16),
            packed,
            pltpu.VMEM((table, width), BF16),
            pltpu.VMEM((nodes, table), F32),
            pltpu.VMEM((2, 2 * nodes, table), BF16),
            pltpu.VMEM((width if width // edge_count % 128 else 16, width), BF16),
            pltpu.VMEM((late_count, *gat_weight.shape), BF16),
            pltpu.SemaphoreType.DMA((late_count,)),
        ],
    )
    got_ends = lax.all_to_all(send_ends, everyone, split_axis=0, concat_axis=0, tiled=True)
    tied = lax.optimization_barrier((*mlp_across, send_ends))[:-1]
    mlp_shards = []
    for shard, held in zip(mlp_across, tied):
        mlp_shards += [shard, swap(held, "edge", 1)]
    early = list(range(0, edge_count, 2))
    late = list(range(1, edge_count, 2))
    many = slots > cands
    rows, part = call(
        functools.partial(first_kernel, early, cands),
        (
            shape((cands, 2 * width) if many else (slots, width), BF16),
            shape((1, cands, hidden) if many else (2, slots, hidden), F32),
        ),
        [("v", got_ends), ("v", for_score)] + [("v", mlp_shards[i]) for i in early],
        [packed],
        cost=pl.CostEstimate(flops=20 * 10**9, bytes_accessed=60 * 10**6, transcendentals=0),
    )
    scores, send_back = call(
        functools.partial(score_kernel, late, cands),
        (shape((1, cands), F32), shape((slots * pieces, 128), BF16)),
        [("v", rows), ("v", part), ("v", for_score)] + [("v", w) for w in mlp_shards],
        [
            packed,
            pltpu.VMEM((2, 2 * slots, hidden), BF16),
            pltpu.VMEM((2, slots, width), F32),
            pltpu.VMEM(part.shape, F32),
        ],
    )
    got_back = lax.all_to_all(send_back, everyone, split_axis=0, concat_axis=0, tiled=True)
    node_grad = call(
        scatter_kernel, shape((nodes, width), F32), [("v", pick), ("v", got_back)], [packed]
    )
    return (node_out, scores.reshape(1, 1, cands), node_grad)


def solution(mesh):
    in_specs = (
        P(("dom", "edge"), None),
        P("edge", None),
        P(),
        P(),
        P(("dom", "edge"), None),
        P(("dom", "edge")),
        P("dom", "edge", None, None),
        P("dom", "edge", None),
        P("dom", "edge", None, None, None),
        P("dom", "edge", None, None),
        P("dom", "edge"),
        P("dom", "edge", None),
        P("edge", None),
        P(),
    )
    out_specs = (P(("dom", "edge"), None), P("dom", "edge", None), P(("dom", "edge"), None))
    return jax.shard_map(local, mesh=mesh, in_specs=in_specs, out_specs=out_specs, check_vma=False)
```

```python
import functools

import jax
import jax.numpy as jnp
from jax import lax
from jax.experimental import pallas as pl
from jax.experimental.pallas import tpu as pltpu
from jax.sharding import PartitionSpec as P

F32 = jnp.float32
BF16 = jnp.bfloat16
LOG2_E = 1.4426950408889634
DEAD = 64.0
VMEM = pl.BlockSpec(memory_space=pltpu.VMEM)
SPACES = {
    "v": VMEM,
    "s": pl.BlockSpec(memory_space=pltpu.SMEM),
    "f": pl.BlockSpec(memory_space=pl.ANY),
    "any": pl.BlockSpec(memory_space=pl.ANY),
}


def dot(a, b, dims=((1,), (0,))):
    return lax.dot_general(a, b, (dims, ((), ())), preferred_element_type=F32)


def call(kernel, outs, ins, scratch=(), vmem_mib=20, out_space="v", cost=None):
    fetched = [i for i, (space, _) in enumerate(ins) if space == "f"]

    def body(*refs):
        refs = list(refs)
        local_count = len(fetched) + 1
        own, (held, sems) = refs[:-local_count], (refs[-local_count:-1], refs[-1])
        copies = []
        for n, i in enumerate(fetched):
            copies.append(pltpu.make_async_copy(own[i], held[n], sems.at[n]))
            copies[-1].start()
            own[i] = held[n]

        def ready():
            for copy in copies:
                copy.wait()

        kernel(ready, *own)

    return pl.pallas_call(
        body,
        out_shape=outs,
        in_specs=[SPACES[space] for space, _ in ins],
        out_specs=jax.tree.map(lambda _: SPACES[out_space], outs),
        scratch_shapes=list(scratch)
        + [pltpu.VMEM(ins[i][1].shape, ins[i][1].dtype) for i in fetched]
        + [pltpu.SemaphoreType.DMA((max(1, len(fetched)),))],
        cost_estimate=cost,
        compiler_params=pltpu.CompilerParams(vmem_limit_bytes=vmem_mib * 1024 * 1024),
    )(*[array for _, array in ins])


def halo_kernel(ready, count_ref, rows_ref, feats_ref, out_ref):
    doms, block = rows_ref.shape
    at = lax.broadcasted_iota(jnp.int32, (1, block), 1)
    ready()
    pieces = [
        jnp.where(at < count_ref[:, s : s + 1], rows_ref[s : s + 1, :], -1) for s in range(doms)
    ]
    flat = jnp.concatenate(pieces, axis=1)
    total = doms * block
    nodes = feats_ref.shape[0]
    pick = (lax.broadcasted_iota(jnp.int32, (nodes, total), 0) == flat).astype(F32).astype(BF16)
    rows = dot(pick, feats_ref[...], ((0,), (0,)))
    first = lax.broadcasted_iota(jnp.int32, (16, total), 0) == 0
    dead = jnp.where(first & (flat < 0), 1.0, 0.0).astype(BF16)
    mark_at = (lax.broadcasted_iota(jnp.int32, (16, 128), 0) == 0) & (
        lax.broadcasted_iota(jnp.int32, (16, 128), 1) == 0
    )
    mark = jnp.where(mark_at, DEAD, 0.0).astype(BF16)
    out_ref[:, :128] = (rows[:, :128] + dot(dead, mark, ((0,), (0,)))).astype(BF16)
    out_ref[:, 128:] = rows[:, 128:].astype(BF16)


def three_parts(values):
    high = values.astype(BF16).astype(F32)
    middle = (values - high).astype(BF16).astype(F32)
    return jnp.concatenate([high, middle, values - high - middle], axis=0)


def block_diagonal(parts, heads):
    parts = parts.astype(F32)
    wide = jnp.concatenate([parts] * heads, axis=1)
    lane_head = lax.broadcasted_iota(jnp.int32, wide.shape, 1) // parts.shape[1]
    row_head = lax.broadcasted_iota(jnp.int32, wide.shape, 0) % heads
    wide = jnp.where(lane_head == row_head, wide, 0.0)
    return jnp.concatenate([wide, jnp.zeros((heads, wide.shape[1]), F32)], axis=0).astype(BF16)


def prepare_kernel(
    table,
    ready,
    live_ref,
    neigh_ref,
    degree_ref,
    src_ref,
    dst_ref,
    ends_ref,
    cand_ref,
    labels_ref,
    out_w_ref,
    for_attend_ref,
    for_score_ref,
    pick_ref,
):
    ready()
    nodes, ends = pick_ref.shape
    heads, size = src_ref.shape
    slots = neigh_ref.shape[0]
    ids = neigh_ref[...]
    ids = jnp.where(lax.broadcasted_iota(jnp.int32, ids.shape, 0) < degree_ref[...], ids, -1)
    for base in range(0, table, nodes):
        at = base + lax.broadcasted_iota(jnp.int32, (nodes, nodes), 0)
        total = jnp.zeros((nodes, nodes), F32)
        if base == 0:
            total = (at == lax.broadcasted_iota(jnp.int32, (nodes, nodes), 1)).astype(F32)
        for j in range(slots):
            total = total + (at == ids[j : j + 1, :]).astype(F32)
        total = total.T
        power = jnp.where(total > 1, 2.0, total)
        power = jnp.where(total > 2, 4.0, power)
        power = jnp.where(total > 5, 8.0, power)
        power = jnp.where(total > 13, 16.0, power)
        for_attend_ref[:, base : base + nodes] = total.astype(BF16)
        for_attend_ref[:, table + base : table + base + nodes] = power.astype(BF16)
    node_at = lax.broadcasted_iota(jnp.int32, (nodes, ends), 0)
    pick = (node_at == ends_ref[...]).astype(F32).astype(BF16)
    pick_ref[...] = pick
    first = 2 * table + size
    for_attend_ref[:, first : first + ends] = pick
    vectors = [three_parts(src_ref[...]), three_parts(dst_ref[...])]
    for_attend_ref[: 6 * heads, 2 * table : first] = jnp.concatenate(vectors, axis=0).astype(BF16)
    cands = cand_ref.shape[1]
    hidden = out_w_ref.shape[1]
    slot_at = lax.broadcasted_iota(jnp.int32, (ends, cands), 0)
    for i in range(2):
        one_hot = (slot_at == cand_ref[i : i + 1, :]).astype(F32).astype(BF16)
        for_score_ref[:ends, i * cands : (i + 1) * cands] = one_hot
    live = (lax.broadcasted_iota(jnp.int32, (1, cands), 1) < live_ref[0, 0]).astype(F32)
    known = jnp.concatenate([live, labels_ref[...].astype(F32), jnp.zeros((14, cands), F32)], axis=0)
    for_score_ref[ends : ends + 16, :cands] = known.astype(BF16)
    whole = jnp.concatenate([three_parts(out_w_ref[...]), jnp.zeros((13, hidden), F32)], axis=0)
    for_score_ref[ends + 16 :, :hidden] = whole.astype(BF16)


def shard_row(i, depth):
    return pl.multiple_of((lax.axis_index("edge") ^ i) * depth, depth)


def shard_dots(rows_ref, shards, whole_ref=None):
    depth = shards[0].shape[0]
    if depth % 128:
        for i, shard in enumerate(shards):
            whole_ref[pl.ds(shard_row(i, depth), depth), :] = shard[...]
        return dot(rows_ref[...], whole_ref[...])
    total = None
    for i, shard in enumerate(shards):
        cols = pl.ds(shard_row(i, depth), depth)
        part = dot(rows_ref[:, cols], shard[...])
        total = part if total is None else total + part
    return total


def attend_kernel(shard_count, heads, slots, ready, own_ref, got_ref, known_ref, *rest):
    shards = rest[:shard_count]
    out_ref, send_ref, proj_ref, stage_ref, rows_ref, bias_ref, mix_ref, whole_ref = rest[-8:]
    ready()
    nodes, width = own_ref.shape
    table = proj_ref.shape[0]
    size = width // heads
    count_ref = known_ref.at[:, :table]
    power_ref = known_ref.at[:, table : 2 * table]
    pick_ref = known_ref.at[:, 2 * table + size : 2 * table + size + slots]
    vectors = known_ref[: 6 * heads, 2 * table : 2 * table + size]
    diag_src = block_diagonal(vectors[: 3 * heads], heads)
    diag_dst = block_diagonal(vectors[3 * heads :], heads)
    rows_ref[:nodes, :] = own_ref[...]
    rows_ref[nodes:, :] = got_ref[...]
    proj_ref[...] = shard_dots(rows_ref, shards, whole_ref).astype(BF16)
    parts = dot(diag_src, proj_ref[...], ((1,), (1,)))
    src = parts[:heads] + parts[heads : 2 * heads] + parts[2 * heads : 3 * heads]
    src = src.astype(BF16).astype(F32) * LOG2_E
    parts = dot(proj_ref[:nodes, :], diag_dst, ((1,), (1,)))
    dst = parts[:, :heads] + parts[:, heads : 2 * heads] + parts[:, 2 * heads : 3 * heads]
    dst = dst * LOG2_E
    first_lane = (lax.broadcasted_iota(jnp.int32, (16, 128), 1) == 0).astype(F32).astype(BF16)
    mark = dot(first_lane, rows_ref[nodes:, :128], ((1,), (1,)))[:1]
    hide = jnp.where(mark < DEAD / 2, 0.0, -jnp.inf)
    hide = jnp.concatenate([jnp.zeros((1, nodes), F32), hide], axis=1)
    bias_ref[...] = jnp.where(count_ref[...] > 0, hide, -jnp.inf)
    chunk = 32
    for h in range(heads):
        for r in range(0, nodes, chunk):
            here = slice(r, r + chunk)
            logit = dst[here, h : h + 1] + src[h : h + 1, :]
            logit = jnp.maximum(logit, 0.2 * logit) + bias_ref[here, :]
            terms = jnp.exp2(logit - jnp.max(logit, axis=1, keepdims=True))
            count = count_ref[here, :]
            power = power_ref[here, :]
            running = jnp.sum(count.astype(F32) * terms, axis=1, keepdims=True)
            weight = (terms * (1.0 / running)).astype(BF16)
            mix_ref[h % 2, here, :] = weight * power
            mix_ref[h % 2, nodes + r : nodes + r + chunk, :] = weight * (count - power)
        both = dot(mix_ref[h % 2], proj_ref[:, h * size : (h + 1) * size])
        total = both[:nodes] + both[nodes:]
        total = jnp.where(total > 0, total, jnp.exp(jnp.minimum(total, 0.0)) - 1.0)
        out_ref[:, h * size : (h + 1) * size] = total.astype(BF16)
    pack_rows(dot(pick_ref[...], out_ref[...], ((0,), (0,))), stage_ref, send_ref)


def pack_rows(rows, stage_ref, out_ref):
    slots, width = rows.shape
    pieces = width // 128
    for c in range(pieces):
        stage_ref[pl.ds(c, slots, stride=pieces), :] = rows[:, c * 128 : (c + 1) * 128]
    out_ref[...] = stage_ref[...].astype(BF16)


def unpack_rows(ref, stage_ref, pieces):
    stage_ref[...] = ref[...].astype(F32)
    slots = ref.shape[0] // pieces
    parts = [stage_ref[pl.ds(c, slots, stride=pieces), :] for c in range(pieces)]
    return jnp.concatenate(parts, axis=1).astype(BF16)


def add_shards(rows_ref, indices, shards, part_ref):
    depth = shards[0].shape[0]
    span = rows_ref.shape[1]
    for i, shard in zip(indices, shards):
        row = shard_row(i, depth)
        cols = pl.ds(pl.multiple_of(row % span, depth), depth)
        part_ref[row // span] += dot(rows_ref[:, cols], shard[...])


def first_kernel(indices, cands, ready, got_ref, known_ref, *rest):
    shards = rest[:-3]
    rows_ref, part_ref, stage_ref = rest[-3:]
    ready()
    slots = known_ref.shape[0] - 32
    width = got_ref.shape[0] * 128 // slots
    rows = unpack_rows(got_ref, stage_ref, width // 128)
    if slots > cands:
        for i in range(2):
            pick = known_ref[:slots, i * cands : (i + 1) * cands]
            pair = dot(pick, rows, ((0,), (0,)))
            rows_ref[:, i * width : (i + 1) * width] = pair.astype(BF16)
    else:
        rows_ref[...] = rows
    part_ref[...] = jnp.zeros_like(part_ref)
    add_shards(rows_ref, indices, shards, part_ref)


def score_kernel(late, cands, ready, rows_ref, first_ref, known_ref, *rest):
    shards = rest[:-6]
    scores_ref, back_ref, stage_ref, sum_ref, grad_ref, part_ref = rest[-6:]
    ready()
    depth, hidden = shards[0].shape
    slots, width = grad_ref.shape[1:]
    picks = [known_ref[:slots, i * cands : (i + 1) * cands] for i in range(2)]
    known = known_ref[slots : slots + 16, :cands].astype(F32).T
    live, label = known[:, :1], known[:, 1:2]
    out_w = known_ref[slots + 16 :, :hidden].astype(F32)
    out_w = out_w[:1] + out_w[1:2] + out_w[2:3]
    part_ref[...] = first_ref[...]
    add_shards(rows_ref, late, [shards[i] for i in late], part_ref)
    if slots > cands:
        pre_act = part_ref[0]
    else:
        pre_act = None
        for i in range(2):
            rest = part_ref[i]
            for _ in range(3):
                high = rest.astype(BF16)
                rest = rest - high.astype(F32)
                term = dot(picks[i], high, ((0,), (0,)))
                pre_act = term if pre_act is None else pre_act + term
    gate = jax.nn.sigmoid(pre_act)
    score = jnp.sum(pre_act * gate * out_w, axis=1, keepdims=True) * live
    scores_ref[...] = jnp.broadcast_to(score, (cands, 128)).T[:1]
    grad_score = (jax.nn.sigmoid(score) - label) * live
    grad_pre = (grad_score * out_w * (gate * (1.0 + pre_act * (1.0 - gate)))).astype(BF16)
    for i in range(2):
        total = dot(picks[i], grad_pre)
        high = total.astype(BF16)
        sum_ref[i, :slots, :] = high
        sum_ref[i, slots:, :] = (total - high.astype(F32)).astype(BF16)
    for i, shard in enumerate(shards):
        row = shard_row(i, depth)
        half = row // width
        col = pl.multiple_of(row % width, depth)
        both = dot(sum_ref[half], shard[...], ((1,), (1,)))
        grad_ref[half, :, pl.ds(col, depth)] = both[:slots] + both[slots:]
    pack_rows(grad_ref[0] + grad_ref[1], stage_ref, back_ref)


def scatter_kernel(ready, pick_ref, got_ref, out_ref, stage_ref):
    ready()
    rows = unpack_rows(got_ref, stage_ref, out_ref.shape[1] // 128)
    out_ref[...] = dot(pick_ref[...], rows)


def swap(array, axis, k):
    count = lax.axis_size(axis)
    return lax.ppermute(array, axis, [(i, i ^ k) for i in range(count)])


def across(shard, edge_count):
    return [shard] + [swap(shard, "edge", 2 * k) for k in range(1, edge_count // 2)]


def from_core(shards):
    return [one for shard in shards for one in (shard, swap(shard, "edge", 1))]


def local(
    node_feats,
    gat_weight,
    attn_src,
    attn_dst,
    neighbours,
    degree,
    halo_rows,
    halo_count,
    endpoint_rows,
    cand_ends,
    cand_count,
    labels,
    mlp_weight,
    out_weight,
):
    nodes, width = node_feats.shape
    dom_count = lax.axis_size("dom")
    edge_count = lax.axis_size("edge")
    block = halo_rows.shape[-1]
    cands = labels.shape[-1]
    hidden = out_weight.shape[0]
    halo = dom_count * block
    table = nodes + halo
    slots = dom_count * edge_count * endpoint_rows.shape[-1]
    pieces = width // 128
    everyone = ("dom", "edge")
    shape = jax.ShapeDtypeStruct

    heads = attn_src.shape[0]
    send_rows = call(
        halo_kernel,
        shape((halo, width), BF16),
        [("f", halo_count[0]), ("f", halo_rows[0, 0]), ("f", node_feats)],
        vmem_mib=60,
    )
    got_rows = lax.all_to_all(send_rows, "dom", split_axis=0, concat_axis=0, tiled=True)
    gat_across = across(gat_weight, edge_count)
    held_mlp = lax.optimization_barrier((mlp_weight, got_rows))[0]
    mlp_across = across(held_mlp, edge_count)
    lanes = -(-(2 * table + attn_src.shape[1] + slots) // 128) * 128
    for_attend, for_score, pick = call(
        functools.partial(prepare_kernel, table),
        (
            shape((nodes, lanes), BF16),
            shape((slots + 32, max(2 * cands, hidden)), BF16),
            shape((nodes, slots), BF16),
        ),
        [
            ("s", cand_count),
            ("f", neighbours.T),
            ("f", degree.reshape(1, nodes)),
            ("f", attn_src),
            ("f", attn_dst),
            ("f", endpoint_rows.reshape(1, slots)),
            ("f", cand_ends[0, 0]),
            ("f", labels[0]),
            ("f", out_weight.reshape(1, hidden)),
        ],
        cost=pl.CostEstimate(flops=10**6, bytes_accessed=10**5, transcendentals=0),
    )
    gat_across = lax.optimization_barrier((*gat_across, for_attend))[:-1]
    gat_shards = from_core(gat_across)
    packed = pltpu.VMEM((slots * pieces, 128), F32)
    node_out, send_ends = call(
        functools.partial(attend_kernel, edge_count, heads, slots),
        (shape((nodes, width), BF16), shape((slots * pieces, 128), BF16)),
        [("v", node_feats), ("v", got_rows), ("v", for_attend)] + [("v", w) for w in gat_shards],
        [
            pltpu.VMEM((table, width), BF16),
            packed,
            pltpu.VMEM((table, width), BF16),
            pltpu.VMEM((nodes, table), F32),
            pltpu.VMEM((2, 2 * nodes, table), BF16),
            pltpu.VMEM((width if width // edge_count % 128 else 16, width), BF16),
        ],
    )
    got_ends = lax.all_to_all(send_ends, everyone, split_axis=0, concat_axis=0, tiled=True)
    tied = lax.optimization_barrier((*mlp_across, send_ends))[:-1]
    mlp_shards = []
    for shard, held in zip(mlp_across, tied):
        mlp_shards += [shard, swap(held, "edge", 1)]
    early = list(range(0, edge_count, 2))
    late = list(range(1, edge_count, 2))
    many = slots > cands
    rows, part = call(
        functools.partial(first_kernel, early, cands),
        (
            shape((cands, 2 * width) if many else (slots, width), BF16),
            shape((1, cands, hidden) if many else (2, slots, hidden), F32),
        ),
        [("v", got_ends), ("v", for_score)] + [("v", mlp_shards[i]) for i in early],
        [packed],
        cost=pl.CostEstimate(flops=20 * 10**9, bytes_accessed=60 * 10**6, transcendentals=0),
    )
    scores, send_back = call(
        functools.partial(score_kernel, late, cands),
        (shape((1, cands), F32), shape((slots * pieces, 128), BF16)),
        [("v", rows), ("v", part), ("v", for_score)] + [("v", w) for w in mlp_shards],
        [
            packed,
            pltpu.VMEM((2, 2 * slots, hidden), BF16),
            pltpu.VMEM((2, slots, width), F32),
            pltpu.VMEM(part.shape, F32),
        ],
    )
    got_back = lax.all_to_all(send_back, everyone, split_axis=0, concat_axis=0, tiled=True)
    node_grad = call(
        scatter_kernel, shape((nodes, width), F32), [("v", pick), ("v", got_back)], [packed]
    )
    return (node_out, scores.reshape(1, 1, cands), node_grad)


def solution(mesh):
    in_specs = (
        P(("dom", "edge"), None),
        P("edge", None),
        P(),
        P(),
        P(("dom", "edge"), None),
        P(("dom", "edge")),
        P("dom", "edge", None, None),
        P("dom", "edge", None),
        P("dom", "edge", None, None, None),
        P("dom", "edge", None, None),
        P("dom", "edge"),
        P("dom", "edge", None),
        P("edge", None),
        P(),
    )
    out_specs = (P(("dom", "edge"), None), P("dom", "edge", None), P(("dom", "edge"), None))
    return jax.shard_map(local, mesh=mesh, in_specs=in_specs, out_specs=out_specs, check_vma=False)
```

```python
import functools

import jax
import jax.numpy as jnp
from jax import lax
from jax.experimental import pallas as pl
from jax.experimental.pallas import tpu as pltpu
from jax.sharding import PartitionSpec as P

F32 = jnp.float32
BF16 = jnp.bfloat16
LOG2_E = 1.4426950408889634
DEAD = 64.0
VMEM = pl.BlockSpec(memory_space=pltpu.VMEM)
SPACES = {
    "v": VMEM,
    "s": pl.BlockSpec(memory_space=pltpu.SMEM),
    "f": pl.BlockSpec(memory_space=pl.ANY),
    "any": pl.BlockSpec(memory_space=pl.ANY),
}


def dot(a, b, dims=((1,), (0,))):
    return lax.dot_general(a, b, (dims, ((), ())), preferred_element_type=F32)


def call(kernel, outs, ins, scratch=(), vmem_mib=20, out_space="v", cost=None):
    fetched = [i for i, (space, _) in enumerate(ins) if space == "f"]

    def body(*refs):
        refs = list(refs)
        local_count = len(fetched) + 1
        own, (held, sems) = refs[:-local_count], (refs[-local_count:-1], refs[-1])
        copies = []
        for n, i in enumerate(fetched):
            copies.append(pltpu.make_async_copy(own[i], held[n], sems.at[n]))
            copies[-1].start()
            own[i] = held[n]

        def ready():
            for copy in copies:
                copy.wait()

        kernel(ready, *own)

    return pl.pallas_call(
        body,
        out_shape=outs,
        in_specs=[SPACES[space] for space, _ in ins],
        out_specs=jax.tree.map(lambda _: SPACES[out_space], outs),
        scratch_shapes=list(scratch)
        + [pltpu.VMEM(ins[i][1].shape, ins[i][1].dtype) for i in fetched]
        + [pltpu.SemaphoreType.DMA((max(1, len(fetched)),))],
        cost_estimate=cost,
        compiler_params=pltpu.CompilerParams(vmem_limit_bytes=vmem_mib * 1024 * 1024),
    )(*[array for _, array in ins])


def halo_kernel(ready, count_ref, rows_ref, feats_ref, out_ref):
    doms, block = rows_ref.shape
    at = lax.broadcasted_iota(jnp.int32, (1, block), 1)
    ready()
    pieces = [
        jnp.where(at < count_ref[:, s : s + 1], rows_ref[s : s + 1, :], -1) for s in range(doms)
    ]
    flat = jnp.concatenate(pieces, axis=1)
    total = doms * block
    nodes = feats_ref.shape[0]
    pick = (lax.broadcasted_iota(jnp.int32, (nodes, total), 0) == flat).astype(F32).astype(BF16)
    rows = dot(pick, feats_ref[...], ((0,), (0,)))
    first = lax.broadcasted_iota(jnp.int32, (16, total), 0) == 0
    dead = jnp.where(first & (flat < 0), 1.0, 0.0).astype(BF16)
    mark_at = (lax.broadcasted_iota(jnp.int32, (16, 128), 0) == 0) & (
        lax.broadcasted_iota(jnp.int32, (16, 128), 1) == 0
    )
    mark = jnp.where(mark_at, DEAD, 0.0).astype(BF16)
    out_ref[:, :128] = (rows[:, :128] + dot(dead, mark, ((0,), (0,)))).astype(BF16)
    out_ref[:, 128:] = rows[:, 128:].astype(BF16)


def three_parts(values):
    high = values.astype(BF16).astype(F32)
    middle = (values - high).astype(BF16).astype(F32)
    return jnp.concatenate([high, middle, values - high - middle], axis=0)


def block_diagonal(parts, heads):
    parts = parts.astype(F32)
    wide = jnp.concatenate([parts] * heads, axis=1)
    lane_head = lax.broadcasted_iota(jnp.int32, wide.shape, 1) // parts.shape[1]
    row_head = lax.broadcasted_iota(jnp.int32, wide.shape, 0) % heads
    wide = jnp.where(lane_head == row_head, wide, 0.0)
    return jnp.concatenate([wide, jnp.zeros((heads, wide.shape[1]), F32)], axis=0).astype(BF16)


def prepare_kernel(
    table,
    ready,
    live_ref,
    neigh_ref,
    degree_ref,
    src_ref,
    dst_ref,
    ends_ref,
    cand_ref,
    labels_ref,
    out_w_ref,
    for_attend_ref,
    for_score_ref,
    pick_ref,
):
    ready()
    nodes, ends = pick_ref.shape
    heads, size = src_ref.shape
    slots = neigh_ref.shape[0]
    ids = neigh_ref[...]
    ids = jnp.where(lax.broadcasted_iota(jnp.int32, ids.shape, 0) < degree_ref[...], ids, -1)
    for base in range(0, table, nodes):
        at = base + lax.broadcasted_iota(jnp.int32, (nodes, nodes), 0)
        total = jnp.zeros((nodes, nodes), F32)
        if base == 0:
            total = (at == lax.broadcasted_iota(jnp.int32, (nodes, nodes), 1)).astype(F32)
        for j in range(slots):
            total = total + (at == ids[j : j + 1, :]).astype(F32)
        total = total.T
        power = jnp.where(total > 1, 2.0, total)
        power = jnp.where(total > 2, 4.0, power)
        power = jnp.where(total > 5, 8.0, power)
        power = jnp.where(total > 13, 16.0, power)
        for_attend_ref[:, base : base + nodes] = total.astype(BF16)
        for_attend_ref[:, table + base : table + base + nodes] = power.astype(BF16)
    node_at = lax.broadcasted_iota(jnp.int32, (nodes, ends), 0)
    pick = (node_at == ends_ref[...]).astype(F32).astype(BF16)
    pick_ref[...] = pick
    first = 2 * table + size
    for_attend_ref[:, first : first + ends] = pick
    vectors = [three_parts(src_ref[...]), three_parts(dst_ref[...])]
    for_attend_ref[: 6 * heads, 2 * table : first] = jnp.concatenate(vectors, axis=0).astype(BF16)
    cands = cand_ref.shape[1]
    hidden = out_w_ref.shape[1]
    slot_at = lax.broadcasted_iota(jnp.int32, (ends, cands), 0)
    for i in range(2):
        one_hot = (slot_at == cand_ref[i : i + 1, :]).astype(F32).astype(BF16)
        for_score_ref[:ends, i * cands : (i + 1) * cands] = one_hot
    live = (lax.broadcasted_iota(jnp.int32, (1, cands), 1) < live_ref[0, 0]).astype(F32)
    known = jnp.concatenate([live, labels_ref[...].astype(F32), jnp.zeros((14, cands), F32)], axis=0)
    for_score_ref[ends : ends + 16, :cands] = known.astype(BF16)
    whole = jnp.concatenate([three_parts(out_w_ref[...]), jnp.zeros((13, hidden), F32)], axis=0)
    for_score_ref[ends + 16 :, :hidden] = whole.astype(BF16)


def shard_row(i, depth):
    return pl.multiple_of((lax.axis_index("edge") ^ i) * depth, depth)


def shard_dots(rows_ref, shards, whole_ref=None):
    depth = shards[0].shape[0]
    if depth % 128:
        for i, shard in enumerate(shards):
            whole_ref[pl.ds(shard_row(i, depth), depth), :] = shard[...]
        return dot(rows_ref[...], whole_ref[...])
    total = None
    for i, shard in enumerate(shards):
        cols = pl.ds(shard_row(i, depth), depth)
        part = dot(rows_ref[:, cols], shard[...])
        total = part if total is None else total + part
    return total


def attend_kernel(shard_count, heads, slots, ready, own_ref, got_ref, known_ref, *rest):
    shards = rest[:shard_count]
    out_ref, send_ref, proj_ref, stage_ref, rows_ref, bias_ref, mix_ref, whole_ref = rest[-8:]
    ready()
    nodes, width = own_ref.shape
    table = proj_ref.shape[0]
    size = width // heads
    count_ref = known_ref.at[:, :table]
    power_ref = known_ref.at[:, table : 2 * table]
    pick_ref = known_ref.at[:, 2 * table + size : 2 * table + size + slots]
    vectors = known_ref[: 6 * heads, 2 * table : 2 * table + size]
    diag_src = block_diagonal(vectors[: 3 * heads], heads)
    diag_dst = block_diagonal(vectors[3 * heads :], heads)
    rows_ref[:nodes, :] = own_ref[...]
    rows_ref[nodes:, :] = got_ref[...]
    proj_ref[...] = shard_dots(rows_ref, shards, whole_ref).astype(BF16)
    parts = dot(diag_src, proj_ref[...], ((1,), (1,)))
    src = parts[:heads] + parts[heads : 2 * heads] + parts[2 * heads : 3 * heads]
    src = src.astype(BF16).astype(F32) * LOG2_E
    parts = dot(proj_ref[:nodes, :], diag_dst, ((1,), (1,)))
    dst = parts[:, :heads] + parts[:, heads : 2 * heads] + parts[:, 2 * heads : 3 * heads]
    dst = dst * LOG2_E
    first_lane = (lax.broadcasted_iota(jnp.int32, (16, 128), 1) == 0).astype(F32).astype(BF16)
    mark = dot(first_lane, rows_ref[nodes:, :128], ((1,), (1,)))[:1]
    hide = jnp.where(mark < DEAD / 2, 0.0, -jnp.inf)
    hide = jnp.concatenate([jnp.zeros((1, nodes), F32), hide], axis=1)
    bias_ref[...] = jnp.where(count_ref[...] > 0, hide, -jnp.inf)
    chunk = 32
    for h in range(heads):
        for r in range(0, nodes, chunk):
            here = slice(r, r + chunk)
            logit = dst[here, h : h + 1] + src[h : h + 1, :]
            logit = jnp.maximum(logit, 0.2 * logit) + bias_ref[here, :]
            terms = jnp.exp2(logit - jnp.max(logit, axis=1, keepdims=True))
            count = count_ref[here, :]
            power = power_ref[here, :]
            running = jnp.sum(count.astype(F32) * terms, axis=1, keepdims=True)
            weight = (terms * (1.0 / running)).astype(BF16)
            mix_ref[h % 2, here, :] = weight * power
            mix_ref[h % 2, nodes + r : nodes + r + chunk, :] = weight * (count - power)
        both = dot(mix_ref[h % 2], proj_ref[:, h * size : (h + 1) * size])
        total = both[:nodes] + both[nodes:]
        total = jnp.where(total > 0, total, jnp.exp(jnp.minimum(total, 0.0)) - 1.0)
        out_ref[:, h * size : (h + 1) * size] = total.astype(BF16)
    pack_rows(dot(pick_ref[...], out_ref[...], ((0,), (0,))), stage_ref, send_ref)


def pack_rows(rows, stage_ref, out_ref):
    slots, width = rows.shape
    pieces = width // 128
    for c in range(pieces):
        stage_ref[pl.ds(c, slots, stride=pieces), :] = rows[:, c * 128 : (c + 1) * 128]
    out_ref[...] = stage_ref[...].astype(BF16)


def unpack_rows(ref, stage_ref, pieces):
    stage_ref[...] = ref[...].astype(F32)
    slots = ref.shape[0] // pieces
    parts = [stage_ref[pl.ds(c, slots, stride=pieces), :] for c in range(pieces)]
    return jnp.concatenate(parts, axis=1).astype(BF16)


def add_shards(rows_ref, indices, shards, part_ref):
    depth = shards[0].shape[0]
    span = rows_ref.shape[1]
    for i, shard in zip(indices, shards):
        row = shard_row(i, depth)
        cols = pl.ds(pl.multiple_of(row % span, depth), depth)
        part_ref[row // span] += dot(rows_ref[:, cols], shard[...])


def first_kernel(indices, cands, ready, got_ref, known_ref, *rest):
    shards = rest[:-3]
    rows_ref, part_ref, stage_ref = rest[-3:]
    ready()
    slots = known_ref.shape[0] - 32
    width = got_ref.shape[0] * 128 // slots
    rows = unpack_rows(got_ref, stage_ref, width // 128)
    if slots > cands:
        for i in range(2):
            pick = known_ref[:slots, i * cands : (i + 1) * cands]
            pair = dot(pick, rows, ((0,), (0,)))
            rows_ref[:, i * width : (i + 1) * width] = pair.astype(BF16)
    else:
        rows_ref[...] = rows
    part_ref[...] = jnp.zeros_like(part_ref)
    add_shards(rows_ref, indices, shards, part_ref)


def score_kernel(late, cands, ready, rows_ref, first_ref, known_ref, *rest):
    shards = rest[:-6]
    scores_ref, back_ref, stage_ref, sum_ref, grad_ref, part_ref = rest[-6:]
    ready()
    depth, hidden = shards[0].shape
    slots, width = grad_ref.shape[1:]
    picks = [known_ref[:slots, i * cands : (i + 1) * cands] for i in range(2)]
    known = known_ref[slots : slots + 16, :cands].astype(F32).T
    live, label = known[:, :1], known[:, 1:2]
    out_w = known_ref[slots + 16 :, :hidden].astype(F32)
    out_w = out_w[:1] + out_w[1:2] + out_w[2:3]
    part_ref[...] = first_ref[...]
    add_shards(rows_ref, late, [shards[i] for i in late], part_ref)
    if slots > cands:
        pre_act = part_ref[0]
    else:
        pre_act = None
        for i in range(2):
            rest = part_ref[i]
            for _ in range(3):
                high = rest.astype(BF16)
                rest = rest - high.astype(F32)
                term = dot(picks[i], high, ((0,), (0,)))
                pre_act = term if pre_act is None else pre_act + term
    gate = jax.nn.sigmoid(pre_act)
    score = jnp.sum(pre_act * gate * out_w, axis=1, keepdims=True) * live
    scores_ref[...] = jnp.broadcast_to(score, (cands, 128)).T[:1]
    grad_score = (jax.nn.sigmoid(score) - label) * live
    grad_pre = (grad_score * out_w * (gate * (1.0 + pre_act * (1.0 - gate)))).astype(BF16)
    for i in range(2):
        total = dot(picks[i], grad_pre)
        high = total.astype(BF16)
        sum_ref[i, :slots, :] = high
        sum_ref[i, slots:, :] = (total - high.astype(F32)).astype(BF16)
    for i, shard in enumerate(shards):
        row = shard_row(i, depth)
        half = row // width
        col = pl.multiple_of(row % width, depth)
        both = dot(sum_ref[half], shard[...], ((1,), (1,)))
        grad_ref[half, :, pl.ds(col, depth)] = both[:slots] + both[slots:]
    pack_rows(grad_ref[0] + grad_ref[1], stage_ref, back_ref)


def scatter_kernel(ready, pick_ref, got_ref, out_ref, stage_ref):
    ready()
    rows = unpack_rows(got_ref, stage_ref, out_ref.shape[1] // 128)
    out_ref[...] = dot(pick_ref[...], rows)


def swap(array, axis, k):
    count = lax.axis_size(axis)
    return lax.ppermute(array, axis, [(i, i ^ k) for i in range(count)])


def across(shard, edge_count):
    return [shard] + [swap(shard, "edge", 2 * k) for k in range(1, edge_count // 2)]


def from_core(shards):
    return [one for shard in shards for one in (shard, swap(shard, "edge", 1))]


def local(
    node_feats,
    gat_weight,
    attn_src,
    attn_dst,
    neighbours,
    degree,
    halo_rows,
    halo_count,
    endpoint_rows,
    cand_ends,
    cand_count,
    labels,
    mlp_weight,
    out_weight,
):
    nodes, width = node_feats.shape
    dom_count = lax.axis_size("dom")
    edge_count = lax.axis_size("edge")
    block = halo_rows.shape[-1]
    cands = labels.shape[-1]
    hidden = out_weight.shape[0]
    halo = dom_count * block
    table = nodes + halo
    slots = dom_count * edge_count * endpoint_rows.shape[-1]
    pieces = width // 128
    everyone = ("dom", "edge")
    shape = jax.ShapeDtypeStruct

    heads = attn_src.shape[0]
    send_rows = call(
        halo_kernel,
        shape((halo, width), BF16),
        [("f", halo_count[0]), ("f", halo_rows[0, 0]), ("f", node_feats)],
        vmem_mib=60,
    )
    got_rows = lax.all_to_all(send_rows, "dom", split_axis=0, concat_axis=0, tiled=True)
    gat_across = across(gat_weight, edge_count)
    mlp_across = across(mlp_weight, edge_count)
    lanes = -(-(2 * table + attn_src.shape[1] + slots) // 128) * 128
    for_attend, for_score, pick = call(
        functools.partial(prepare_kernel, table),
        (
            shape((nodes, lanes), BF16),
            shape((slots + 32, max(2 * cands, hidden)), BF16),
            shape((nodes, slots), BF16),
        ),
        [
            ("s", cand_count),
            ("f", neighbours.T),
            ("f", degree.reshape(1, nodes)),
            ("f", attn_src),
            ("f", attn_dst),
            ("f", endpoint_rows.reshape(1, slots)),
            ("f", cand_ends[0, 0]),
            ("f", labels[0]),
            ("f", out_weight.reshape(1, hidden)),
        ],
        vmem_mib=60,
    )
    gat_across = lax.optimization_barrier((*gat_across, for_attend))[:-1]
    gat_shards = from_core(gat_across)
    packed = pltpu.VMEM((slots * pieces, 128), F32)
    node_out, send_ends = call(
        functools.partial(attend_kernel, edge_count, heads, slots),
        (shape((nodes, width), BF16), shape((slots * pieces, 128), BF16)),
        [("v", node_feats), ("v", got_rows), ("v", for_attend)] + [("v", w) for w in gat_shards],
        [
            pltpu.VMEM((table, width), BF16),
            packed,
            pltpu.VMEM((table, width), BF16),
            pltpu.VMEM((nodes, table), F32),
            pltpu.VMEM((2, 2 * nodes, table), BF16),
            pltpu.VMEM((width if width // edge_count % 128 else 16, width), BF16),
        ],
        cost=pl.CostEstimate(
            flops=2 * table * width * (width + 2 * nodes),
            bytes_accessed=2 * width * (width + table + 2 * nodes) + 2 * nodes * lanes,
            transcendentals=nodes * table * heads,
        ),
    )
    got_ends = lax.all_to_all(send_ends, everyone, split_axis=0, concat_axis=0, tiled=True)
    tied = lax.optimization_barrier((*mlp_across, send_ends))[:-1]
    mlp_shards = []
    for shard, held in zip(mlp_across, tied):
        mlp_shards += [shard, swap(held, "edge", 1)]
    early = list(range(0, edge_count, 2))
    late = list(range(1, edge_count, 2))
    many = slots > cands
    rows, part = call(
        functools.partial(first_kernel, early, cands),
        (
            shape((cands, 2 * width) if many else (slots, width), BF16),
            shape((1, cands, hidden) if many else (2, slots, hidden), F32),
        ),
        [("v", got_ends), ("v", for_score)] + [("v", mlp_shards[i]) for i in early],
        [packed],
        cost=pl.CostEstimate(flops=20 * 10**9, bytes_accessed=60 * 10**6, transcendentals=0),
    )
    scores, send_back = call(
        functools.partial(score_kernel, late, cands),
        (shape((1, cands), F32), shape((slots * pieces, 128), BF16)),
        [("v", rows), ("v", part), ("v", for_score)] + [("v", w) for w in mlp_shards],
        [
            packed,
            pltpu.VMEM((2, 2 * slots, hidden), BF16),
            pltpu.VMEM((2, slots, width), F32),
            pltpu.VMEM(part.shape, F32),
        ],
    )
    got_back = lax.all_to_all(send_back, everyone, split_axis=0, concat_axis=0, tiled=True)
    node_grad = call(
        scatter_kernel, shape((nodes, width), F32), [("v", pick), ("v", got_back)], [packed]
    )
    return (node_out, scores.reshape(1, 1, cands), node_grad)


def solution(mesh):
    in_specs = (
        P(("dom", "edge"), None),
        P("edge", None),
        P(),
        P(),
        P(("dom", "edge"), None),
        P(("dom", "edge")),
        P("dom", "edge", None, None),
        P("dom", "edge", None),
        P("dom", "edge", None, None, None),
        P("dom", "edge", None, None),
        P("dom", "edge"),
        P("dom", "edge", None),
        P("edge", None),
        P(),
    )
    out_specs = (P(("dom", "edge"), None), P("dom", "edge", None), P(("dom", "edge"), None))
    return jax.shard_map(local, mesh=mesh, in_specs=in_specs, out_specs=out_specs, check_vma=False)
```
